32 devices in a mesh: tm: 8 (over z, x), space: 4 (over y, core).
Axes of the slice: x: 2, y: 2, z: 4, core: 2. Of those that a mesh axis runs over, the one named last changes fastest.
Arguments:
- snapshots: float32 [512, 16384], P('tm', 'space'), as said below
- space_factor: float32 [16384, 256], P('space'), as said below
Outputs:
- time_factor: float32 [512, 256], P('tm')
- loadings: float32 [256, 16384], P('tm', 'space')
Inputs may be any that keep to these rules, and one draw needn't show every extreme that they name: `snapshots`: entries are real values. `space_factor`: entries are real values; columns have norms between 0.05 and 1, the previous sweep's singular values.
All inputs are finite; a program needn't handle non-finite values.
Results may differ from the reference program's by a relative error of at most 0.0001.
Values sent between devices are 32-bit elements; how exact they have to be, the bound alone decides.
No kernel may reach another device: no remote copies, remote signals or barrier semaphores. Data moves between devices by JAX's collectives and lax.ppermute only.
A program may use at most 64 MiB of HBM per device.

```python
import math
import jax
import jax.numpy as jnp
from jax import lax

P_SIZE = 16384
RANK = 256
NS = 2
TIME = 512


def draw_snapshots(key, part):
    keys = jax.random.split(jax.random.fold_in(key, 11), 3)
    ramp = jnp.arange(TIME, dtype=jnp.float32) / TIME
    row_scale = jnp.exp(ramp * math.log(3.0)) * jnp.exp(jax.random.uniform(keys[1], (TIME,)) * math.log(10.0)) / 6.0
    base = jax.random.normal(keys[0], (TIME, P_SIZE), jnp.float32)
    col_scale = jnp.exp(jax.random.uniform(keys[2], (P_SIZE,)) * math.log(10.0)) / 3.2
    return base * row_scale[:, None] * col_scale[None, :]


def draw_space_factor(key, part):
    keys = jax.random.split(jax.random.fold_in(key, 23), 2)
    base = jax.random.normal(keys[0], (P_SIZE, RANK), jnp.float32)
    col_scale = jnp.exp(jax.random.uniform(keys[1], (RANK,)) * math.log(10.0)) / 10.0
    return base * col_scale[None, :] / math.sqrt(P_SIZE)


def setup_inputs(seed: int = 0) -> dict:
    key_of = jax.random.split(jax.random.key(seed), 3)
    snapshots = draw_snapshots(jax.random.fold_in(key_of[2], 71), 0)
    space_factor = draw_space_factor(jax.random.fold_in(key_of[2], 71), 0)
    return dict(snapshots=snapshots, space_factor=space_factor)


def reference(snapshots, space_factor):
    highest = lax.Precision.HIGHEST
    projected = jnp.dot(snapshots, space_factor, precision=highest, preferred_element_type=jnp.float32)
    factor = projected / jnp.sqrt(jnp.sum(projected * projected))
    identity_mat = jnp.eye(RANK, dtype=jnp.float32)
    for sweep in range(NS):
        correlation = jnp.dot(factor.T, factor, precision=highest, preferred_element_type=jnp.float32)
        factor = jnp.dot(factor, 1.5 * identity_mat - 0.5 * correlation, precision=highest, preferred_element_type=jnp.float32)
    loadings = jnp.dot(factor.T, snapshots, precision=highest, preferred_element_type=jnp.float32)
    return (factor * jnp.float32(math.sqrt(TIME)), loadings)
```

```python
import math

import jax
import jax.numpy as jnp
from jax import lax
from jax.sharding import PartitionSpec as P

NS = 2


def inner(left, right):
    return lax.dot_general(
        left,
        right,
        (((0,), (0,)), ((), ())),
        precision=lax.Precision.HIGH,
        preferred_element_type=jnp.float32,
    )


def matmul(left, right):
    return jnp.dot(left, right, precision=lax.Precision.HIGH, preferred_element_type=jnp.float32)


def polar_mixing(gram):
    identity_mat = jnp.eye(gram.shape[0], dtype=jnp.float32)
    total = jnp.trace(gram)
    correlation = gram / total
    mixing = None
    for sweep in range(NS):
        update = 1.5 * identity_mat - 0.5 * correlation
        mixing = update if mixing is None else matmul(mixing, update)
        if sweep < NS - 1:
            correlation = matmul(matmul(correlation, update), update)
    return mixing / jnp.sqrt(total)


def on_device(snapshots, space_factor):
    rows, points = snapshots.shape
    rank = space_factor.shape[1]
    times, spaces = lax.axis_size("tm"), lax.axis_size("space")
    scaling = jnp.float32(math.sqrt(times * rows))

    columns = lax.all_to_all(snapshots, "tm", split_axis=1, concat_axis=0, tiled=True)

    partial = matmul(snapshots, space_factor).reshape(spaces, rows // spaces, rank)
    piece = jnp.sum(lax.all_to_all(partial, "space", 0, 0, tiled=True), axis=0)
    copies = jnp.broadcast_to(piece, (times * spaces,) + piece.shape)
    projected = lax.all_to_all(copies, ("tm", "space"), 0, 0, tiled=True).reshape(times * rows, rank)

    factor = matmul(projected, polar_mixing(inner(projected, projected)))
    own = lax.dynamic_slice_in_dim(factor, lax.axis_index("tm") * rows, rows, axis=0)
    loadings = lax.all_to_all(inner(factor, columns), "tm", split_axis=0, concat_axis=1, tiled=True)
    return (own * scaling, loadings)


def solution(mesh):
    return jax.shard_map(
        on_device,
        mesh=mesh,
        in_specs=(P("tm", "space"), P("space", None)),
        out_specs=(P("tm", None), P("tm", "space")),
        check_vma=False,
    )
```

```python
import math

import jax
import jax.numpy as jnp
from jax import lax
from jax.sharding import PartitionSpec as P

NS = 2


def inner(left, right):
    return lax.dot_general(
        left,
        right,
        (((0,), (0,)), ((), ())),
        precision=lax.Precision.HIGH,
        preferred_element_type=jnp.float32,
    )


def matmul(left, right):
    return jnp.dot(left, right, precision=lax.Precision.HIGH, preferred_element_type=jnp.float32)


def polar_mixing(gram):
    identity_mat = jnp.eye(gram.shape[0], dtype=jnp.float32)
    total = jnp.trace(gram)
    correlation = gram / total
    mixing = None
    for sweep in range(NS):
        update = 1.5 * identity_mat - 0.5 * correlation
        mixing = update if mixing is None else matmul(mixing, update)
        if sweep < NS - 1:
            correlation = matmul(matmul(correlation, update), update)
    return mixing / jnp.sqrt(total)


def swap(value, axis, offset):
    return lax.ppermute(value, axis, [(i, i ^ offset) for i in range(lax.axis_size(axis))])


def gather_projected(partial):
    rows, rank = partial.shape
    times, spaces = lax.axis_size("tm"), lax.axis_size("space")
    core = lax.axis_index("space") % 2
    half = rows // 2
    halves = partial.reshape(2, half, rank)
    mine = lax.dynamic_index_in_dim(halves, core, 0, keepdims=False)
    other = lax.dynamic_index_in_dim(halves, 1 - core, 0, keepdims=False)

    terms = [mine] + [swap(other if k % 2 else mine, "space", k) for k in range(1, spaces)]
    while len(terms) > 1:
        terms = [a + b for a, b in zip(terms[::2], terms[1::2])]
    piece = terms[0]

    pieces = jnp.stack([piece] + [swap(piece, "tm", k) for k in range(1, times)])
    pieces = pieces[lax.axis_index("tm") ^ jnp.arange(times)]
    theirs = swap(pieces, "space", 1)
    low, high = jnp.where(core == 0, pieces, theirs), jnp.where(core == 0, theirs, pieces)
    return jnp.concatenate([low, high], axis=1).reshape(times * rows, rank)


def on_device(snapshots, space_factor):
    rows, points = snapshots.shape
    times = lax.axis_size("tm")
    scaling = jnp.float32(math.sqrt(times * rows))

    columns = lax.all_to_all(snapshots, "tm", split_axis=1, concat_axis=0, tiled=True)

    projected = gather_projected(matmul(snapshots, space_factor))
    factor = matmul(projected, polar_mixing(inner(projected, projected)))
    own = lax.dynamic_slice_in_dim(factor, lax.axis_index("tm") * rows, rows, axis=0)
    loadings = lax.all_to_all(inner(factor, columns), "tm", split_axis=0, concat_axis=1, tiled=True)
    return (own * scaling, loadings)


def solution(mesh):
    return jax.shard_map(
        on_device,
        mesh=mesh,
        in_specs=(P("tm", "space"), P("space", None)),
        out_specs=(P("tm", None), P("tm", "space")),
        check_vma=False,
    )
```

```python
import functools
import math

import jax
import jax.numpy as jnp
from jax import lax
from jax.experimental import pallas as pl
from jax.experimental.pallas import tpu as pltpu
from jax.sharding import PartitionSpec as P

VMEM_LIMIT = 48 * 1024 * 1024
ANY = pl.BlockSpec(memory_space=pl.ANY)
VMEM = pl.BlockSpec(memory_space=pltpu.VMEM)
PARAMS = pltpu.CompilerParams(vmem_limit_bytes=VMEM_LIMIT)
ROWS_BY_ROWS = (((0,), (0,)), ((), ()))
ROWS_BY_COLUMNS = (((1,), (0,)), ((), ()))


def split(value):
    high = value.astype(jnp.bfloat16)
    return high, (value - high.astype(jnp.float32)).astype(jnp.bfloat16)


def dot(left, right, dims=ROWS_BY_COLUMNS):
    return lax.dot_general(left, right, dims, preferred_element_type=jnp.float32)


def product(left, right, dims=ROWS_BY_COLUMNS):
    (left_high, left_low), (right_high, right_low) = left, right
    return dot(left_high, right_high, dims) + (
        dot(left_high, right_low, dims) + dot(left_low, right_high, dims)
    )


def project_kernel(snapshots_ref, factor_ref, partial_ref):
    rows = snapshots_ref.shape[0]
    high, low = split(snapshots_ref[...])
    factor_high, factor_low = split(factor_ref[...])
    both = dot(jnp.concatenate([high, low], axis=0), factor_high)
    term = both[:rows] + (both[rows:] + dot(high, factor_low))

    @pl.when(pl.program_id(0) == 0)
    def _():
        partial_ref[...] = term

    @pl.when(pl.program_id(0) != 0)
    def _():
        partial_ref[...] += term


def project(snapshots, space_factor):
    rows, points = snapshots.shape
    rank = space_factor.shape[1]
    depth = min(512, points)
    return pl.pallas_call(
        project_kernel,
        grid=(points // depth,),
        in_specs=[
            pl.BlockSpec((rows, depth), lambda i: (0, i)),
            pl.BlockSpec((depth, rank), lambda i: (i, 0)),
        ],
        out_specs=pl.BlockSpec((rows, rank), lambda i: (0, 0)),
        out_shape=jax.ShapeDtypeStruct((rows, rank), jnp.float32),
        compiler_params=PARAMS,
    )(snapshots, space_factor)


def cut_kernel(snapshots_ref, _, parts_ref, sems):
    parts, _, width = parts_ref.shape
    copies = [
        pltpu.make_async_copy(
            snapshots_ref.at[:, pl.ds(i * width, width)], parts_ref.at[i], sems.at[i]
        )
        for i in range(parts)
    ]
    for copy in copies:
        copy.start()
    for copy in copies:
        copy.wait()


def cut(snapshots, parts, after):
    rows, points = snapshots.shape
    if points // parts % 128:
        return snapshots.reshape(rows, parts, points // parts).transpose(1, 0, 2)
    return pl.pallas_call(
        cut_kernel,
        in_specs=[ANY, ANY],
        out_specs=ANY,
        out_shape=jax.ShapeDtypeStruct((parts, rows, points // parts), jnp.float32),
        scratch_shapes=[pltpu.SemaphoreType.DMA((parts,))],
        compiler_params=PARAMS,
    )(snapshots, after)


def mix_kernel(scaling, index_ref, low_ref, high_ref, high_t_ref, low_t_ref, own_ref):
    times, half, rank = low_ref.shape
    projected = jnp.concatenate([low_ref[...], high_ref[...]], axis=1).reshape(times * 2 * half, rank)
    high, low = split(projected)
    cross = dot(high, low, ROWS_BY_ROWS)
    gram = dot(high, high, ROWS_BY_ROWS) + (cross + cross.T)
    diagonal = lax.broadcasted_iota(jnp.int32, (rank, rank), 0) == lax.broadcasted_iota(
        jnp.int32, (rank, rank), 1
    )
    total = jnp.sum(projected * projected)
    correlation = gram / total
    correlation_split = split(correlation)
    square = product(correlation_split, correlation_split)
    tail = jnp.where(diagonal, 1.6875, 0.0) - 0.5625 * correlation + 0.0625 * square
    mixing = (jnp.where(diagonal, 2.25, 0.0) - 2.4375 * correlation) + product(split(square), split(tail))
    factor = product((high, low), split(mixing)) * lax.rsqrt(total)
    factor_high, factor_low = split(factor.T)
    high_t_ref[...] = factor_high
    low_t_ref[...] = factor_low
    rows = 2 * half
    own = jnp.zeros((rows, rank), jnp.float32)
    for i in range(times):
        own = jnp.where(index_ref[0] == i, factor[i * rows : (i + 1) * rows], own)
    own_ref[...] = own * scaling


def mix(index, low, high):
    times, half, rank = low.shape
    total = times * 2 * half
    return pl.pallas_call(
        functools.partial(mix_kernel, math.sqrt(total)),
        in_specs=[pl.BlockSpec(memory_space=pltpu.SMEM), VMEM, VMEM],
        out_specs=[VMEM] * 3,
        out_shape=[
            jax.ShapeDtypeStruct((rank, total), jnp.bfloat16),
            jax.ShapeDtypeStruct((rank, total), jnp.bfloat16),
            jax.ShapeDtypeStruct((2 * half, rank), jnp.float32),
        ],
        compiler_params=PARAMS,
    )(index, low, high)


def load_kernel(high_ref, low_ref, columns_ref, blocks_ref):
    value = product((high_ref[...], low_ref[...]), split(columns_ref[...]))
    blocks_ref[...] = value.reshape(blocks_ref.shape)


def load(high, low, columns, blocks):
    rank, _ = high.shape
    return pl.pallas_call(
        load_kernel,
        in_specs=[VMEM] * 3,
        out_specs=VMEM,
        out_shape=jax.ShapeDtypeStruct((blocks, rank // blocks, columns.shape[1]), jnp.float32),
        compiler_params=PARAMS,
    )(high, low, columns)


def swap(value, axis, offset):
    return lax.ppermute(value, axis, [(i, i ^ offset) for i in range(lax.axis_size(axis))])


def on_device(snapshots, space_factor):
    rows, points = snapshots.shape
    rank = space_factor.shape[1]
    times, spaces = lax.axis_size("tm"), lax.axis_size("space")
    index = lax.axis_index("tm")
    core = lax.axis_index("space") % 2

    halves = project(snapshots, space_factor).reshape(2, rows // 2, rank)
    mine = lax.dynamic_index_in_dim(halves, core, 0, keepdims=False)
    other = lax.dynamic_index_in_dim(halves, 1 - core, 0, keepdims=False)
    terms = [mine] + [swap(other if k % 2 else mine, "space", k) for k in range(1, spaces)]
    while len(terms) > 1:
        terms = [a + b for a, b in zip(terms[::2], terms[1::2])]
    piece = terms[0]

    received = [swap(piece, "tm", k) for k in range(1, times)]
    pieces = jnp.stack([piece] + received)[index ^ jnp.arange(times)]
    theirs = swap(pieces, "space", 1)
    low, high = jnp.where(core == 0, pieces, theirs), jnp.where(core == 0, theirs, pieces)

    columns = lax.all_to_all(cut(snapshots, times, received[0]), "tm", 0, 0, tiled=True)

    high_t, low_t, own = mix(index.reshape(1), low, high)
    blocks = load(high_t, low_t, columns.reshape(times * rows, points // times), times)
    loadings = lax.all_to_all(blocks, "tm", split_axis=0, concat_axis=0, tiled=True)
    return own, loadings.transpose(1, 0, 2).reshape(rank // times, points)


def solution(mesh):
    return jax.shard_map(
        on_device,
        mesh=mesh,
        in_specs=(P("tm", "space"), P("space", None)),
        out_specs=(P("tm", None), P("tm", "space")),
        check_vma=False,
    )
```

```python
import functools
import math

import jax
import jax.numpy as jnp
from jax import lax
from jax.experimental import pallas as pl
from jax.experimental.pallas import tpu as pltpu
from jax.sharding import PartitionSpec as P

MIB = 1024 * 1024
ANY = pl.BlockSpec(memory_space=pl.ANY)
SMEM = pl.BlockSpec(memory_space=pltpu.SMEM)
VMEM = pl.BlockSpec(memory_space=pltpu.VMEM)
ROWS_BY_ROWS = (((0,), (0,)), ((), ()))
ROWS_BY_COLUMNS = (((1,), (0,)), ((), ()))
COLUMNS_BY_COLUMNS = (((1,), (1,)), ((), ()))


def params(mib=48):
    return pltpu.CompilerParams(vmem_limit_bytes=mib * MIB)


def split(value):
    high = value.astype(jnp.bfloat16)
    return high, (value - high.astype(jnp.float32)).astype(jnp.bfloat16)


def dot(left, right, dims=ROWS_BY_COLUMNS):
    return lax.dot_general(left, right, dims, preferred_element_type=jnp.float32)


def product(left, right, dims=ROWS_BY_COLUMNS):
    (left_high, left_low), (right_high, right_low) = left, right
    return dot(left_high, right_high, dims) + (
        dot(left_high, right_low, dims) + dot(left_low, right_high, dims)
    )


def project_kernel(snapshots_ref, factor_ref, partial_ref):
    rows = snapshots_ref.shape[0]
    high, low = split(snapshots_ref[...])
    factor_high, factor_low = split(factor_ref[...])
    both = dot(jnp.concatenate([high, low], axis=0), factor_high)
    term = both[:rows] + (both[rows:] + dot(high, factor_low))

    @pl.when(pl.program_id(0) == 0)
    def _():
        partial_ref[...] = term

    @pl.when(pl.program_id(0) != 0)
    def _():
        partial_ref[...] += term


def project(snapshots, space_factor):
    rows, points = snapshots.shape
    rank = space_factor.shape[1]
    depth = min(512, points)
    return pl.pallas_call(
        project_kernel,
        grid=(points // depth,),
        in_specs=[
            pl.BlockSpec((rows, depth), lambda i: (0, i)),
            pl.BlockSpec((depth, rank), lambda i: (i, 0)),
        ],
        out_specs=pl.BlockSpec((rows, rank), lambda i: (0, 0)),
        out_shape=jax.ShapeDtypeStruct((rows, rank), jnp.float32),
        compiler_params=params(60),
    )(snapshots, space_factor)


def cut_kernel(snapshots_ref, _, *refs):
    *parts, sems = refs
    width = parts[0].shape[1]
    member = lax.rem(lax.axis_index("tm"), len(parts))
    copies = []
    for k, part in enumerate(parts):
        start = pl.multiple_of((member ^ k) * width, width)
        copies.append(pltpu.make_async_copy(snapshots_ref.at[:, pl.ds(start, width)], part, sems.at[k]))
    for copy in copies:
        copy.start()
    for copy in copies:
        copy.wait()


def cut(snapshots, parts, after):
    rows, points = snapshots.shape
    return pl.pallas_call(
        cut_kernel,
        in_specs=[ANY, ANY],
        out_specs=[ANY] * parts,
        out_shape=[jax.ShapeDtypeStruct((rows, points // parts), jnp.float32)] * parts,
        scratch_shapes=[pltpu.SemaphoreType.DMA((parts,))],
        compiler_params=params(),
    )(snapshots, after)


def mix_kernel(times, group, order, index_ref, mine_ref, theirs_ref, high_t_ref, low_t_ref, own_ref):
    total_half, rank = mine_ref.shape
    half = total_half // times
    mine = mine_ref[...].reshape(times, half, rank)
    theirs = theirs_ref[...].reshape(times, half, rank)
    first = index_ref[1] == 0
    low_rows, high_rows = jnp.where(first, mine, theirs), jnp.where(first, theirs, mine)
    projected = jnp.concatenate([low_rows, high_rows], axis=1).reshape(2 * total_half, rank)
    high, low = split(projected)
    cross = dot(high, low, ROWS_BY_ROWS)
    gram = dot(high, high, ROWS_BY_ROWS) + (cross + cross.T)
    diagonal = lax.broadcasted_iota(jnp.int32, (rank, rank), 0) == lax.broadcasted_iota(
        jnp.int32, (rank, rank), 1
    )
    total = jnp.sum(projected * projected)
    correlation = gram / total
    correlation_split = split(correlation)
    square = product(correlation_split, correlation_split)
    tail = jnp.where(diagonal, 1.6875, 0.0) - 0.5625 * correlation + 0.0625 * square
    mixing = (jnp.where(diagonal, 2.25, 0.0) - 2.4375 * correlation) + product(split(square), split(tail))

    mixing_high, mixing_low = split(mixing)

    rows = 2 * half
    places = [order.index(k) for k in range(group)]
    high = jnp.concatenate([high[i * rows : (i + 1) * rows] for i in places], axis=0)
    low = jnp.concatenate([low[i * rows : (i + 1) * rows] for i in places], axis=0)
    scale = lax.rsqrt(total)
    own = product((high[:rows], low[:rows]), (mixing_high, mixing_low))
    own_ref[...] = own * (scale * math.sqrt(times * rows))
    width = rank // times
    row = lax.broadcasted_iota(jnp.int32, (rank, rank), 0)
    source = ((row // width) ^ index_ref[0]) * width + row % width
    move = jnp.where(source == lax.broadcasted_iota(jnp.int32, (rank, rank), 1), 1.0, 0.0).astype(jnp.bfloat16)
    moved = dot(move, jnp.concatenate([mixing_high, mixing_low], axis=1)).astype(jnp.bfloat16)
    turned = product((moved[:, :rank], moved[:, rank:]), (high, low), COLUMNS_BY_COLUMNS) * scale
    turned_high, turned_low = split(turned)
    high_t_ref[...] = turned_high
    low_t_ref[...] = turned_low


def mix(index, mine, theirs, times, group, order):
    total_half, rank = mine.shape
    rows = 2 * total_half // times
    return pl.pallas_call(
        functools.partial(mix_kernel, times, group, order),
        in_specs=[SMEM, VMEM, VMEM],
        out_specs=[VMEM] * 3,
        out_shape=[
            jax.ShapeDtypeStruct((rank, group * rows), jnp.bfloat16),
            jax.ShapeDtypeStruct((rank, group * rows), jnp.bfloat16),
            jax.ShapeDtypeStruct((rows, rank), jnp.float32),
        ],
        compiler_params=params(),
    )(index, mine, theirs)


def load_kernel(group, high_ref, low_ref, *refs):
    parts, blocks = refs[:group], refs[group:]
    columns = jnp.concatenate([part[...] for part in parts], axis=0)
    value = product((high_ref[...], low_ref[...]), split(columns))
    width = value.shape[0] // len(blocks)
    for i, block in enumerate(blocks):
        block[...] = value[i * width : (i + 1) * width]


def load(high, low, parts, blocks):
    rank = high.shape[0]
    columns = parts[0].shape[1]
    return pl.pallas_call(
        functools.partial(load_kernel, len(parts)),
        in_specs=[VMEM] * (2 + len(parts)),
        out_specs=[VMEM] * blocks,
        out_shape=[jax.ShapeDtypeStruct((rank // blocks, columns), jnp.float32)] * blocks,
        compiler_params=params(),
    )(high, low, *parts)


def join_kernel(group, *refs):
    *parts, out_ref = refs
    width = parts[0].shape[1]
    member = lax.rem(lax.axis_index("tm"), group)
    for k in range(group):
        value = parts[k][...]
        if k == 0:
            for term in parts[group:]:
                value = value + term[...]
        out_ref[:, pl.ds(pl.multiple_of((member ^ k) * width, width), width)] = value


def join(parts, terms):
    rows, width = parts[0].shape
    group = len(parts)
    return pl.pallas_call(
        functools.partial(join_kernel, group),
        in_specs=[VMEM] * (group + len(terms)),
        out_specs=VMEM,
        out_shape=jax.ShapeDtypeStruct((rows, group * width), jnp.float32),
        compiler_params=params(),
    )(*parts, *terms)


def swap(value, axis, offset):
    return lax.ppermute(value, axis, [(i, i ^ offset) for i in range(lax.axis_size(axis))])


def on_device(snapshots, space_factor):
    rows, points = snapshots.shape
    rank = space_factor.shape[1]
    times, spaces = lax.axis_size("tm"), lax.axis_size("space")
    group = min(4, times)
    index = lax.axis_index("tm")
    core = lax.axis_index("space") % 2

    partial = project(snapshots, space_factor)
    halves = partial.reshape(2, rows // 2, rank)
    mine = lax.dynamic_index_in_dim(halves, core, 0, keepdims=False)
    other = lax.dynamic_index_in_dim(halves, 1 - core, 0, keepdims=False)
    terms = [mine] + [swap(other if k % 2 else mine, "space", k) for k in range(1, spaces)]
    while len(terms) > 1:
        terms = [a + b for a, b in zip(terms[::2], terms[1::2])]

    pieces, *parts = lax.optimization_barrier((terms[0], *cut(snapshots, group, partial)))
    parts = [part if k == 0 else swap(part, "tm", k) for k, part in enumerate(parts)]

    order = [0]
    offsets = [1 << i for i in range(times.bit_length() - 1)]
    for offset in [o for o in offsets if o >= group] + [o for o in offsets if o < group]:
        pieces = jnp.concatenate([pieces, swap(pieces, "tm", offset)], axis=0)
        if offset < group:
            pieces, parts[offset] = lax.optimization_barrier((pieces, parts[offset]))
        order = order + [k ^ offset for k in order]
    high_t, low_t, own = mix(jnp.stack([index, core]), pieces, swap(pieces, "space", 1), times, group, order)

    blocks = load(high_t, low_t, parts, times)
    sums = []
    for k in [*range(1, group), 0]:
        sums.append([blocks[k]] + [swap(blocks[q + k], "tm", q) for q in range(group, times, group)])
    received = [swap(sum(sums[k - 1][1:], sums[k - 1][0]), "tm", k) for k in range(1, group)]
    last = sums[-1]
    return own, join([last[0], *received], last[1:])


def solution(mesh):
    return jax.shard_map(
        on_device,
        mesh=mesh,
        in_specs=(P("tm", "space"), P("space", None)),
        out_specs=(P("tm", None), P("tm", "space")),
        check_vma=False,
    )
```

```python
import functools
import math

import jax
import jax.numpy as jnp
from jax import lax
from jax.experimental import pallas as pl
from jax.experimental.pallas import tpu as pltpu
from jax.sharding import PartitionSpec as P

MIB = 1024 * 1024
ANY = pl.BlockSpec(memory_space=pl.ANY)
SMEM = pl.BlockSpec(memory_space=pltpu.SMEM)
VMEM = pl.BlockSpec(memory_space=pltpu.VMEM)
ROWS_BY_ROWS = (((0,), (0,)), ((), ()))
ROWS_BY_COLUMNS = (((1,), (0,)), ((), ()))
COLUMNS_BY_COLUMNS = (((1,), (1,)), ((), ()))


def params(mib=48):
    return pltpu.CompilerParams(vmem_limit_bytes=mib * MIB)


def split(value):
    high = value.astype(jnp.bfloat16)
    return high, (value - high.astype(jnp.float32)).astype(jnp.bfloat16)


def dot(left, right, dims=ROWS_BY_COLUMNS):
    return lax.dot_general(left, right, dims, preferred_element_type=jnp.float32)


def product(left, right, dims=ROWS_BY_COLUMNS):
    (left_high, left_low), (right_high, right_low) = left, right
    return dot(left_high, right_high, dims) + (
        dot(left_high, right_low, dims) + dot(left_low, right_high, dims)
    )


def project_kernel(depth, snapshots_ref, factor_ref, mine_ref, other_ref, *refs):
    *parts, snapshots_buf, factor_buf, load_sems, part_sems = refs
    rows, points = snapshots_ref.shape
    half = rows // 2
    loads = []
    for i, start in enumerate(range(0, points, depth)):
        span = pl.ds(start, depth)
        loads.append(
            (
                pltpu.make_async_copy(snapshots_ref.at[:, span], snapshots_buf.at[:, span], load_sems.at[0, i]),
                pltpu.make_async_copy(factor_ref.at[span, :], factor_buf.at[span, :], load_sems.at[1, i]),
            )
        )
        for copy in loads[-1]:
            copy.start()
    width = parts[0].shape[1]
    member = lax.rem(lax.axis_index("tm"), len(parts))
    cuts = []
    for k, part in enumerate(parts):
        start = pl.multiple_of((member ^ k) * width, width)
        cuts.append(pltpu.make_async_copy(snapshots_ref.at[:, pl.ds(start, width)], part, part_sems.at[k]))
        cuts[-1].start()
    value = None
    for i, start in enumerate(range(0, points, depth)):
        for copy in loads[i]:
            copy.wait()
        high, low = split(snapshots_buf[:, start : start + depth])
        factor_high, factor_low = split(factor_buf[start : start + depth, :])
        both = dot(jnp.concatenate([high, low], axis=0), factor_high)
        term = both[:rows] + (both[rows:] + dot(high, factor_low))
        value = term if value is None else value + term
    first = lax.rem(lax.axis_index("space"), 2) == 0
    mine_ref[...] = jnp.where(first, value[:half], value[half:])
    other_ref[...] = jnp.where(first, value[half:], value[:half])
    for copy in cuts:
        copy.wait()


def project(snapshots, space_factor, group):
    rows, points = snapshots.shape
    rank = space_factor.shape[1]
    depth = min(512, points)
    half = jax.ShapeDtypeStruct((rows // 2, rank), jnp.float32)
    part = jax.ShapeDtypeStruct((rows, points // group), jnp.float32)
    mine, other, *parts = pl.pallas_call(
        functools.partial(project_kernel, depth),
        in_specs=[ANY, ANY],
        out_specs=[VMEM] * (2 + group),
        out_shape=[half, half] + [part] * group,
        scratch_shapes=[
            pltpu.VMEM((rows, points), jnp.float32),
            pltpu.VMEM((points, rank), jnp.float32),
            pltpu.SemaphoreType.DMA((2, points // depth)),
            pltpu.SemaphoreType.DMA((group,)),
        ],
        compiler_params=params(60),
    )(snapshots, space_factor)
    return mine, other, parts


def mix_kernel(times, group, order, index_ref, mine_ref, theirs_ref, high_t_ref, low_t_ref, own_ref):
    total_half, rank = mine_ref.shape
    half = total_half // times
    mine = mine_ref[...].reshape(times, half, rank)
    theirs = theirs_ref[...].reshape(times, half, rank)
    first = index_ref[1] == 0
    low_rows, high_rows = jnp.where(first, mine, theirs), jnp.where(first, theirs, mine)
    projected = jnp.concatenate([low_rows, high_rows], axis=1).reshape(2 * total_half, rank)
    high, low = split(projected)
    cross = dot(high, low, ROWS_BY_ROWS)
    gram = dot(high, high, ROWS_BY_ROWS) + (cross + cross.T)
    diagonal = lax.broadcasted_iota(jnp.int32, (rank, rank), 0) == lax.broadcasted_iota(
        jnp.int32, (rank, rank), 1
    )
    total = jnp.sum(projected * projected)
    correlation = gram / total
    correlation_split = split(correlation)
    square = product(correlation_split, correlation_split)
    tail = jnp.where(diagonal, 1.6875, 0.0) - 0.5625 * correlation + 0.0625 * square
    mixing = (jnp.where(diagonal, 2.25, 0.0) - 2.4375 * correlation) + product(split(square), split(tail))

    mixing_high, mixing_low = split(mixing)

    rows = 2 * half
    places = [order.index(k) for k in range(group)]
    high = jnp.concatenate([high[i * rows : (i + 1) * rows] for i in places], axis=0)
    low = jnp.concatenate([low[i * rows : (i + 1) * rows] for i in places], axis=0)
    scale = lax.rsqrt(total)
    own = product((high[:rows], low[:rows]), (mixing_high, mixing_low))
    own_ref[...] = own * (scale * math.sqrt(times * rows))
    width = rank // times
    row = lax.broadcasted_iota(jnp.int32, (rank, rank), 0)
    source = ((row // width) ^ index_ref[0]) * width + row % width
    move = jnp.where(source == lax.broadcasted_iota(jnp.int32, (rank, rank), 1), 1.0, 0.0).astype(jnp.bfloat16)
    moved = dot(move, jnp.concatenate([mixing_high, mixing_low], axis=1)).astype(jnp.bfloat16)
    turned = product((moved[:, :rank], moved[:, rank:]), (high, low), COLUMNS_BY_COLUMNS) * scale
    turned_high, turned_low = split(turned)
    high_t_ref[...] = turned_high
    low_t_ref[...] = turned_low


def mix(index, mine, theirs, times, group, order):
    total_half, rank = mine.shape
    rows = 2 * total_half // times
    return pl.pallas_call(
        functools.partial(mix_kernel, times, group, order),
        in_specs=[SMEM, VMEM, VMEM],
        out_specs=[VMEM] * 3,
        out_shape=[
            jax.ShapeDtypeStruct((rank, group * rows), jnp.bfloat16),
            jax.ShapeDtypeStruct((rank, group * rows), jnp.bfloat16),
            jax.ShapeDtypeStruct((rows, rank), jnp.float32),
        ],
        compiler_params=params(),
    )(index, mine, theirs)


def load_kernel(group, high_ref, low_ref, *refs):
    parts, blocks = refs[:group], refs[group:]
    columns = jnp.concatenate([part[...] for part in parts], axis=0)
    value = product((high_ref[...], low_ref[...]), split(columns))
    width = value.shape[0] // len(blocks)
    for i, block in enumerate(blocks):
        block[...] = value[i * width : (i + 1) * width]


def load(high, low, parts, blocks):
    rank = high.shape[0]
    columns = parts[0].shape[1]
    return pl.pallas_call(
        functools.partial(load_kernel, len(parts)),
        in_specs=[VMEM] * (2 + len(parts)),
        out_specs=[VMEM] * blocks,
        out_shape=[jax.ShapeDtypeStruct((rank // blocks, columns), jnp.float32)] * blocks,
        compiler_params=params(),
    )(high, low, *parts)


def join_kernel(group, *refs):
    *parts, out_ref = refs
    width = parts[0].shape[1]
    member = lax.rem(lax.axis_index("tm"), group)
    for k in range(group):
        value = parts[k][...]
        if k == 0:
            for term in parts[group:]:
                value = value + term[...]
        out_ref[:, pl.ds(pl.multiple_of((member ^ k) * width, width), width)] = value


def join(parts, terms):
    rows, width = parts[0].shape
    group = len(parts)
    return pl.pallas_call(
        functools.partial(join_kernel, group),
        in_specs=[VMEM] * (group + len(terms)),
        out_specs=VMEM,
        out_shape=jax.ShapeDtypeStruct((rows, group * width), jnp.float32),
        compiler_params=params(),
    )(*parts, *terms)


def swap(value, axis, offset):
    return lax.ppermute(value, axis, [(i, i ^ offset) for i in range(lax.axis_size(axis))])


def on_device(snapshots, space_factor):
    rows, points = snapshots.shape
    rank = space_factor.shape[1]
    times, spaces = lax.axis_size("tm"), lax.axis_size("space")
    group = min(4, times)
    index = lax.axis_index("tm")
    core = lax.axis_index("space") % 2

    mine, other, parts = project(snapshots, space_factor, group)
    parts = [part if k == 0 else swap(part, "tm", k) for k, part in enumerate(parts)]

    terms = [mine] + [swap(other if k % 2 else mine, "space", k) for k in range(1, spaces)]
    while len(terms) > 1:
        terms = [a + b for a, b in zip(terms[::2], terms[1::2])]

    pieces, order = terms[0], [0]
    offsets = [1 << i for i in range(times.bit_length() - 1)]
    for offset in [o for o in offsets if o >= group] + [o for o in offsets if o < group]:
        pieces = jnp.concatenate([pieces, swap(pieces, "tm", offset)], axis=0)
        if offset < group:
            pieces, parts[offset] = lax.optimization_barrier((pieces, parts[offset]))
        order = order + [k ^ offset for k in order]
    theirs, *parts = lax.optimization_barrier((swap(pieces, "space", 1), *parts))
    high_t, low_t, own = mix(jnp.stack([index, core]), pieces, theirs, times, group, order)

    blocks = load(high_t, low_t, parts, times)
    sums, arrived = {}, []
    for i, k in enumerate(reversed(range(group))):
        terms = [blocks[q + k] for q in range(group, times, group)]
        if i >= 2:
            terms, arrived[i - 2] = lax.optimization_barrier((terms, arrived[i - 2]))
        arrived.append([swap(term, "tm", q) for term, q in zip(terms, range(group, times, group))])
    received = []
    for k in range(1, group):
        received.append(swap(sum(arrived[group - 1 - k], blocks[k]), "tm", k))
    return own, join([blocks[0], *received], arrived[-1])


def solution(mesh):
    return jax.shard_map(
        on_device,
        mesh=mesh,
        in_specs=(P("tm", "space"), P("space", None)),
        out_specs=(P("tm", None), P("tm", "space")),
        check_vma=False,
    )
```

```python
import functools
import math

import jax
import jax.numpy as jnp
from jax import lax
from jax.experimental import pallas as pl
from jax.experimental.pallas import tpu as pltpu
from jax.sharding import PartitionSpec as P

MIB = 1024 * 1024
HBM = pl.BlockSpec(memory_space=pltpu.HBM)
SMEM = pl.BlockSpec(memory_space=pltpu.SMEM)
VMEM = pl.BlockSpec(memory_space=pltpu.VMEM)
ROWS_BY_ROWS = (((0,), (0,)), ((), ()))
ROWS_BY_COLUMNS = (((1,), (0,)), ((), ()))
COLUMNS_BY_COLUMNS = (((1,), (1,)), ((), ()))


def params(mib=48):
    return pltpu.CompilerParams(vmem_limit_bytes=mib * MIB)


def split(value):
    high = value.astype(jnp.bfloat16)
    return high, (value - high.astype(jnp.float32)).astype(jnp.bfloat16)


def dot(left, right, dims=ROWS_BY_COLUMNS):
    return lax.dot_general(left, right, dims, preferred_element_type=jnp.float32)


def product(left, right, dims=ROWS_BY_COLUMNS):
    (left_high, left_low), (right_high, right_low) = left, right
    return dot(left_high, right_high, dims) + (
        dot(left_high, right_low, dims) + dot(left_low, right_high, dims)
    )


def project_kernel(depth, snapshots_ref, factor_ref, mine_ref, other_ref, *refs):
    *parts, snapshots_buf, factor_buf, sems = refs
    rows, points = snapshots_ref.shape
    half = rows // 2
    snapshots_copy = pltpu.make_async_copy(snapshots_ref, snapshots_buf, sems.at[points // depth])
    snapshots_copy.start()
    copies = []
    for i, start in enumerate(range(0, points, depth)):
        span = pl.ds(start, depth)
        copies.append(pltpu.make_async_copy(factor_ref.at[span, :], factor_buf.at[span, :], sems.at[i]))
        copies[-1].start()
    snapshots_copy.wait()
    width = parts[0].shape[1]
    member = lax.rem(lax.axis_index("tm"), len(parts))
    for k, part in enumerate(parts):
        part[...] = snapshots_buf[:, pl.ds(pl.multiple_of((member ^ k) * width, width), width)]
    value = None
    for i, start in enumerate(range(0, points, depth)):
        copies[i].wait()
        high, low = split(snapshots_buf[:, start : start + depth])
        factor_high, factor_low = split(factor_buf[start : start + depth, :])
        both = dot(jnp.concatenate([high, low], axis=0), factor_high)
        term = both[:rows] + (both[rows:] + dot(high, factor_low))
        value = term if value is None else value + term
    first = lax.rem(lax.axis_index("space"), 2) == 0
    mine_ref[...] = jnp.where(first, value[:half], value[half:])
    other_ref[...] = jnp.where(first, value[half:], value[:half])


def project(snapshots, space_factor, group):
    rows, points = snapshots.shape
    rank = space_factor.shape[1]
    depth = min(512, points)
    half = jax.ShapeDtypeStruct((rows // 2, rank), jnp.float32)
    part = jax.ShapeDtypeStruct((rows, points // group), jnp.float32)
    mine, other, *parts = pl.pallas_call(
        functools.partial(project_kernel, depth),
        in_specs=[HBM, HBM],
        out_specs=[VMEM] * (2 + group),
        out_shape=[half, half] + [part] * group,
        scratch_shapes=[
            pltpu.VMEM((rows, points), jnp.float32),
            pltpu.VMEM((points, rank), jnp.float32),
            pltpu.SemaphoreType.DMA((points // depth + 1,)),
        ],
        compiler_params=params(52),
    )(snapshots, space_factor)
    return mine, other, parts


def load_kernel(times, group, order, index_ref, mine_ref, theirs_ref, *refs):
    parts, own_ref, blocks = refs[:group], refs[group], refs[group + 1 :]
    total_half, rank = mine_ref.shape
    half = total_half // times
    mine = mine_ref[...].reshape(times, half, rank)
    theirs = theirs_ref[...].reshape(times, half, rank)
    first = index_ref[1] == 0
    low_rows, high_rows = jnp.where(first, mine, theirs), jnp.where(first, theirs, mine)
    projected = jnp.concatenate([low_rows, high_rows], axis=1).reshape(2 * total_half, rank)
    high, low = split(projected)
    cross = dot(high, low, ROWS_BY_ROWS)
    gram = dot(high, high, ROWS_BY_ROWS) + (cross + cross.T)
    diagonal = lax.broadcasted_iota(jnp.int32, (rank, rank), 0) == lax.broadcasted_iota(
        jnp.int32, (rank, rank), 1
    )
    total = jnp.sum(projected * projected)
    correlation = gram / total
    correlation_split = split(correlation)
    square = product(correlation_split, correlation_split)
    tail = jnp.where(diagonal, 1.6875, 0.0) - 0.5625 * correlation + 0.0625 * square
    mixing = (jnp.where(diagonal, 2.25, 0.0) - 2.4375 * correlation) + product(split(square), split(tail))

    mixing_high, mixing_low = split(mixing)

    rows = 2 * half
    places = [order.index(k) for k in range(group)]
    high = jnp.concatenate([high[i * rows : (i + 1) * rows] for i in places], axis=0)
    low = jnp.concatenate([low[i * rows : (i + 1) * rows] for i in places], axis=0)
    scale = lax.rsqrt(total)
    own = product((high[:rows], low[:rows]), (mixing_high, mixing_low))
    own_ref[...] = own * (scale * math.sqrt(times * rows))
    width = rank // times
    row = lax.broadcasted_iota(jnp.int32, (rank, rank), 0)
    source = ((row // width) ^ index_ref[0]) * width + row % width
    move = jnp.where(source == lax.broadcasted_iota(jnp.int32, (rank, rank), 1), 1.0, 0.0).astype(jnp.bfloat16)
    moved = dot(move, jnp.concatenate([mixing_high, mixing_low], axis=1)).astype(jnp.bfloat16)
    turned = product((moved[:, :rank], moved[:, rank:]), (high, low), COLUMNS_BY_COLUMNS) * scale
    columns = jnp.concatenate([part[...] for part in parts], axis=0)
    value = product(split(turned), split(columns))
    for i, block in enumerate(blocks):
        block[...] = value[i * width : (i + 1) * width]


def load(index, mine, theirs, parts, times, order):
    total_half, rank = mine.shape
    rows = 2 * total_half // times
    group = len(parts)
    columns = parts[0].shape[1]
    own, *blocks = pl.pallas_call(
        functools.partial(load_kernel, times, group, order),
        in_specs=[SMEM] + [VMEM] * (2 + group),
        out_specs=[VMEM] * (1 + times),
        out_shape=[jax.ShapeDtypeStruct((rows, rank), jnp.float32)]
        + [jax.ShapeDtypeStruct((rank // times, columns), jnp.float32)] * times,
        compiler_params=params(),
    )(index, mine, theirs, *parts)
    return own, blocks


def join_kernel(group, *refs):
    *parts, out_ref = refs
    width = parts[0].shape[1]
    member = lax.rem(lax.axis_index("tm"), group)
    for k in range(group):
        value = parts[k][...]
        if k == 0:
            for term in parts[group:]:
                value = value + term[...]
        out_ref[:, pl.ds(pl.multiple_of((member ^ k) * width, width), width)] = value


def join(parts, terms):
    rows, width = parts[0].shape
    group = len(parts)
    return pl.pallas_call(
        functools.partial(join_kernel, group),
        in_specs=[VMEM] * (group + len(terms)),
        out_specs=VMEM,
        out_shape=jax.ShapeDtypeStruct((rows, group * width), jnp.float32),
        compiler_params=params(),
    )(*parts, *terms)


def swap(value, axis, offset):
    return lax.ppermute(value, axis, [(i, i ^ offset) for i in range(lax.axis_size(axis))])


def on_device(snapshots, space_factor):
    rows, points = snapshots.shape
    rank = space_factor.shape[1]
    times, spaces = lax.axis_size("tm"), lax.axis_size("space")
    group = min(4, times)
    index = lax.axis_index("tm")
    core = lax.axis_index("space") % 2

    mine, other, parts = project(snapshots, space_factor, group)
    parts = [part if k == 0 else swap(part, "tm", k) for k, part in enumerate(parts)]

    terms = [mine] + [swap(other if k % 2 else mine, "space", k) for k in range(1, spaces)]
    while len(terms) > 1:
        terms = [a + b for a, b in zip(terms[::2], terms[1::2])]

    pieces, order = terms[0], [0]
    offsets = [1 << i for i in range(times.bit_length() - 1)]
    for offset in [o for o in offsets if o >= group] + [o for o in offsets if o < group]:
        pieces = jnp.concatenate([pieces, swap(pieces, "tm", offset)], axis=0)
        if len(order) == 1:
            pieces, parts[1:-1] = lax.optimization_barrier((pieces, parts[1:-1]))
        elif len(order) == 2:
            pieces, parts[-1] = lax.optimization_barrier((pieces, parts[-1]))
        order = order + [k ^ offset for k in order]
    theirs = swap(pieces, "space", 1)

    own, blocks = load(jnp.stack([index, core]), pieces, theirs, parts, times, order)
    arrived = []
    for i, k in enumerate(reversed(range(group))):
        terms = [blocks[q + k] for q in range(group, times, group)]
        if i >= 2:
            terms, arrived[i - 2] = lax.optimization_barrier((terms, arrived[i - 2]))
        arrived.append([swap(term, "tm", q) for term, q in zip(terms, range(group, times, group))])
    received = []
    for k in range(1, group):
        received.append(swap(sum(arrived[group - 1 - k], blocks[k]), "tm", k))
    return own, join([blocks[0], *received], arrived[-1])


def solution(mesh):
    return jax.shard_map(
        on_device,
        mesh=mesh,
        in_specs=(P("tm", "space"), P("space", None)),
        out_specs=(P("tm", None), P("tm", "space")),
        check_vma=False,
    )
```

```python
import functools
import math

import jax
import jax.numpy as jnp
from jax import lax
from jax.experimental import pallas as pl
from jax.experimental.pallas import tpu as pltpu
from jax.sharding import PartitionSpec as P

MIB = 1024 * 1024
HBM = pl.BlockSpec(memory_space=pltpu.HBM)
SMEM = pl.BlockSpec(memory_space=pltpu.SMEM)
VMEM = pl.BlockSpec(memory_space=pltpu.VMEM)
FREE = pl.CostEstimate(flops=0, bytes_accessed=0, transcendentals=0)
ROWS_BY_ROWS = (((0,), (0,)), ((), ()))
ROWS_BY_COLUMNS = (((1,), (0,)), ((), ()))


def params(mib=48):
    return pltpu.CompilerParams(vmem_limit_bytes=mib * MIB)


def split(value):
    high = value.astype(jnp.bfloat16)
    return high, (value - high.astype(jnp.float32)).astype(jnp.bfloat16)


def dot(left, right, dims=ROWS_BY_COLUMNS):
    return lax.dot_general(left, right, dims, preferred_element_type=jnp.float32)


def product(left, right, dims=ROWS_BY_COLUMNS):
    (left_high, left_low), (right_high, right_low) = left, right
    return dot(left_high, right_high, dims) + (
        dot(left_high, right_low, dims) + dot(left_low, right_high, dims)
    )


def cut_kernel(snapshots_ref, parts_ref, sems):
    parts, _, width = parts_ref.shape
    copies = [
        pltpu.make_async_copy(snapshots_ref.at[:, pl.ds(i * width, width)], parts_ref.at[i], sems.at[i])
        for i in range(parts)
    ]
    for copy in copies:
        copy.start()
    for copy in copies:
        copy.wait()


def cut(snapshots, parts):
    rows, points = snapshots.shape
    width = points // parts
    if width % 128:
        return snapshots.reshape(rows, parts, width).transpose(1, 0, 2)
    return pl.pallas_call(
        cut_kernel,
        in_specs=[HBM],
        out_specs=VMEM,
        out_shape=jax.ShapeDtypeStruct((parts, rows, width), jnp.float32),
        scratch_shapes=[pltpu.SemaphoreType.DMA((parts,))],
        compiler_params=params(52),
        cost_estimate=FREE,
    )(snapshots)


def project_kernel(depth, snapshots_ref, factor_ref, mine_ref, other_ref, snapshots_buf, factor_buf, sems):
    rows, points = snapshots_ref.shape
    half = rows // 2
    snapshots_copy = pltpu.make_async_copy(snapshots_ref, snapshots_buf, sems.at[points // depth])
    snapshots_copy.start()
    copies = []
    for i, start in enumerate(range(0, points, depth)):
        span = pl.ds(start, depth)
        copies.append(pltpu.make_async_copy(factor_ref.at[span, :], factor_buf.at[span, :], sems.at[i]))
        copies[-1].start()
    snapshots_copy.wait()
    value = None
    for i, start in enumerate(range(0, points, depth)):
        copies[i].wait()
        high, low = split(snapshots_buf[:, start : start + depth])
        factor_high, factor_low = split(factor_buf[start : start + depth, :])
        both = dot(jnp.concatenate([high, low], axis=0), factor_high)
        term = both[:rows] + (both[rows:] + dot(high, factor_low))
        value = term if value is None else value + term
    first = lax.rem(lax.axis_index("space"), 2) == 0
    mine_ref[...] = jnp.where(first, value[:half], value[half:])
    other_ref[...] = jnp.where(first, value[half:], value[:half])


def project(snapshots, space_factor):
    rows, points = snapshots.shape
    rank = space_factor.shape[1]
    depth = min(512, points)
    half = jax.ShapeDtypeStruct((rows // 2, rank), jnp.float32)
    return pl.pallas_call(
        functools.partial(project_kernel, depth),
        in_specs=[HBM, HBM],
        out_specs=[VMEM] * 2,
        out_shape=[half] * 2,
        scratch_shapes=[
            pltpu.VMEM((rows, points), jnp.float32),
            pltpu.VMEM((points, rank), jnp.float32),
            pltpu.SemaphoreType.DMA((points // depth + 1,)),
        ],
        compiler_params=params(53),
        cost_estimate=FREE,
    )(snapshots, space_factor)


def mix_kernel(times, core_ref, mine_ref, theirs_ref, high_t_ref, low_t_ref, own_ref):
    total_half, rank = mine_ref.shape
    half = total_half // times
    mine = mine_ref[...].reshape(times, half, rank)
    theirs = theirs_ref[...].reshape(times, half, rank)
    first = core_ref[0] == 0
    low_rows, high_rows = jnp.where(first, mine, theirs), jnp.where(first, theirs, mine)
    projected = jnp.concatenate([low_rows, high_rows], axis=1).reshape(2 * total_half, rank)
    high, low = split(projected)
    cross = dot(high, low, ROWS_BY_ROWS)
    gram = dot(high, high, ROWS_BY_ROWS) + (cross + cross.T)
    diagonal = lax.broadcasted_iota(jnp.int32, (rank, rank), 0) == lax.broadcasted_iota(
        jnp.int32, (rank, rank), 1
    )
    total = jnp.sum(projected * projected)
    correlation = gram / total
    correlation_split = split(correlation)
    square = product(correlation_split, correlation_split)
    tail = jnp.where(diagonal, 1.6875, 0.0) - 0.5625 * correlation + 0.0625 * square
    mixing = (jnp.where(diagonal, 2.25, 0.0) - 2.4375 * correlation) + product(split(square), split(tail))
    scale = lax.rsqrt(total)
    factor = product((high, low), split(mixing)) * scale
    rows = 2 * half
    own_ref[...] = factor[:rows] * math.sqrt(times * rows)
    high_t_ref[...], low_t_ref[...] = split(factor.T)


def mix(core, mine, theirs, times):
    total_half, rank = mine.shape
    total = 2 * total_half
    return pl.pallas_call(
        functools.partial(mix_kernel, times),
        in_specs=[SMEM, VMEM, VMEM],
        out_specs=[VMEM] * 3,
        out_shape=[
            jax.ShapeDtypeStruct((rank, total), jnp.bfloat16),
            jax.ShapeDtypeStruct((rank, total), jnp.bfloat16),
            jax.ShapeDtypeStruct((total // times, rank), jnp.float32),
        ],
        compiler_params=params(),
        cost_estimate=FREE,
    )(core, mine, theirs)


def load_kernel(order, index_ref, high_ref, low_ref, columns_ref, blocks_ref):
    columns = jnp.concatenate([columns_ref[index_ref[0] ^ k] for k in order], axis=0)
    value = product((high_ref[...], low_ref[...]), split(columns))
    blocks_ref[...] = value.reshape(blocks_ref.shape)


def load(index, high, low, columns, order):
    rank, _ = high.shape
    blocks, _, width = columns.shape
    return pl.pallas_call(
        functools.partial(load_kernel, order),
        in_specs=[SMEM] + [VMEM] * 3,
        out_specs=VMEM,
        out_shape=jax.ShapeDtypeStruct((blocks, rank // blocks, width), jnp.float32),
        compiler_params=params(),
        cost_estimate=FREE,
    )(index, high, low, columns)


def swap(value, axis, offset):
    return lax.ppermute(value, axis, [(i, i ^ offset) for i in range(lax.axis_size(axis))])


def on_device(snapshots, space_factor):
    rows, points = snapshots.shape
    rank = space_factor.shape[1]
    times, spaces = lax.axis_size("tm"), lax.axis_size("space")
    index = lax.axis_index("tm")
    core = lax.axis_index("space") % 2

    snapshots, parts = lax.optimization_barrier((snapshots, cut(snapshots, times)))
    columns = lax.all_to_all(parts, "tm", 0, 0, tiled=True)

    mine, other = project(snapshots, space_factor)
    mine = mine + swap(other, "space", 1)
    for i in range(1, spaces.bit_length() - 1):
        mine = mine + swap(mine, "space", 1 << i)

    order = [0]
    for i in range(times.bit_length() - 1):
        mine = jnp.concatenate([mine, swap(mine, "tm", 1 << i)], axis=0)
        order = order + [k ^ 1 << i for k in order]
    high_t, low_t, own = mix(core.reshape(1), mine, swap(mine, "space", 1), times)

    blocks = load(index.reshape(1), high_t, low_t, columns, order)
    loadings = lax.all_to_all(blocks, "tm", 0, 0, tiled=True)
    return own, loadings.transpose(1, 0, 2).reshape(rank // times, points)


def solution(mesh):
    return jax.shard_map(
        on_device,
        mesh=mesh,
        in_specs=(P("tm", "space"), P("space", None)),
        out_specs=(P("tm", None), P("tm", "space")),
        check_vma=False,
    )
```

```python
import functools
import math

import jax
import jax.numpy as jnp
from jax import lax
from jax.experimental import pallas as pl
from jax.experimental.pallas import tpu as pltpu
from jax.sharding import PartitionSpec as P

MIB = 1024 * 1024
HBM = pl.BlockSpec(memory_space=pltpu.HBM)
SMEM = pl.BlockSpec(memory_space=pltpu.SMEM)
VMEM = pl.BlockSpec(memory_space=pltpu.VMEM)
FREE = pl.CostEstimate(flops=0, bytes_accessed=0, transcendentals=0)
ROWS_BY_ROWS = (((0,), (0,)), ((), ()))
ROWS_BY_COLUMNS = (((1,), (0,)), ((), ()))


def params(mib=48):
    return pltpu.CompilerParams(vmem_limit_bytes=mib * MIB)


def split(value):
    high = value.astype(jnp.bfloat16)
    return high, (value - high.astype(jnp.float32)).astype(jnp.bfloat16)


def dot(left, right, dims=ROWS_BY_COLUMNS):
    return lax.dot_general(left, right, dims, preferred_element_type=jnp.float32)


def product(left, right, dims=ROWS_BY_COLUMNS):
    (left_high, left_low), (right_high, right_low) = left, right
    return dot(left_high, right_high, dims) + (
        dot(left_high, right_low, dims) + dot(left_low, right_high, dims)
    )


def cut_kernel(step, snapshots_ref, parts_ref, buf, sems):
    parts, rows, width = parts_ref.shape
    spans = [pl.ds(start, step) for start in range(0, rows, step)]
    copies = [
        pltpu.make_async_copy(snapshots_ref.at[span, :], buf.at[span, :], sems.at[i]) for i, span in enumerate(spans)
    ]
    for copy in copies:
        copy.start()
    for copy, span in zip(copies, spans):
        copy.wait()
        for i in range(parts):
            parts_ref[i, span, :] = buf[span, i * width : (i + 1) * width]


def cut(snapshots, parts):
    rows, points = snapshots.shape
    width = points // parts
    if width % 128:
        return snapshots.reshape(rows, parts, width).transpose(1, 0, 2)
    step = 8 if rows % 8 == 0 else rows
    return pl.pallas_call(
        functools.partial(cut_kernel, step),
        in_specs=[HBM],
        out_specs=VMEM,
        out_shape=jax.ShapeDtypeStruct((parts, rows, width), jnp.float32),
        scratch_shapes=[pltpu.VMEM((rows, points), jnp.float32), pltpu.SemaphoreType.DMA((rows // step,))],
        compiler_params=params(52),
        cost_estimate=FREE,
    )(snapshots)


def project_kernel(depth, snapshots_ref, factor_ref, mine_ref, other_ref, snapshots_buf, factor_buf, sems):
    rows, points = snapshots_ref.shape
    half = rows // 2
    snapshots_copy = pltpu.make_async_copy(snapshots_ref, snapshots_buf, sems.at[points // depth])
    snapshots_copy.start()
    copies = []
    for i, start in enumerate(range(0, points, depth)):
        span = pl.ds(start, depth)
        copies.append(pltpu.make_async_copy(factor_ref.at[span, :], factor_buf.at[span, :], sems.at[i]))
        copies[-1].start()
    snapshots_copy.wait()
    value = None
    for i, start in enumerate(range(0, points, depth)):
        copies[i].wait()
        high, low = split(snapshots_buf[:, start : start + depth])
        factor_high, factor_low = split(factor_buf[start : start + depth, :])
        both = dot(jnp.concatenate([high, low], axis=0), factor_high)
        term = both[:rows] + (both[rows:] + dot(high, factor_low))
        value = term if value is None else value + term
    first = lax.rem(lax.axis_index("space"), 2) == 0
    mine_ref[...] = jnp.where(first, value[:half], value[half:])
    other_ref[...] = jnp.where(first, value[half:], value[:half])


def project(snapshots, space_factor):
    rows, points = snapshots.shape
    rank = space_factor.shape[1]
    depth = min(512, points)
    half = jax.ShapeDtypeStruct((rows // 2, rank), jnp.float32)
    return pl.pallas_call(
        functools.partial(project_kernel, depth),
        in_specs=[HBM, HBM],
        out_specs=[VMEM] * 2,
        out_shape=[half] * 2,
        scratch_shapes=[
            pltpu.VMEM((rows, points), jnp.float32),
            pltpu.VMEM((points, rank), jnp.float32),
            pltpu.SemaphoreType.DMA((points // depth + 1,)),
        ],
        compiler_params=params(53),
        cost_estimate=FREE,
    )(snapshots, space_factor)


def mix_kernel(times, core_ref, mine_ref, theirs_ref, high_t_ref, low_t_ref, own_ref):
    total_half, rank = mine_ref.shape
    half = total_half // times
    mine = mine_ref[...].reshape(times, half, rank)
    theirs = theirs_ref[...].reshape(times, half, rank)
    first = core_ref[0] == 0
    low_rows, high_rows = jnp.where(first, mine, theirs), jnp.where(first, theirs, mine)
    projected = jnp.concatenate([low_rows, high_rows], axis=1).reshape(2 * total_half, rank)
    high, low = split(projected)
    cross = dot(high, low, ROWS_BY_ROWS)
    gram = dot(high, high, ROWS_BY_ROWS) + (cross + cross.T)
    diagonal = lax.broadcasted_iota(jnp.int32, (rank, rank), 0) == lax.broadcasted_iota(
        jnp.int32, (rank, rank), 1
    )
    total = jnp.sum(projected * projected)
    correlation = gram / total
    correlation_split = split(correlation)
    square = product(correlation_split, correlation_split)
    tail = jnp.where(diagonal, 1.6875, 0.0) - 0.5625 * correlation + 0.0625 * square
    mixing = (jnp.where(diagonal, 2.25, 0.0) - 2.4375 * correlation) + product(split(square), split(tail))
    scale = lax.rsqrt(total)
    factor = product((high, low), split(mixing)) * scale
    rows = 2 * half
    own_ref[...] = factor[:rows] * math.sqrt(times * rows)
    high_t_ref[...], low_t_ref[...] = split(factor.T)


def mix(core, mine, theirs, times):
    total_half, rank = mine.shape
    total = 2 * total_half
    return pl.pallas_call(
        functools.partial(mix_kernel, times),
        in_specs=[SMEM, VMEM, VMEM],
        out_specs=[VMEM] * 3,
        out_shape=[
            jax.ShapeDtypeStruct((rank, total), jnp.bfloat16),
            jax.ShapeDtypeStruct((rank, total), jnp.bfloat16),
            jax.ShapeDtypeStruct((total // times, rank), jnp.float32),
        ],
        compiler_params=params(),
        cost_estimate=FREE,
    )(core, mine, theirs)


def load_kernel(order, index_ref, high_ref, low_ref, columns_ref, blocks_ref):
    columns = jnp.concatenate([columns_ref[index_ref[0] ^ k] for k in order], axis=0)
    value = product((high_ref[...], low_ref[...]), split(columns))
    blocks_ref[...] = value.reshape(blocks_ref.shape)


def load(index, high, low, columns, order):
    rank, _ = high.shape
    blocks, _, width = columns.shape
    return pl.pallas_call(
        functools.partial(load_kernel, order),
        in_specs=[SMEM] + [VMEM] * 3,
        out_specs=VMEM,
        out_shape=jax.ShapeDtypeStruct((blocks, rank // blocks, width), jnp.float32),
        compiler_params=params(),
        cost_estimate=FREE,
    )(index, high, low, columns)


def swap(value, axis, offset):
    return lax.ppermute(value, axis, [(i, i ^ offset) for i in range(lax.axis_size(axis))])


def on_device(snapshots, space_factor):
    rows, points = snapshots.shape
    rank = space_factor.shape[1]
    times, spaces = lax.axis_size("tm"), lax.axis_size("space")
    index = lax.axis_index("tm")
    core = lax.axis_index("space") % 2

    snapshots, parts = lax.optimization_barrier((snapshots, cut(snapshots, times)))
    columns = lax.all_to_all(parts, "tm", 0, 0, tiled=True)

    mine, other = project(snapshots, space_factor)
    mine = mine + swap(other, "space", 1)
    for i in range(1, spaces.bit_length() - 1):
        mine = mine + swap(mine, "space", 1 << i)

    order, bits = [0], range(times.bit_length() - 1)
    for i in [*bits[2:], *bits[:2]]:
        mine = jnp.concatenate([mine, swap(mine, "tm", 1 << i)], axis=0)
        order = order + [k ^ 1 << i for k in order]
    high_t, low_t, own = mix(core.reshape(1), mine, swap(mine, "space", 1), times)

    blocks = load(index.reshape(1), high_t, low_t, columns, order)
    loadings = lax.all_to_all(blocks, "tm", 0, 0, tiled=True)
    return own, loadings.transpose(1, 0, 2).reshape(rank // times, points)


def solution(mesh):
    return jax.shard_map(
        on_device,
        mesh=mesh,
        in_specs=(P("tm", "space"), P("space", None)),
        out_specs=(P("tm", None), P("tm", "space")),
        check_vma=False,
    )
```

```python
import functools
import math

import jax
import jax.numpy as jnp
from jax import lax
from jax.experimental import pallas as pl
from jax.experimental.pallas import tpu as pltpu
from jax.sharding import PartitionSpec as P

MIB = 1024 * 1024
HBM = pl.BlockSpec(memory_space=pltpu.HBM)
SMEM = pl.BlockSpec(memory_space=pltpu.SMEM)
VMEM = pl.BlockSpec(memory_space=pltpu.VMEM)
FREE = pl.CostEstimate(flops=0, bytes_accessed=0, transcendentals=0)
ROWS_BY_ROWS = (((0,), (0,)), ((), ()))
ROWS_BY_COLUMNS = (((1,), (0,)), ((), ()))
COLUMNS_BY_COLUMNS = (((1,), (1,)), ((), ()))


def params(mib=48):
    return pltpu.CompilerParams(vmem_limit_bytes=mib * MIB)


def split(value):
    high = value.astype(jnp.bfloat16)
    return high, (value - high.astype(jnp.float32)).astype(jnp.bfloat16)


def dot(left, right, dims=ROWS_BY_COLUMNS):
    return lax.dot_general(left, right, dims, preferred_element_type=jnp.float32)


def product(left, right, dims=ROWS_BY_COLUMNS):
    (left_high, left_low), (right_high, right_low) = left, right
    return dot(left_high, right_high, dims) + (
        dot(left_high, right_low, dims) + dot(left_low, right_high, dims)
    )


def project_kernel(depth, snapshots_ref, factor_ref, mine_ref, other_ref, *refs):
    *parts, snapshots_buf, factor_buf, sems = refs
    rows, points = snapshots_ref.shape
    half = rows // 2
    snapshots_copy = pltpu.make_async_copy(snapshots_ref, snapshots_buf, sems.at[points // depth])
    snapshots_copy.start()
    copies = []
    for i, start in enumerate(range(0, points, depth)):
        span = pl.ds(start, depth)
        copies.append(pltpu.make_async_copy(factor_ref.at[span, :], factor_buf.at[span, :], sems.at[i]))
        copies[-1].start()
    snapshots_copy.wait()
    width = parts[0].shape[1]
    member = lax.rem(lax.axis_index("tm"), len(parts))
    for k, part in enumerate(parts):
        part[...] = snapshots_buf[:, pl.ds(pl.multiple_of((member ^ k) * width, width), width)]
    value = None
    for i, start in enumerate(range(0, points, depth)):
        copies[i].wait()
        high, low = split(snapshots_buf[:, start : start + depth])
        factor_high, factor_low = split(factor_buf[start : start + depth, :])
        both = dot(jnp.concatenate([high, low], axis=0), factor_high)
        term = both[:rows] + (both[rows:] + dot(high, factor_low))
        value = term if value is None else value + term
    first = lax.rem(lax.axis_index("space"), 2) == 0
    mine_ref[...] = jnp.where(first, value[:half], value[half:])
    other_ref[...] = jnp.where(first, value[half:], value[:half])


def project(snapshots, space_factor, group):
    rows, points = snapshots.shape
    rank = space_factor.shape[1]
    depth = min(512, points)
    half = jax.ShapeDtypeStruct((rows // 2, rank), jnp.float32)
    part = jax.ShapeDtypeStruct((rows, points // group), jnp.float32)
    mine, other, *parts = pl.pallas_call(
        functools.partial(project_kernel, depth),
        in_specs=[HBM, HBM],
        out_specs=[VMEM] * (2 + group),
        out_shape=[half, half] + [part] * group,
        scratch_shapes=[
            pltpu.VMEM((rows, points), jnp.float32),
            pltpu.VMEM((points, rank), jnp.float32),
            pltpu.SemaphoreType.DMA((points // depth + 1,)),
        ],
        compiler_params=params(52),
        cost_estimate=FREE,
    )(snapshots, space_factor)
    return mine, other, parts


def mix_kernel(times, order, index_ref, mine_ref, theirs_ref, high_t_ref, low_t_ref, own_ref):
    total_half, rank = mine_ref.shape
    half = total_half // times
    mine = mine_ref[...].reshape(times, half, rank)
    theirs = theirs_ref[...].reshape(times, half, rank)
    first = index_ref[1] == 0
    low_rows, high_rows = jnp.where(first, mine, theirs), jnp.where(first, theirs, mine)
    projected = jnp.concatenate([low_rows, high_rows], axis=1).reshape(2 * total_half, rank)
    high, low = split(projected)
    cross = dot(high, low, ROWS_BY_ROWS)
    gram = dot(high, high, ROWS_BY_ROWS) + (cross + cross.T)
    row = lax.broadcasted_iota(jnp.int32, (rank, rank), 0)
    column = lax.broadcasted_iota(jnp.int32, (rank, rank), 1)
    total = jnp.sum(projected * projected)
    correlation = gram / total
    correlation_split = split(correlation)
    square = product(correlation_split, correlation_split)
    tail = jnp.where(row == column, 1.6875, 0.0) - 0.5625 * correlation + 0.0625 * square
    mixing = (jnp.where(row == column, 2.25, 0.0) - 2.4375 * correlation) + product(split(square), split(tail))
    mixing_high, mixing_low = split(mixing)

    rows = 2 * half
    group = high_t_ref.shape[1] // rows
    places = [order.index(k) for k in range(group)]
    high = jnp.concatenate([high[i * rows : (i + 1) * rows] for i in places], axis=0)
    low = jnp.concatenate([low[i * rows : (i + 1) * rows] for i in places], axis=0)
    scale = lax.rsqrt(total)
    own = product((high[:rows], low[:rows]), (mixing_high, mixing_low))
    own_ref[...] = own * (scale * math.sqrt(times * rows))
    width = rank // times
    source = ((row // width) ^ index_ref[0]) * width + row % width
    move = jnp.where(source == column, 1.0, 0.0).astype(jnp.bfloat16)
    moved = dot(move, jnp.concatenate([mixing_high, mixing_low], axis=1)).astype(jnp.bfloat16)
    turned = product((moved[:, :rank], moved[:, rank:]), (high, low), COLUMNS_BY_COLUMNS) * scale
    high_t_ref[...], low_t_ref[...] = split(turned)


def mix(index, mine, theirs, times, group, order):
    total_half, rank = mine.shape
    rows = 2 * total_half // times
    factor = jax.ShapeDtypeStruct((rank, group * rows), jnp.bfloat16)
    return pl.pallas_call(
        functools.partial(mix_kernel, times, order),
        in_specs=[SMEM, VMEM, VMEM],
        out_specs=[VMEM] * 3,
        out_shape=[factor, factor, jax.ShapeDtypeStruct((rows, rank), jnp.float32)],
        compiler_params=params(),
        cost_estimate=FREE,
    )(index, mine, theirs)


def load_kernel(group, high_ref, low_ref, *refs):
    parts, blocks = refs[:group], refs[group:]
    columns = jnp.concatenate([part[...] for part in parts], axis=0)
    value = product((high_ref[...], low_ref[...]), split(columns))
    width = value.shape[0] // len(blocks)
    for i, block in enumerate(blocks):
        block[...] = value[i * width : (i + 1) * width]


def load(high, low, parts, blocks):
    rank = high.shape[0]
    columns = parts[0].shape[1]
    return pl.pallas_call(
        functools.partial(load_kernel, len(parts)),
        in_specs=[VMEM] * (2 + len(parts)),
        out_specs=[VMEM] * blocks,
        out_shape=[jax.ShapeDtypeStruct((rank // blocks, columns), jnp.float32)] * blocks,
        compiler_params=params(),
        cost_estimate=FREE,
    )(high, low, *parts)


def join_kernel(group, *refs):
    *terms, out_ref = refs
    terms = terms[-group:] + terms[:-group]
    width = terms[0].shape[1]
    member = lax.rem(lax.axis_index("tm"), group)
    for k in range(group):
        value = terms[k][...]
        for term in terms[group + k :: group]:
            value = value + term[...]
        out_ref[:, pl.ds(pl.multiple_of((member ^ k) * width, width), width)] = value


def join(terms, group):
    rows, width = terms[0].shape
    return pl.pallas_call(
        functools.partial(join_kernel, group),
        in_specs=[VMEM] * len(terms),
        out_specs=VMEM,
        out_shape=jax.ShapeDtypeStruct((rows, group * width), jnp.float32),
        compiler_params=params(),
        cost_estimate=FREE,
    )(*terms[group:], *terms[:group])


def swap(value, axis, offset):
    return lax.ppermute(value, axis, [(i, i ^ offset) for i in range(lax.axis_size(axis))])


def on_device(snapshots, space_factor):
    rows, points = snapshots.shape
    rank = space_factor.shape[1]
    times, spaces = lax.axis_size("tm"), lax.axis_size("space")
    group = min(4, times)
    index = lax.axis_index("tm")
    core = lax.axis_index("space") % 2

    mine, other, parts = project(snapshots, space_factor, group)
    parts = [part if k == 0 else swap(part, "tm", k) for k, part in enumerate(parts)]

    mine = mine + swap(other, "space", 1)
    for i in range(1, spaces.bit_length() - 1):
        mine = mine + swap(mine, "space", 1 << i)

    order, offsets = [0], [1 << i for i in range(times.bit_length() - 1)]
    for offset in [o for o in offsets if o >= group] + [o for o in offsets if o < group]:
        if offset < group:
            mine, parts[offset] = lax.optimization_barrier((mine, parts[offset]))
        mine = jnp.concatenate([mine, swap(mine, "tm", offset)], axis=0)
        order = order + [k ^ offset for k in order]
    theirs, parts[-1] = lax.optimization_barrier((swap(mine, "space", 1), parts[-1]))
    high_t, low_t, own = mix(jnp.stack([index, core]), mine, theirs, times, group, order)

    blocks = list(load(high_t, low_t, parts, times))
    terms = [blocks[0]] + [None] * (times - 1)
    for k in [*range(group, times), *range(1, group)]:
        if 1 < k < group:
            blocks[k], terms[k - 1] = lax.optimization_barrier((blocks[k], terms[k - 1]))
        terms[k] = swap(blocks[k], "tm", k)
    return own, join(terms, group)


def solution(mesh):
    return jax.shard_map(
        on_device,
        mesh=mesh,
        in_specs=(P("tm", "space"), P("space", None)),
        out_specs=(P("tm", None), P("tm", "space")),
        check_vma=False,
    )
```

```python
import functools
import math

import jax
import jax.numpy as jnp
from jax import lax
from jax.experimental import pallas as pl
from jax.experimental.pallas import tpu as pltpu
from jax.sharding import PartitionSpec as P

MIB = 1024 * 1024
HBM = pl.BlockSpec(memory_space=pltpu.HBM)
SMEM = pl.BlockSpec(memory_space=pltpu.SMEM)
VMEM = pl.BlockSpec(memory_space=pltpu.VMEM)
FREE = pl.CostEstimate(flops=0, bytes_accessed=0, transcendentals=0)
ROWS_BY_ROWS = (((0,), (0,)), ((), ()))
ROWS_BY_COLUMNS = (((1,), (0,)), ((), ()))
COLUMNS_BY_COLUMNS = (((1,), (1,)), ((), ()))


def params(mib=48):
    return pltpu.CompilerParams(vmem_limit_bytes=mib * MIB)


def split(value):
    high = value.astype(jnp.bfloat16)
    return high, (value - high.astype(jnp.float32)).astype(jnp.bfloat16)


def dot(left, right, dims=ROWS_BY_COLUMNS):
    return lax.dot_general(left, right, dims, preferred_element_type=jnp.float32)


def product(left, right, dims=ROWS_BY_COLUMNS):
    (left_high, left_low), (right_high, right_low) = left, right
    return dot(left_high, right_high, dims) + (
        dot(left_high, right_low, dims) + dot(left_low, right_high, dims)
    )


def project_kernel(depth, snapshots_ref, factor_ref, mine_ref, other_ref, *refs):
    *parts, snapshots_buf, factor_buf, sems = refs
    rows, points = snapshots_ref.shape
    half = rows // 2
    snapshots_copy = pltpu.make_async_copy(snapshots_ref, snapshots_buf, sems.at[points // depth])
    snapshots_copy.start()
    copies = []
    for i, start in enumerate(range(0, points, depth)):
        span = pl.ds(start, depth)
        copies.append(pltpu.make_async_copy(factor_ref.at[span, :], factor_buf.at[span, :], sems.at[i]))
        copies[-1].start()
    snapshots_copy.wait()
    width = parts[0].shape[1]
    member = lax.rem(lax.axis_index("tm"), len(parts))
    for k, part in enumerate(parts):
        part[...] = snapshots_buf[:, pl.ds(pl.multiple_of((member ^ k) * width, width), width)]
    value = None
    for i, start in enumerate(range(0, points, depth)):
        copies[i].wait()
        high, low = split(snapshots_buf[:, start : start + depth])
        factor_high, factor_low = split(factor_buf[start : start + depth, :])
        both = dot(jnp.concatenate([high, low], axis=0), factor_high)
        term = both[:rows] + (both[rows:] + dot(high, factor_low))
        value = term if value is None else value + term
    first = lax.rem(lax.axis_index("space"), 2) == 0
    mine_ref[...] = jnp.where(first, value[:half], value[half:])
    other_ref[...] = jnp.where(first, value[half:], value[:half])


def project(snapshots, space_factor, group):
    rows, points = snapshots.shape
    rank = space_factor.shape[1]
    depth = min(512, points)
    half = jax.ShapeDtypeStruct((rows // 2, rank), jnp.float32)
    part = jax.ShapeDtypeStruct((rows, points // group), jnp.float32)
    mine, other, *parts = pl.pallas_call(
        functools.partial(project_kernel, depth),
        in_specs=[HBM, HBM],
        out_specs=[VMEM] * (2 + group),
        out_shape=[half, half] + [part] * group,
        scratch_shapes=[
            pltpu.VMEM((rows, points), jnp.float32),
            pltpu.VMEM((points, rank), jnp.float32),
            pltpu.SemaphoreType.DMA((points // depth + 1,)),
        ],
        compiler_params=params(52),
        cost_estimate=FREE,
    )(snapshots, space_factor)
    return mine, other, parts


def mix_kernel(index_ref, mine_ref, theirs_ref, high_t_ref, low_t_ref, own_ref):
    times, half, rank = mine_ref.shape
    total_half = times * half
    mine = jnp.stack([mine_ref[index_ref[0] ^ k] for k in range(times)])
    theirs = jnp.stack([theirs_ref[index_ref[0] ^ k] for k in range(times)])
    first = index_ref[1] == 0
    low_rows, high_rows = jnp.where(first, mine, theirs), jnp.where(first, theirs, mine)
    projected = jnp.concatenate([low_rows, high_rows], axis=1).reshape(2 * total_half, rank)
    high, low = split(projected)
    cross = dot(high, low, ROWS_BY_ROWS)
    gram = dot(high, high, ROWS_BY_ROWS) + (cross + cross.T)
    row = lax.broadcasted_iota(jnp.int32, (rank, rank), 0)
    column = lax.broadcasted_iota(jnp.int32, (rank, rank), 1)
    total = jnp.sum(projected * projected)
    correlation = gram / total
    correlation_split = split(correlation)
    square = product(correlation_split, correlation_split)
    tail = jnp.where(row == column, 1.6875, 0.0) - 0.5625 * correlation + 0.0625 * square
    mixing = (jnp.where(row == column, 2.25, 0.0) - 2.4375 * correlation) + product(split(square), split(tail))
    mixing_high, mixing_low = split(mixing)

    rows = 2 * half
    high, low = high[: high_t_ref.shape[1]], low[: high_t_ref.shape[1]]
    scale = lax.rsqrt(total)
    own = product((high[:rows], low[:rows]), (mixing_high, mixing_low))
    own_ref[...] = own * (scale * math.sqrt(times * rows))
    width = rank // times
    source = ((row // width) ^ index_ref[0]) * width + row % width
    move = jnp.where(source == column, 1.0, 0.0).astype(jnp.bfloat16)
    moved = dot(move, jnp.concatenate([mixing_high, mixing_low], axis=1)).astype(jnp.bfloat16)
    turned = product((moved[:, :rank], moved[:, rank:]), (high, low), COLUMNS_BY_COLUMNS) * scale
    high_t_ref[...], low_t_ref[...] = split(turned)


def mix(index, mine, theirs, group):
    times, half, rank = mine.shape
    rows = 2 * half
    factor = jax.ShapeDtypeStruct((rank, group * rows), jnp.bfloat16)
    return pl.pallas_call(
        mix_kernel,
        in_specs=[SMEM, VMEM, VMEM],
        out_specs=[VMEM] * 3,
        out_shape=[factor, factor, jax.ShapeDtypeStruct((rows, rank), jnp.float32)],
        compiler_params=params(),
        cost_estimate=FREE,
    )(index, mine, theirs)


def load_kernel(group, high_ref, low_ref, *refs):
    parts, blocks = refs[:group], refs[group:]
    columns = jnp.concatenate([part[...] for part in parts], axis=0)
    value = product((high_ref[...], low_ref[...]), split(columns))
    width = value.shape[0] // len(blocks)
    for i, block in enumerate(blocks):
        block[...] = value[i * width : (i + 1) * width]


def load(high, low, parts, blocks):
    rank = high.shape[0]
    columns = parts[0].shape[1]
    return pl.pallas_call(
        functools.partial(load_kernel, len(parts)),
        in_specs=[VMEM] * (2 + len(parts)),
        out_specs=[VMEM] * blocks,
        out_shape=[jax.ShapeDtypeStruct((rank // blocks, columns), jnp.float32)] * blocks,
        compiler_params=params(),
        cost_estimate=FREE,
    )(high, low, *parts)


def join_kernel(group, *refs):
    *terms, out_ref = refs
    width = terms[0].shape[1]
    member = lax.rem(lax.axis_index("tm"), group)
    for k in range(group):
        value = terms[k][...]
        for term in terms[group + k :: group]:
            value = value + term[...]
        out_ref[:, pl.ds(pl.multiple_of((member ^ k) * width, width), width)] = value


def join(terms, group):
    rows, width = terms[0].shape
    return pl.pallas_call(
        functools.partial(join_kernel, group),
        in_specs=[VMEM] * len(terms),
        out_specs=VMEM,
        out_shape=jax.ShapeDtypeStruct((rows, group * width), jnp.float32),
        compiler_params=params(),
        cost_estimate=FREE,
    )(*terms)


def swap(value, axis, offset):
    return lax.ppermute(value, axis, [(i, i ^ offset) for i in range(lax.axis_size(axis))])


def on_device(snapshots, space_factor):
    rows, points = snapshots.shape
    rank = space_factor.shape[1]
    times, spaces = lax.axis_size("tm"), lax.axis_size("space")
    group = min(4, times)
    index = lax.axis_index("tm")
    core = lax.axis_index("space") % 2

    mine, other, parts = project(snapshots, space_factor, group)
    parts = [part if k == 0 else swap(part, "tm", k) for k, part in enumerate(parts)]

    mine = mine + swap(other, "space", 1)
    for i in range(1, spaces.bit_length() - 1):
        mine = mine + swap(mine, "space", 1 << i)

    mine, *parts[1:-1] = lax.optimization_barrier((mine, *parts[1:-1]))
    mine = lax.all_to_all(jnp.broadcast_to(mine, (times, *mine.shape)), "tm", 0, 0, tiled=True)
    theirs, parts[-1] = lax.optimization_barrier((swap(mine, "space", 1), parts[-1]))
    high_t, low_t, own = mix(jnp.stack([index, core]), mine, theirs, group)

    blocks = list(load(high_t, low_t, parts, times))
    terms = [blocks[0]] + [None] * (times - 1)
    for k in [*range(group, times), *range(1, group)]:
        if k == group - 1:
            blocks[k], terms[1] = lax.optimization_barrier((blocks[k], terms[1]))
        terms[k] = swap(blocks[k], "tm", k)
    return own, join(terms, group)


def solution(mesh):
    return jax.shard_map(
        on_device,
        mesh=mesh,
        in_specs=(P("tm", "space"), P("space", None)),
        out_specs=(P("tm", None), P("tm", "space")),
        check_vma=False,
    )
```

```python
import functools
import math

import jax
import jax.numpy as jnp
from jax import lax
from jax.experimental import pallas as pl
from jax.experimental.pallas import tpu as pltpu
from jax.sharding import PartitionSpec as P

MIB = 1024 * 1024
HBM = pl.BlockSpec(memory_space=pltpu.HBM)
SMEM = pl.BlockSpec(memory_space=pltpu.SMEM)
VMEM = pl.BlockSpec(memory_space=pltpu.VMEM)
FREE = pl.CostEstimate(flops=0, bytes_accessed=0, transcendentals=0)
ROWS_BY_ROWS = (((0,), (0,)), ((), ()))
ROWS_BY_COLUMNS = (((1,), (0,)), ((), ()))
COLUMNS_BY_COLUMNS = (((1,), (1,)), ((), ()))


def params(mib=48):
    return pltpu.CompilerParams(vmem_limit_bytes=mib * MIB)


def split(value):
    high = value.astype(jnp.bfloat16)
    return high, (value - high.astype(jnp.float32)).astype(jnp.bfloat16)


def dot(left, right, dims=ROWS_BY_COLUMNS):
    return lax.dot_general(left, right, dims, preferred_element_type=jnp.float32)


def product(left, right, dims=ROWS_BY_COLUMNS):
    (left_high, left_low), (right_high, right_low) = left, right
    return dot(left_high, right_high, dims) + (
        dot(left_high, right_low, dims) + dot(left_low, right_high, dims)
    )


def project_kernel(depth, snapshots_ref, factor_ref, mine_ref, other_ref, *refs):
    *parts, snapshots_buf, factor_buf, sems = refs
    rows, points = snapshots_ref.shape
    half = rows // 2
    snapshots_copy = pltpu.make_async_copy(snapshots_ref, snapshots_buf, sems.at[points // depth])
    snapshots_copy.start()
    copies = []
    for i, start in enumerate(range(0, points, depth)):
        span = pl.ds(start, depth)
        copies.append(pltpu.make_async_copy(factor_ref.at[span, :], factor_buf.at[span, :], sems.at[i]))
        copies[-1].start()
    snapshots_copy.wait()
    width = parts[0].shape[1]
    member = lax.rem(lax.axis_index("tm"), len(parts))
    for k, part in enumerate(parts):
        part[...] = snapshots_buf[:, pl.ds(pl.multiple_of((member ^ k) * width, width), width)]
    value = None
    for i, start in enumerate(range(0, points, depth)):
        copies[i].wait()
        high, low = split(snapshots_buf[:, start : start + depth])
        factor_high, factor_low = split(factor_buf[start : start + depth, :])
        both = dot(jnp.concatenate([high, low], axis=0), factor_high)
        term = both[:rows] + (both[rows:] + dot(high, factor_low))
        value = term if value is None else value + term
    first = lax.rem(lax.axis_index("space"), 2) == 0
    mine_ref[...] = jnp.where(first, value[:half], value[half:])
    other_ref[...] = jnp.where(first, value[half:], value[:half])


def project(snapshots, space_factor, group):
    rows, points = snapshots.shape
    rank = space_factor.shape[1]
    depth = min(512, points)
    half = jax.ShapeDtypeStruct((rows // 2, rank), jnp.float32)
    part = jax.ShapeDtypeStruct((rows, points // group), jnp.float32)
    mine, other, *parts = pl.pallas_call(
        functools.partial(project_kernel, depth),
        in_specs=[HBM, HBM],
        out_specs=[VMEM] * (2 + group),
        out_shape=[half, half] + [part] * group,
        scratch_shapes=[
            pltpu.VMEM((rows, points), jnp.float32),
            pltpu.VMEM((points, rank), jnp.float32),
            pltpu.SemaphoreType.DMA((points // depth + 1,)),
        ],
        compiler_params=params(52),
        cost_estimate=FREE,
    )(snapshots, space_factor)
    return mine, other, parts


def mix_kernel(times, order, index_ref, mine_ref, theirs_ref, high_t_ref, low_t_ref, own_ref):
    total_half, rank = mine_ref.shape
    half = total_half // times
    mine = mine_ref[...].reshape(times, half, rank)
    theirs = theirs_ref[...].reshape(times, half, rank)
    first = index_ref[1] == 0
    low_rows, high_rows = jnp.where(first, mine, theirs), jnp.where(first, theirs, mine)
    projected = jnp.concatenate([low_rows, high_rows], axis=1).reshape(2 * total_half, rank)
    high, low = split(projected)
    cross = dot(high, low, ROWS_BY_ROWS)
    gram = dot(high, high, ROWS_BY_ROWS) + (cross + cross.T)
    row = lax.broadcasted_iota(jnp.int32, (rank, rank), 0)
    column = lax.broadcasted_iota(jnp.int32, (rank, rank), 1)
    total = jnp.sum(projected * projected)
    correlation = gram / total
    correlation_split = split(correlation)
    square = product(correlation_split, correlation_split)
    tail = jnp.where(row == column, 1.6875, 0.0) - 0.5625 * correlation + 0.0625 * square
    mixing = (jnp.where(row == column, 2.25, 0.0) - 2.4375 * correlation) + product(split(square), split(tail))
    mixing_high, mixing_low = split(mixing)

    rows = 2 * half
    group = high_t_ref.shape[1] // rows
    places = [order.index(k) for k in range(group)]
    high = jnp.concatenate([high[i * rows : (i + 1) * rows] for i in places], axis=0)
    low = jnp.concatenate([low[i * rows : (i + 1) * rows] for i in places], axis=0)
    scale = lax.rsqrt(total)
    own = product((high[:rows], low[:rows]), (mixing_high, mixing_low))
    own_ref[...] = own * (scale * math.sqrt(times * rows))
    width = rank // times
    source = ((row // width) ^ index_ref[0]) * width + row % width
    move = jnp.where(source == column, 1.0, 0.0).astype(jnp.bfloat16)
    moved = dot(move, jnp.concatenate([mixing_high, mixing_low], axis=1)).astype(jnp.bfloat16)
    turned = product((moved[:, :rank], moved[:, rank:]), (high, low), COLUMNS_BY_COLUMNS) * scale
    high_t_ref[...], low_t_ref[...] = split(turned)


def mix(index, mine, theirs, times, group, order):
    total_half, rank = mine.shape
    rows = 2 * total_half // times
    factor = jax.ShapeDtypeStruct((rank, group * rows), jnp.bfloat16)
    return pl.pallas_call(
        functools.partial(mix_kernel, times, order),
        in_specs=[SMEM, VMEM, VMEM],
        out_specs=[VMEM] * 3,
        out_shape=[factor, factor, jax.ShapeDtypeStruct((rows, rank), jnp.float32)],
        compiler_params=params(),
        cost_estimate=FREE,
    )(index, mine, theirs)


def load_kernel(group, high_ref, low_ref, *refs):
    parts, blocks = refs[:group], refs[group:]
    columns = jnp.concatenate([part[...] for part in parts], axis=0)
    value = product((high_ref[...], low_ref[...]), split(columns))
    width = value.shape[0] // len(blocks)
    for i, block in enumerate(blocks):
        block[...] = value[i * width : (i + 1) * width]


def load(high, low, parts, blocks):
    rank = high.shape[0]
    columns = parts[0].shape[1]
    return pl.pallas_call(
        functools.partial(load_kernel, len(parts)),
        in_specs=[VMEM] * (2 + len(parts)),
        out_specs=[VMEM] * blocks,
        out_shape=[jax.ShapeDtypeStruct((rank // blocks, columns), jnp.float32)] * blocks,
        compiler_params=params(),
        cost_estimate=FREE,
    )(high, low, *parts)


def join_kernel(group, *refs):
    *terms, out_ref, buf, sems = refs
    width = terms[0].shape[1]
    member = lax.rem(lax.axis_index("tm"), group)
    copies = []
    for k in range(group):
        value = terms[k][...]
        for term in terms[group + k :: group]:
            value = value + term[...]
        buf[k] = value
        span = pl.ds(pl.multiple_of((member ^ k) * width, width), width)
        copies.append(pltpu.make_async_copy(buf.at[k], out_ref.at[:, span], sems.at[k]))
        copies[-1].start()
    for copy in copies:
        copy.wait()


def join(terms, group):
    rows, width = terms[0].shape
    return pl.pallas_call(
        functools.partial(join_kernel, group),
        in_specs=[VMEM] * len(terms),
        out_specs=HBM,
        out_shape=jax.ShapeDtypeStruct((rows, group * width), jnp.float32),
        scratch_shapes=[pltpu.VMEM((group, rows, width), jnp.float32), pltpu.SemaphoreType.DMA((group,))],
        compiler_params=params(),
        cost_estimate=FREE,
    )(*terms)


def swap(value, axis, offset):
    return lax.ppermute(value, axis, [(i, i ^ offset) for i in range(lax.axis_size(axis))])


def on_device(snapshots, space_factor):
    rows, points = snapshots.shape
    rank = space_factor.shape[1]
    times, spaces = lax.axis_size("tm"), lax.axis_size("space")
    group = min(4, times)
    index = lax.axis_index("tm")
    core = lax.axis_index("space") % 2

    mine, other, parts = project(snapshots, space_factor, group)
    parts = [part if k == 0 else swap(part, "tm", k) for k, part in enumerate(parts)]

    mine = mine + swap(other, "space", 1)
    for i in range(1, spaces.bit_length() - 1):
        mine = mine + swap(mine, "space", 1 << i)

    pair = jnp.concatenate([mine, swap(mine, "tm", 1)], axis=0)
    pair, *parts = lax.optimization_barrier((pair, *parts))
    offsets = [*range(group, times, 2), *range(2, group, 2)]
    mine = jnp.concatenate([pair] + [swap(pair, "tm", k) for k in offsets], axis=0)
    order = [k ^ i for k in [0, *offsets] for i in range(2)]
    high_t, low_t, own = mix(jnp.stack([index, core]), mine, swap(mine, "space", 1), times, group, order)

    blocks = list(load(high_t, low_t, parts, times))
    terms = [blocks[0]] + [None] * (times - 1)
    for k in [*range(group, times), *range(1, group)]:
        if k == group - 1:
            blocks[k], terms[1] = lax.optimization_barrier((blocks[k], terms[1]))
        terms[k] = swap(blocks[k], "tm", k)
    return own, join(terms, group)


def solution(mesh):
    return jax.shard_map(
        on_device,
        mesh=mesh,
        in_specs=(P("tm", "space"), P("space", None)),
        out_specs=(P("tm", None), P("tm", "space")),
        check_vma=False,
    )
```

```python
import functools
import math

import jax
import jax.numpy as jnp
from jax import lax
from jax.experimental import pallas as pl
from jax.experimental.pallas import tpu as pltpu
from jax.sharding import PartitionSpec as P

MIB = 1024 * 1024
WHOLE_SHARE = 0.75
HBM = pl.BlockSpec(memory_space=pltpu.HBM)
SMEM = pl.BlockSpec(memory_space=pltpu.SMEM)
VMEM = pl.BlockSpec(memory_space=pltpu.VMEM)
FREE = pl.CostEstimate(flops=0, bytes_accessed=0, transcendentals=0)
ROWS_BY_ROWS = (((0,), (0,)), ((), ()))
ROWS_BY_COLUMNS = (((1,), (0,)), ((), ()))
COLUMNS_BY_COLUMNS = (((1,), (1,)), ((), ()))


def params(mib=48):
    return pltpu.CompilerParams(vmem_limit_bytes=mib * MIB)


def split(value):
    high = value.astype(jnp.bfloat16)
    return high, (value - high.astype(jnp.float32)).astype(jnp.bfloat16)


def dot(left, right, dims=ROWS_BY_COLUMNS):
    return lax.dot_general(left, right, dims, preferred_element_type=jnp.float32)


def product(left, right, dims=ROWS_BY_COLUMNS):
    (left_high, left_low), (right_high, right_low) = left, right
    return dot(left_high, right_high, dims) + (
        dot(left_high, right_low, dims) + dot(left_low, right_high, dims)
    )


def project_kernel(depth, group, wide, snapshots_ref, factor_ref, halves_ref, *refs):
    *pieces, snapshots_buf, factor_buf, sems = refs
    rows, points = snapshots_ref.shape
    half = rows // 2
    snapshots_copy = pltpu.make_async_copy(snapshots_ref, snapshots_buf, sems.at[points // depth])
    snapshots_copy.start()
    copies = []
    for i, start in enumerate(range(0, points, depth)):
        span = pl.ds(start, depth)
        copies.append(pltpu.make_async_copy(factor_ref.at[span, :], factor_buf.at[span, :], sems.at[i]))
        copies[-1].start()
    snapshots_copy.wait()
    share = points // group
    parts, slabs = (pieces[:-1], pieces[-1]) if wide else (pieces, None)
    member = lax.rem(lax.axis_index("tm"), group)
    for k, part in enumerate(parts):
        start = pl.multiple_of((member ^ k) * share, share)
        part[...] = snapshots_buf[:, pl.ds(start, part.shape[1])]
    if wide:
        times = slabs.shape[0]
        for i in range(times):
            end = (i % group + 1) * share - (times - 1 - i) // group * wide
            slabs[i] = snapshots_buf[:, end - wide : end]
    value = None
    for i, start in enumerate(range(0, points, depth)):
        copies[i].wait()
        high, low = split(snapshots_buf[:, start : start + depth])
        factor_high, factor_low = split(factor_buf[start : start + depth, :])
        both = dot(jnp.concatenate([high, low], axis=0), factor_high)
        term = both[:rows] + (both[rows:] + dot(high, factor_low))
        value = term if value is None else value + term
    first = lax.rem(lax.axis_index("space"), 2) == 0
    halves_ref[0] = jnp.where(first, value[:half], value[half:])
    halves_ref[1] = jnp.where(first, value[half:], value[:half])


def project(snapshots, space_factor, group, groups, wide):
    rows, points = snapshots.shape
    rank = space_factor.shape[1]
    depth = min(512, points)
    narrow = points // group - groups * wide
    pieces = [jax.ShapeDtypeStruct((rows, narrow), jnp.float32)] * (group if narrow else 0)
    if wide:
        pieces = [*pieces, jax.ShapeDtypeStruct((group * groups, rows, wide), jnp.float32)]
    halves, *pieces = pl.pallas_call(
        functools.partial(project_kernel, depth, group, wide),
        in_specs=[HBM, HBM],
        out_specs=[VMEM] * (1 + len(pieces)),
        out_shape=[jax.ShapeDtypeStruct((2, rows // 2, rank), jnp.float32), *pieces],
        scratch_shapes=[
            pltpu.VMEM((rows, points), jnp.float32),
            pltpu.VMEM((points, rank), jnp.float32),
            pltpu.SemaphoreType.DMA((points // depth + 1,)),
        ],
        compiler_params=params(52),
        cost_estimate=FREE,
    )(snapshots, space_factor)
    return (halves, pieces[:-1], pieces[-1:]) if wide else (halves, pieces, [])


def mix_kernel(times, order, index_ref, mine_ref, theirs_ref, high_t_ref, low_t_ref, own_ref):
    total_half, rank = mine_ref.shape
    half = total_half // times
    mine = mine_ref[...].reshape(times, half, rank)
    theirs = theirs_ref[...].reshape(times, half, rank)
    first = index_ref[1] == 0
    low_rows, high_rows = jnp.where(first, mine, theirs), jnp.where(first, theirs, mine)
    projected = jnp.concatenate([low_rows, high_rows], axis=1).reshape(2 * total_half, rank)
    high, low = split(projected)
    cross = dot(high, low, ROWS_BY_ROWS)
    gram = dot(high, high, ROWS_BY_ROWS) + (cross + cross.T)
    row = lax.broadcasted_iota(jnp.int32, (rank, rank), 0)
    column = lax.broadcasted_iota(jnp.int32, (rank, rank), 1)
    total = jnp.sum(projected * projected)
    correlation = gram / total
    correlation_split = split(correlation)
    square = product(correlation_split, correlation_split)
    tail = jnp.where(row == column, 1.6875, 0.0) - 0.5625 * correlation + 0.0625 * square
    mixing = (jnp.where(row == column, 2.25, 0.0) - 2.4375 * correlation) + product(split(square), split(tail))
    mixing_high, mixing_low = split(mixing)

    rows = 2 * half
    places = [order.index(k) for k in range(times)]
    high = jnp.concatenate([high[i * rows : (i + 1) * rows] for i in places], axis=0)
    low = jnp.concatenate([low[i * rows : (i + 1) * rows] for i in places], axis=0)
    scale = lax.rsqrt(total)
    own = product((high[:rows], low[:rows]), (mixing_high, mixing_low))
    own_ref[...] = own * (scale * math.sqrt(times * rows))
    width = rank // times
    source = ((row // width) ^ index_ref[0]) * width + row % width
    move = jnp.where(source == column, 1.0, 0.0).astype(jnp.bfloat16)
    moved = dot(move, jnp.concatenate([mixing_high, mixing_low], axis=1)).astype(jnp.bfloat16)
    turned = product((moved[:, :rank], moved[:, rank:]), (high, low), COLUMNS_BY_COLUMNS) * scale
    high_t_ref[...], low_t_ref[...] = split(turned)


def mix(index, mine, theirs, times, order):
    total_half, rank = mine.shape
    rows = 2 * total_half // times
    factor = jax.ShapeDtypeStruct((rank, times * rows), jnp.bfloat16)
    return pl.pallas_call(
        functools.partial(mix_kernel, times, order),
        in_specs=[SMEM, VMEM, VMEM],
        out_specs=[VMEM] * 3,
        out_shape=[factor, factor, jax.ShapeDtypeStruct((rows, rank), jnp.float32)],
        compiler_params=params(),
        cost_estimate=FREE,
    )(index, mine, theirs)


def load_kernel(group, wide, index_ref, high_ref, low_ref, *refs):
    parts, slabs, blocks = refs[:group], refs[group : group + wide], refs[group + wide :]
    high, low = high_ref[...], low_ref[...]
    values = []
    if parts:
        columns = jnp.concatenate([part[...] for part in parts], axis=0)
        depth = columns.shape[0]
        values.append(product((high[:, :depth], low[:, :depth]), split(columns)))
    for slab in slabs:
        columns = jnp.concatenate([slab[index_ref[0] ^ k] for k in range(len(blocks))], axis=0)
        values.append(product((high, low), split(columns)))
    rows = high.shape[0] // len(blocks)
    for i, block in enumerate(blocks):
        block[...] = jnp.concatenate([value[i * rows : (i + 1) * rows] for value in values], axis=1)


def load(index, high, low, parts, slabs, blocks):
    rank = high.shape[0]
    columns = sum(piece.shape[-1] for piece in [*parts[:1], *slabs])
    return pl.pallas_call(
        functools.partial(load_kernel, len(parts), len(slabs)),
        in_specs=[SMEM] + [VMEM] * (2 + len(parts) + len(slabs)),
        out_specs=[VMEM] * blocks,
        out_shape=[jax.ShapeDtypeStruct((rank // blocks, columns), jnp.float32)] * blocks,
        compiler_params=params(),
        cost_estimate=FREE,
    )(index, high, low, *parts, *slabs)


def join_kernel(group, wide, *refs):
    *terms, out_ref, buf, sems = refs
    groups = len(terms) // group
    rows, share = buf.shape[1:]
    narrow = share - groups * wide
    index = lax.axis_index("tm")
    member, place = lax.rem(index, group), lax.div(index, group)
    copies = []
    for k in range(group):
        members = terms[k::group]
        if narrow:
            value = members[0][:, :narrow]
            for term in members[1:]:
                value = value + term[:, :narrow]
            buf[k, :, :narrow] = value
        if wide:
            for g, term in enumerate(members):
                buf[k, :, pl.ds(pl.multiple_of(narrow + (place ^ g) * wide, 128), wide)] = term[:, narrow:]
        span = pl.ds(pl.multiple_of((member ^ k) * share, share), share)
        copies.append(pltpu.make_async_copy(buf.at[k], out_ref.at[:, span], sems.at[k]))
        copies[-1].start()
    for copy in copies:
        copy.wait()


def join(terms, group, wide, points):
    rows = terms[0].shape[0]
    return pl.pallas_call(
        functools.partial(join_kernel, group, wide),
        in_specs=[VMEM] * len(terms),
        out_specs=HBM,
        out_shape=jax.ShapeDtypeStruct((rows, points), jnp.float32),
        scratch_shapes=[pltpu.VMEM((group, rows, points // group), jnp.float32), pltpu.SemaphoreType.DMA((group,))],
        compiler_params=params(),
        cost_estimate=FREE,
    )(*terms)


def swap(value, axis, offset):
    return lax.ppermute(value, axis, [(i, i ^ offset) for i in range(lax.axis_size(axis))])


def on_device(snapshots, space_factor):
    rows, points = snapshots.shape
    times, spaces = lax.axis_size("tm"), lax.axis_size("space")
    group = min(4, times)
    groups = times // group
    index = lax.axis_index("tm")
    core = lax.axis_index("space") % 2
    wide = int(points // group * WHOLE_SHARE) // groups // 128 * 128

    halves, parts, slabs = project(snapshots, space_factor, group, groups, wide)
    order = [0]
    for i in range(groups.bit_length() - 1):
        halves = jnp.concatenate([halves, swap(halves, "tm", group << i)], axis=1)
        order = order + [k ^ group << i for k in order]
    if wide:
        halves, slabs = lax.optimization_barrier((halves, slabs))
        slabs = [lax.all_to_all(slab, "tm", 0, 0, tiled=True) for slab in slabs]
    parts = [part if k == 0 else swap(part, "tm", k) for k, part in enumerate(parts)]

    mine = halves[0] + swap(halves[1], "space", 1)
    for i in range(1, spaces.bit_length() - 1):
        mine = mine + swap(mine, "space", 1 << i)

    for i in range(group.bit_length() - 1):
        mine = jnp.concatenate([mine, swap(mine, "tm", 1 << i)], axis=0)
        order = order + [k ^ 1 << i for k in order]
        if parts:
            mine, parts[1 << i] = lax.optimization_barrier((mine, parts[1 << i]))
    theirs = swap(mine, "space", 1)
    if parts:
        theirs, parts[-1] = lax.optimization_barrier((theirs, parts[-1]))
    high_t, low_t, own = mix(jnp.stack([index, core]), mine, theirs, times, order)

    blocks = list(load(index.reshape(1), high_t, low_t, parts, slabs, times))
    terms = [blocks[0]] + [None] * (times - 1)
    for k in [*range(group, times), *range(1, group)]:
        if k == group - 1:
            blocks[k], terms[1] = lax.optimization_barrier((blocks[k], terms[1]))
        terms[k] = swap(blocks[k], "tm", k)
    return own, join(terms, group, wide, points)


def solution(mesh):
    return jax.shard_map(
        on_device,
        mesh=mesh,
        in_specs=(P("tm", "space"), P("space", None)),
        out_specs=(P("tm", None), P("tm", "space")),
        check_vma=False,
    )
```

```python
import functools
import math

import jax
import jax.numpy as jnp
from jax import lax
from jax.experimental import pallas as pl
from jax.experimental.pallas import tpu as pltpu
from jax.sharding import PartitionSpec as P

MIB = 1024 * 1024
HBM = pl.BlockSpec(memory_space=pltpu.HBM)
SMEM = pl.BlockSpec(memory_space=pltpu.SMEM)
VMEM = pl.BlockSpec(memory_space=pltpu.VMEM)
FREE = pl.CostEstimate(flops=0, bytes_accessed=0, transcendentals=0)
ROWS_BY_ROWS = (((0,), (0,)), ((), ()))
ROWS_BY_COLUMNS = (((1,), (0,)), ((), ()))
COLUMNS_BY_COLUMNS = (((1,), (1,)), ((), ()))


def params(mib=48):
    return pltpu.CompilerParams(vmem_limit_bytes=mib * MIB)


def split(value):
    high = value.astype(jnp.bfloat16)
    return high, (value - high.astype(jnp.float32)).astype(jnp.bfloat16)


def dot(left, right, dims=ROWS_BY_COLUMNS):
    return lax.dot_general(left, right, dims, preferred_element_type=jnp.float32)


def product(left, right, dims=ROWS_BY_COLUMNS):
    (left_high, left_low), (right_high, right_low) = left, right
    return dot(left_high, right_high, dims) + (
        dot(left_high, right_low, dims) + dot(left_low, right_high, dims)
    )


def project_kernel(depth, snapshots_ref, factor_ref, mine_ref, other_ref, *refs):
    *parts, snapshots_buf, factor_buf, sems = refs
    rows, points = snapshots_ref.shape
    half = rows // 2
    snapshots_copy = pltpu.make_async_copy(snapshots_ref, snapshots_buf, sems.at[points // depth])
    snapshots_copy.start()
    copies = []
    for i, start in enumerate(range(0, points, depth)):
        span = pl.ds(start, depth)
        copies.append(pltpu.make_async_copy(factor_ref.at[span, :], factor_buf.at[span, :], sems.at[i]))
        copies[-1].start()
    snapshots_copy.wait()
    width = parts[0].shape[1]
    member = lax.rem(lax.axis_index("tm"), len(parts))
    for k, part in enumerate(parts):
        part[...] = snapshots_buf[:, pl.ds(pl.multiple_of((member ^ k) * width, width), width)]
    value = None
    for i, start in enumerate(range(0, points, depth)):
        copies[i].wait()
        high, low = split(snapshots_buf[:, start : start + depth])
        factor_high, factor_low = split(factor_buf[start : start + depth, :])
        both = dot(jnp.concatenate([high, low], axis=0), factor_high)
        term = both[:rows] + (both[rows:] + dot(high, factor_low))
        value = term if value is None else value + term
    first = lax.rem(lax.axis_index("space"), 2) == 0
    mine_ref[...] = jnp.where(first, value[:half], value[half:])
    other_ref[...] = jnp.where(first, value[half:], value[:half])


def project(snapshots, space_factor, group):
    rows, points = snapshots.shape
    rank = space_factor.shape[1]
    depth = min(512, points)
    half = jax.ShapeDtypeStruct((rows // 2, rank), jnp.float32)
    part = jax.ShapeDtypeStruct((rows, points // group), jnp.float32)
    mine, other, *parts = pl.pallas_call(
        functools.partial(project_kernel, depth),
        in_specs=[HBM, HBM],
        out_specs=[VMEM] * (2 + group),
        out_shape=[half, half] + [part] * group,
        scratch_shapes=[
            pltpu.VMEM((rows, points), jnp.float32),
            pltpu.VMEM((points, rank), jnp.float32),
            pltpu.SemaphoreType.DMA((points // depth + 1,)),
        ],
        compiler_params=params(52),
        cost_estimate=FREE,
    )(snapshots, space_factor)
    return mine, other, parts


def mix_kernel(times, order, index_ref, mine_ref, theirs_ref, high_t_ref, low_t_ref, own_ref):
    total_half, rank = mine_ref.shape
    half = total_half // times
    mine = mine_ref[...].reshape(times, half, rank)
    theirs = theirs_ref[...].reshape(times, half, rank)
    first = index_ref[1] == 0
    low_rows, high_rows = jnp.where(first, mine, theirs), jnp.where(first, theirs, mine)
    projected = jnp.concatenate([low_rows, high_rows], axis=1).reshape(2 * total_half, rank)
    high, low = split(projected)
    cross = dot(high, low, ROWS_BY_ROWS)
    gram = dot(high, high, ROWS_BY_ROWS) + (cross + cross.T)
    row = lax.broadcasted_iota(jnp.int32, (rank, rank), 0)
    column = lax.broadcasted_iota(jnp.int32, (rank, rank), 1)
    total = jnp.sum(projected * projected)
    correlation = gram / total
    correlation_split = split(correlation)
    square = product(correlation_split, correlation_split)
    tail = jnp.where(row == column, 1.6875, 0.0) - 0.5625 * correlation + 0.0625 * square
    mixing = (jnp.where(row == column, 2.25, 0.0) - 2.4375 * correlation) + product(split(square), split(tail))
    mixing_high, mixing_low = split(mixing)

    rows = 2 * half
    group = high_t_ref.shape[1] // rows
    places = [order.index(k) for k in range(group)]
    high = jnp.concatenate([high[i * rows : (i + 1) * rows] for i in places], axis=0)
    low = jnp.concatenate([low[i * rows : (i + 1) * rows] for i in places], axis=0)
    scale = lax.rsqrt(total)
    own = product((high[:rows], low[:rows]), (mixing_high, mixing_low))
    own_ref[...] = own * (scale * math.sqrt(times * rows))
    width = rank // times
    source = ((row // width) ^ index_ref[0]) * width + row % width
    move = jnp.where(source == column, 1.0, 0.0).astype(jnp.bfloat16)
    moved = dot(move, jnp.concatenate([mixing_high, mixing_low], axis=1)).astype(jnp.bfloat16)
    turned = product((moved[:, :rank], moved[:, rank:]), (high, low), COLUMNS_BY_COLUMNS) * scale
    high_t_ref[...], low_t_ref[...] = split(turned)


def mix(index, mine, theirs, times, group, order):
    total_half, rank = mine.shape
    rows = 2 * total_half // times
    factor = jax.ShapeDtypeStruct((rank, group * rows), jnp.bfloat16)
    return pl.pallas_call(
        functools.partial(mix_kernel, times, order),
        in_specs=[SMEM, VMEM, VMEM],
        out_specs=[VMEM] * 3,
        out_shape=[factor, factor, jax.ShapeDtypeStruct((rows, rank), jnp.float32)],
        compiler_params=params(),
        cost_estimate=FREE,
    )(index, mine, theirs)


def load_kernel(group, high_ref, low_ref, *refs):
    parts, blocks = refs[:group], refs[group:]
    columns = jnp.concatenate([part[...] for part in parts], axis=0)
    value = product((high_ref[...], low_ref[...]), split(columns))
    width = value.shape[0] // len(blocks)
    for i, block in enumerate(blocks):
        block[...] = value[i * width : (i + 1) * width]


def load(high, low, parts, blocks):
    rank = high.shape[0]
    columns = parts[0].shape[1]
    return pl.pallas_call(
        functools.partial(load_kernel, len(parts)),
        in_specs=[VMEM] * (2 + len(parts)),
        out_specs=[VMEM] * blocks,
        out_shape=[jax.ShapeDtypeStruct((rank // blocks, columns), jnp.float32)] * blocks,
        compiler_params=params(),
        cost_estimate=FREE,
    )(high, low, *parts)


def join_kernel(group, *refs):
    *terms, out_ref, buf, sems = refs
    width = terms[0].shape[1]
    member = lax.rem(lax.axis_index("tm"), group)
    copies = []
    for k in range(group):
        value = terms[k][...]
        for term in terms[group + k :: group]:
            value = value + term[...]
        buf[k] = value
        span = pl.ds(pl.multiple_of((member ^ k) * width, width), width)
        copies.append(pltpu.make_async_copy(buf.at[k], out_ref.at[:, span], sems.at[k]))
        copies[-1].start()
    for copy in copies:
        copy.wait()


def join(terms, group):
    rows, width = terms[0].shape
    return pl.pallas_call(
        functools.partial(join_kernel, group),
        in_specs=[VMEM] * len(terms),
        out_specs=HBM,
        out_shape=jax.ShapeDtypeStruct((rows, group * width), jnp.float32),
        scratch_shapes=[pltpu.VMEM((group, rows, width), jnp.float32), pltpu.SemaphoreType.DMA((group,))],
        compiler_params=params(),
        cost_estimate=FREE,
    )(*terms)


def swap(value, axis, offset):
    return lax.ppermute(value, axis, [(i, i ^ offset) for i in range(lax.axis_size(axis))])


def on_device(snapshots, space_factor):
    rows, points = snapshots.shape
    rank = space_factor.shape[1]
    times, spaces = lax.axis_size("tm"), lax.axis_size("space")
    group = min(4, times)
    index = lax.axis_index("tm")
    core = lax.axis_index("space") % 2

    mine, other, parts = project(snapshots, space_factor, group)
    parts = [part if k == 0 else swap(part, "tm", k) for k, part in enumerate(parts)]

    mine = mine + swap(other, "space", 1)
    for i in range(1, spaces.bit_length() - 1):
        mine = mine + swap(mine, "space", 1 << i)

    near = group // 2
    order = [k for k in range(times) if k % group < near]
    mine = jnp.concatenate([mine] + [swap(mine, "tm", k) for k in order[1:]], axis=0)
    mine, parts[1] = lax.optimization_barrier((mine, parts[1]))
    for offset in range(near, group, near):
        mine = jnp.concatenate([mine, swap(mine, "tm", offset)], axis=0)
        order = order + [k ^ offset for k in order]
    mine, parts[2] = lax.optimization_barrier((mine, parts[2]))
    theirs, parts[3] = lax.optimization_barrier((swap(mine, "space", 1), parts[3]))
    high_t, low_t, own = mix(jnp.stack([index, core]), mine, theirs, times, group, order)

    blocks = list(load(high_t, low_t, parts, times))
    terms = [blocks[0]] + [None] * (times - 1)
    for k in [*range(group, times), *range(1, group)]:
        if k == group - 1:
            blocks[k], terms[1] = lax.optimization_barrier((blocks[k], terms[1]))
        terms[k] = swap(blocks[k], "tm", k)
    return own, join(terms, group)


def solution(mesh):
    return jax.shard_map(
        on_device,
        mesh=mesh,
        in_specs=(P("tm", "space"), P("space", None)),
        out_specs=(P("tm", None), P("tm", "space")),
        check_vma=False,
    )
```

```python
import functools
import math

import jax
import jax.numpy as jnp
from jax import lax
from jax.experimental import pallas as pl
from jax.experimental.pallas import tpu as pltpu
from jax.sharding import PartitionSpec as P

MIB = 1024 * 1024
HBM = pl.BlockSpec(memory_space=pltpu.HBM)
SMEM = pl.BlockSpec(memory_space=pltpu.SMEM)
VMEM = pl.BlockSpec(memory_space=pltpu.VMEM)
FREE = pl.CostEstimate(flops=0, bytes_accessed=0, transcendentals=0)
ROWS_BY_ROWS = (((0,), (0,)), ((), ()))
ROWS_BY_COLUMNS = (((1,), (0,)), ((), ()))
COLUMNS_BY_COLUMNS = (((1,), (1,)), ((), ()))


def params(mib=48):
    return pltpu.CompilerParams(vmem_limit_bytes=mib * MIB)


def split(value):
    high = value.astype(jnp.bfloat16)
    return high, (value - high.astype(jnp.float32)).astype(jnp.bfloat16)


def dot(left, right, dims=ROWS_BY_COLUMNS):
    return lax.dot_general(left, right, dims, preferred_element_type=jnp.float32)


def product(left, right, dims=ROWS_BY_COLUMNS):
    (left_high, left_low), (right_high, right_low) = left, right
    return dot(left_high, right_high, dims) + (
        dot(left_high, right_low, dims) + dot(left_low, right_high, dims)
    )


def project_kernel(depth, snapshots_ref, factor_ref, mine_ref, other_ref, *refs):
    *parts, snapshots_buf, factor_buf, sems = refs
    rows, points = snapshots_ref.shape
    half = rows // 2
    snapshots_copy = pltpu.make_async_copy(snapshots_ref, snapshots_buf, sems.at[points // depth])
    snapshots_copy.start()
    copies = []
    for i, start in enumerate(range(0, points, depth)):
        span = pl.ds(start, depth)
        copies.append(pltpu.make_async_copy(factor_ref.at[span, :], factor_buf.at[span, :], sems.at[i]))
        copies[-1].start()
    snapshots_copy.wait()
    width = parts[0].shape[1]
    member = lax.rem(lax.axis_index("tm"), len(parts))
    for k, part in enumerate(parts):
        part[...] = snapshots_buf[:, pl.ds(pl.multiple_of((member ^ k) * width, width), width)]
    value = None
    for i, start in enumerate(range(0, points, depth)):
        copies[i].wait()
        high, low = split(snapshots_buf[:, start : start + depth])
        factor_high, factor_low = split(factor_buf[start : start + depth, :])
        both = dot(jnp.concatenate([high, low], axis=0), factor_high)
        term = both[:rows] + (both[rows:] + dot(high, factor_low))
        value = term if value is None else value + term
    first = lax.rem(lax.axis_index("space"), 2) == 0
    mine_ref[...] = jnp.where(first, value[:half], value[half:])
    other_ref[...] = jnp.where(first, value[half:], value[:half])


def project(snapshots, space_factor, group):
    rows, points = snapshots.shape
    rank = space_factor.shape[1]
    depth = min(512, points)
    half = jax.ShapeDtypeStruct((rows // 2, rank), jnp.float32)
    part = jax.ShapeDtypeStruct((rows, points // group), jnp.float32)
    mine, other, *parts = pl.pallas_call(
        functools.partial(project_kernel, depth),
        in_specs=[HBM, HBM],
        out_specs=[VMEM] * (2 + group),
        out_shape=[half, half] + [part] * group,
        scratch_shapes=[
            pltpu.VMEM((rows, points), jnp.float32),
            pltpu.VMEM((points, rank), jnp.float32),
            pltpu.SemaphoreType.DMA((points // depth + 1,)),
        ],
        compiler_params=params(52),
        cost_estimate=FREE,
    )(snapshots, space_factor)
    return mine, other, parts


def mix_kernel(times, order, index_ref, mine_ref, theirs_ref, high_t_ref, low_t_ref, own_ref):
    total_half, rank = mine_ref.shape
    half = total_half // times
    mine = mine_ref[...].reshape(times, half, rank)
    theirs = theirs_ref[...].reshape(times, half, rank)
    first = index_ref[1] == 0
    low_rows, high_rows = jnp.where(first, mine, theirs), jnp.where(first, theirs, mine)
    projected = jnp.concatenate([low_rows, high_rows], axis=1).reshape(2 * total_half, rank)
    high, low = split(projected)
    cross = dot(high, low, ROWS_BY_ROWS)
    gram = dot(high, high, ROWS_BY_ROWS) + (cross + cross.T)
    row = lax.broadcasted_iota(jnp.int32, (rank, rank), 0)
    column = lax.broadcasted_iota(jnp.int32, (rank, rank), 1)
    total = jnp.sum(projected * projected)
    correlation = gram / total
    correlation_split = split(correlation)
    square = product(correlation_split, correlation_split)
    tail = jnp.where(row == column, 1.6875, 0.0) - 0.5625 * correlation + 0.0625 * square
    mixing = (jnp.where(row == column, 2.25, 0.0) - 2.4375 * correlation) + product(split(square), split(tail))
    mixing_high, mixing_low = split(mixing)

    rows = 2 * half
    group = high_t_ref.shape[1] // rows
    places = [order.index(k) for k in range(group)]
    high = jnp.concatenate([high[i * rows : (i + 1) * rows] for i in places], axis=0)
    low = jnp.concatenate([low[i * rows : (i + 1) * rows] for i in places], axis=0)
    scale = lax.rsqrt(total)
    own = product((high[:rows], low[:rows]), (mixing_high, mixing_low))
    own_ref[...] = own * (scale * math.sqrt(times * rows))
    width = rank // times
    source = ((row // width) ^ index_ref[0]) * width + row % width
    move = jnp.where(source == column, 1.0, 0.0).astype(jnp.bfloat16)
    moved = dot(move, jnp.concatenate([mixing_high, mixing_low], axis=1)).astype(jnp.bfloat16)
    turned = product((moved[:, :rank], moved[:, rank:]), (high, low), COLUMNS_BY_COLUMNS) * scale
    high_t_ref[...], low_t_ref[...] = split(turned)


def mix(index, mine, theirs, times, group, order):
    total_half, rank = mine.shape
    rows = 2 * total_half // times
    factor = jax.ShapeDtypeStruct((rank, group * rows), jnp.bfloat16)
    return pl.pallas_call(
        functools.partial(mix_kernel, times, order),
        in_specs=[SMEM, VMEM, VMEM],
        out_specs=[VMEM] * 3,
        out_shape=[factor, factor, jax.ShapeDtypeStruct((rows, rank), jnp.float32)],
        compiler_params=params(),
        cost_estimate=FREE,
    )(index, mine, theirs)


def load_kernel(group, high_ref, low_ref, *refs):
    parts, blocks = refs[:group], refs[group:]
    columns = jnp.concatenate([part[...] for part in parts], axis=0)
    value = product((high_ref[...], low_ref[...]), split(columns))
    width = value.shape[0] // len(blocks)
    for i, block in enumerate(blocks):
        block[...] = value[i * width : (i + 1) * width]


def load(high, low, parts, blocks):
    rank = high.shape[0]
    columns = parts[0].shape[1]
    return pl.pallas_call(
        functools.partial(load_kernel, len(parts)),
        in_specs=[VMEM] * (2 + len(parts)),
        out_specs=[VMEM] * blocks,
        out_shape=[jax.ShapeDtypeStruct((rank // blocks, columns), jnp.float32)] * blocks,
        compiler_params=params(),
        cost_estimate=FREE,
    )(high, low, *parts)


def join_kernel(group, *refs):
    *terms, out_ref, buf, sems = refs
    width = terms[0].shape[1]
    member = lax.rem(lax.axis_index("tm"), group)
    copies = []
    for k in range(group):
        value = terms[k][...]
        for term in terms[group + k :: group]:
            value = value + term[...]
        buf[k] = value
        span = pl.ds(pl.multiple_of((member ^ k) * width, width), width)
        copies.append(pltpu.make_async_copy(buf.at[k], out_ref.at[:, span], sems.at[k]))
        copies[-1].start()
    for copy in copies:
        copy.wait()


def join(terms, group):
    rows, width = terms[0].shape
    return pl.pallas_call(
        functools.partial(join_kernel, group),
        in_specs=[VMEM] * len(terms),
        out_specs=HBM,
        out_shape=jax.ShapeDtypeStruct((rows, group * width), jnp.float32),
        scratch_shapes=[pltpu.VMEM((group, rows, width), jnp.float32), pltpu.SemaphoreType.DMA((group,))],
        compiler_params=params(),
        cost_estimate=FREE,
    )(*terms)


def swap(value, axis, offset):
    return lax.ppermute(value, axis, [(i, i ^ offset) for i in range(lax.axis_size(axis))])


def on_device(snapshots, space_factor):
    rows, points = snapshots.shape
    rank = space_factor.shape[1]
    times, spaces = lax.axis_size("tm"), lax.axis_size("space")
    group = min(4, times)
    index = lax.axis_index("tm")
    core = lax.axis_index("space") % 2

    mine, other, parts = project(snapshots, space_factor, group)
    parts = [part if k == 0 else swap(part, "tm", k) for k, part in enumerate(parts)]

    mine = mine + swap(other, "space", 1)
    for i in range(1, spaces.bit_length() - 1):
        mine = mine + swap(mine, "space", 1 << i)

    near = group // 2
    order = [k for k in range(times) if k % group < near]
    mine = jnp.concatenate([mine] + [swap(mine, "tm", k) for k in order[1:]], axis=0)
    mine, parts = lax.optimization_barrier((mine, parts))
    for offset in range(near, group, near):
        mine = jnp.concatenate([mine, swap(mine, "tm", offset)], axis=0)
        order = order + [k ^ offset for k in order]
    high_t, low_t, own = mix(jnp.stack([index, core]), mine, swap(mine, "space", 1), times, group, order)

    blocks = list(load(high_t, low_t, parts, times))
    terms = [blocks[0]] + [None] * (times - 1)
    for k in [*range(group, times), *range(1, group)]:
        if k == group - 1:
            blocks[k], terms[1] = lax.optimization_barrier((blocks[k], terms[1]))
        terms[k] = swap(blocks[k], "tm", k)
    return own, join(terms, group)


def solution(mesh):
    return jax.shard_map(
        on_device,
        mesh=mesh,
        in_specs=(P("tm", "space"), P("space", None)),
        out_specs=(P("tm", None), P("tm", "space")),
        check_vma=False,
    )
```

```python
import functools
import math

import jax
import jax.numpy as jnp
from jax import lax
from jax.experimental import pallas as pl
from jax.experimental.pallas import tpu as pltpu
from jax.sharding import PartitionSpec as P

MIB = 1024 * 1024
HBM = pl.BlockSpec(memory_space=pltpu.HBM)
SMEM = pl.BlockSpec(memory_space=pltpu.SMEM)
VMEM = pl.BlockSpec(memory_space=pltpu.VMEM)
FREE = pl.CostEstimate(flops=0, bytes_accessed=0, transcendentals=0)
ROWS_BY_ROWS = (((0,), (0,)), ((), ()))
ROWS_BY_COLUMNS = (((1,), (0,)), ((), ()))
COLUMNS_BY_COLUMNS = (((1,), (1,)), ((), ()))


def params(mib=48):
    return pltpu.CompilerParams(vmem_limit_bytes=mib * MIB)


def split(value):
    high = value.astype(jnp.bfloat16)
    return high, (value - high.astype(jnp.float32)).astype(jnp.bfloat16)


def dot(left, right, dims=ROWS_BY_COLUMNS):
    return lax.dot_general(left, right, dims, preferred_element_type=jnp.float32)


def product(left, right, dims=ROWS_BY_COLUMNS):
    (left_high, left_low), (right_high, right_low) = left, right
    return dot(left_high, right_high, dims) + (
        dot(left_high, right_low, dims) + dot(left_low, right_high, dims)
    )


def project_kernel(depth, snapshots_ref, factor_ref, mine_ref, other_ref, *refs):
    *parts, snapshots_buf, factor_buf, sems = refs
    rows, points = snapshots_ref.shape
    half = rows // 2
    snapshots_copy = pltpu.make_async_copy(snapshots_ref, snapshots_buf, sems.at[points // depth])
    snapshots_copy.start()
    copies = []
    for i, start in enumerate(range(0, points, depth)):
        span = pl.ds(start, depth)
        copies.append(pltpu.make_async_copy(factor_ref.at[span, :], factor_buf.at[span, :], sems.at[i]))
        copies[-1].start()
    snapshots_copy.wait()
    width = parts[0].shape[1]
    member = lax.rem(lax.axis_index("tm"), len(parts))
    for k, part in enumerate(parts):
        part[...] = snapshots_buf[:, pl.ds(pl.multiple_of((member ^ k) * width, width), width)]
    value = None
    for i, start in enumerate(range(0, points, depth)):
        copies[i].wait()
        high, low = split(snapshots_buf[:, start : start + depth])
        factor_high, factor_low = split(factor_buf[start : start + depth, :])
        both = dot(jnp.concatenate([high, low], axis=0), factor_high)
        term = both[:rows] + (both[rows:] + dot(high, factor_low))
        value = term if value is None else value + term
    first = lax.rem(lax.axis_index("space"), 2) == 0
    mine_ref[...] = jnp.where(first, value[:half], value[half:])
    other_ref[...] = jnp.where(first, value[half:], value[:half])


def project(snapshots, space_factor, group):
    rows, points = snapshots.shape
    rank = space_factor.shape[1]
    depth = min(512, points)
    half = jax.ShapeDtypeStruct((rows // 2, rank), jnp.float32)
    part = jax.ShapeDtypeStruct((rows, points // group), jnp.float32)
    mine, other, *parts = pl.pallas_call(
        functools.partial(project_kernel, depth),
        in_specs=[HBM, HBM],
        out_specs=[VMEM] * (2 + group),
        out_shape=[half, half] + [part] * group,
        scratch_shapes=[
            pltpu.VMEM((rows, points), jnp.float32),
            pltpu.VMEM((points, rank), jnp.float32),
            pltpu.SemaphoreType.DMA((points // depth + 1,)),
        ],
        compiler_params=params(52),
        cost_estimate=FREE,
    )(snapshots, space_factor)
    return mine, other, parts


def mix_kernel(times, order, index_ref, mine_ref, theirs_ref, high_t_ref, low_t_ref, own_ref):
    total_half, rank = mine_ref.shape
    half = total_half // times
    mine = mine_ref[...].reshape(times, half, rank)
    theirs = theirs_ref[...].reshape(times, half, rank)
    first = index_ref[1] == 0
    low_rows, high_rows = jnp.where(first, mine, theirs), jnp.where(first, theirs, mine)
    projected = jnp.concatenate([low_rows, high_rows], axis=1).reshape(2 * total_half, rank)
    high, low = split(projected)
    cross = dot(high, low, ROWS_BY_ROWS)
    gram = dot(high, high, ROWS_BY_ROWS) + (cross + cross.T)
    row = lax.broadcasted_iota(jnp.int32, (rank, rank), 0)
    column = lax.broadcasted_iota(jnp.int32, (rank, rank), 1)
    total = jnp.sum(projected * projected)
    correlation = gram / total
    correlation_split = split(correlation)
    square = product(correlation_split, correlation_split)
    tail = jnp.where(row == column, 1.6875, 0.0) - 0.5625 * correlation + 0.0625 * square
    mixing = (jnp.where(row == column, 2.25, 0.0) - 2.4375 * correlation) + product(split(square), split(tail))
    mixing_high, mixing_low = split(mixing)

    rows = 2 * half
    group = high_t_ref.shape[1] // rows
    places = [order.index(k) for k in range(group)]
    high = jnp.concatenate([high[i * rows : (i + 1) * rows] for i in places], axis=0)
    low = jnp.concatenate([low[i * rows : (i + 1) * rows] for i in places], axis=0)
    scale = lax.rsqrt(total)
    own = product((high[:rows], low[:rows]), (mixing_high, mixing_low))
    own_ref[...] = own * (scale * math.sqrt(times * rows))
    width = rank // times
    source = ((row // width) ^ index_ref[0]) * width + row % width
    move = jnp.where(source == column, 1.0, 0.0).astype(jnp.bfloat16)
    moved = dot(move, jnp.concatenate([mixing_high, mixing_low], axis=1)).astype(jnp.bfloat16)
    turned = product((moved[:, :rank], moved[:, rank:]), (high, low), COLUMNS_BY_COLUMNS) * scale
    high_t_ref[...], low_t_ref[...] = split(turned)


def mix(index, mine, theirs, times, group, order):
    total_half, rank = mine.shape
    rows = 2 * total_half // times
    factor = jax.ShapeDtypeStruct((rank, group * rows), jnp.bfloat16)
    return pl.pallas_call(
        functools.partial(mix_kernel, times, order),
        in_specs=[SMEM, VMEM, VMEM],
        out_specs=[VMEM] * 3,
        out_shape=[factor, factor, jax.ShapeDtypeStruct((rows, rank), jnp.float32)],
        compiler_params=params(),
        cost_estimate=FREE,
    )(index, mine, theirs)


def load_kernel(group, high_ref, low_ref, *refs):
    parts, blocks = refs[:group], refs[group:]
    columns = jnp.concatenate([part[...] for part in parts], axis=0)
    value = product((high_ref[...], low_ref[...]), split(columns))
    width = value.shape[0] // len(blocks)
    for i, block in enumerate(blocks):
        block[...] = value[i * width : (i + 1) * width]


def load(high, low, parts, blocks):
    rank = high.shape[0]
    columns = parts[0].shape[1]
    return pl.pallas_call(
        functools.partial(load_kernel, len(parts)),
        in_specs=[VMEM] * (2 + len(parts)),
        out_specs=[VMEM] * blocks,
        out_shape=[jax.ShapeDtypeStruct((rank // blocks, columns), jnp.float32)] * blocks,
        compiler_params=params(),
        cost_estimate=FREE,
    )(high, low, *parts)


def join_kernel(group, *refs):
    *terms, out_ref, buf, sems = refs
    width = terms[0].shape[1]
    member = lax.rem(lax.axis_index("tm"), group)
    copies = []
    for k in range(group):
        value = terms[k][...]
        for term in terms[group + k :: group]:
            value = value + term[...]
        buf[k] = value
        span = pl.ds(pl.multiple_of((member ^ k) * width, width), width)
        copies.append(pltpu.make_async_copy(buf.at[k], out_ref.at[:, span], sems.at[k]))
        copies[-1].start()
    for copy in copies:
        copy.wait()


def join(terms, group):
    rows, width = terms[0].shape
    return pl.pallas_call(
        functools.partial(join_kernel, group),
        in_specs=[VMEM] * len(terms),
        out_specs=HBM,
        out_shape=jax.ShapeDtypeStruct((rows, group * width), jnp.float32),
        scratch_shapes=[pltpu.VMEM((group, rows, width), jnp.float32), pltpu.SemaphoreType.DMA((group,))],
        compiler_params=params(),
        cost_estimate=FREE,
    )(*terms)


def swap(value, axis, offset):
    return lax.ppermute(value, axis, [(i, i ^ offset) for i in range(lax.axis_size(axis))])


def on_device(snapshots, space_factor):
    rows, points = snapshots.shape
    rank = space_factor.shape[1]
    times, spaces = lax.axis_size("tm"), lax.axis_size("space")
    group = min(4, times)
    index = lax.axis_index("tm")
    core = lax.axis_index("space") % 2

    mine, other, parts = project(snapshots, space_factor, group)
    parts = [part if k == 0 else swap(part, "tm", k) for k, part in enumerate(parts)]

    mine = mine + swap(other, "space", 1)
    for i in range(1, spaces.bit_length() - 1):
        mine = mine + swap(mine, "space", 1 << i)

    near = group // 2
    order = [k for k in range(times) if k % group < near]
    mine = jnp.concatenate([mine] + [swap(mine, "tm", k) for k in order[1:]], axis=0)
    mine, *parts[2:] = lax.optimization_barrier((mine, *parts[2:]))
    for offset in range(near, group, near):
        mine = jnp.concatenate([mine, swap(mine, "tm", offset)], axis=0)
        order = order + [k ^ offset for k in order]
    theirs, parts[1] = lax.optimization_barrier((swap(mine, "space", 1), parts[1]))
    high_t, low_t, own = mix(jnp.stack([index, core]), mine, theirs, times, group, order)

    blocks = list(load(high_t, low_t, parts, times))
    terms = [blocks[0]] + [None] * (times - 1)
    for k in [*range(group, times), *range(1, group)]:
        if k == group - 1:
            blocks[k], terms[1] = lax.optimization_barrier((blocks[k], terms[1]))
        terms[k] = swap(blocks[k], "tm", k)
    return own, join(terms, group)


def solution(mesh):
    return jax.shard_map(
        on_device,
        mesh=mesh,
        in_specs=(P("tm", "space"), P("space", None)),
        out_specs=(P("tm", None), P("tm", "space")),
        check_vma=False,
    )
```

```python
import functools
import math

import jax
import jax.numpy as jnp
from jax import lax
from jax.experimental import pallas as pl
from jax.experimental.pallas import tpu as pltpu
from jax.sharding import PartitionSpec as P

MIB = 1024 * 1024
HBM = pl.BlockSpec(memory_space=pltpu.HBM)
SMEM = pl.BlockSpec(memory_space=pltpu.SMEM)
VMEM = pl.BlockSpec(memory_space=pltpu.VMEM)
FREE = pl.CostEstimate(flops=0, bytes_accessed=0, transcendentals=0)
ROWS_BY_ROWS = (((0,), (0,)), ((), ()))
ROWS_BY_COLUMNS = (((1,), (0,)), ((), ()))
COLUMNS_BY_COLUMNS = (((1,), (1,)), ((), ()))


def params(mib=48):
    return pltpu.CompilerParams(vmem_limit_bytes=mib * MIB)


def split(value):
    high = value.astype(jnp.bfloat16)
    return high, (value - high.astype(jnp.float32)).astype(jnp.bfloat16)


def dot(left, right, dims=ROWS_BY_COLUMNS):
    return lax.dot_general(left, right, dims, preferred_element_type=jnp.float32)


def product(left, right, dims=ROWS_BY_COLUMNS):
    (left_high, left_low), (right_high, right_low) = left, right
    return dot(left_high, right_high, dims) + (
        dot(left_high, right_low, dims) + dot(left_low, right_high, dims)
    )


def project_kernel(depth, snapshots_ref, factor_ref, mine_ref, other_ref, *refs):
    *parts, snapshots_buf, factor_buf, sems = refs
    rows, points = snapshots_ref.shape
    half = rows // 2
    snapshots_copy = pltpu.make_async_copy(snapshots_ref, snapshots_buf, sems.at[points // depth])
    snapshots_copy.start()
    copies = []
    for i, start in enumerate(range(0, points, depth)):
        span = pl.ds(start, depth)
        copies.append(pltpu.make_async_copy(factor_ref.at[span, :], factor_buf.at[span, :], sems.at[i]))
        copies[-1].start()
    snapshots_copy.wait()
    width = parts[0].shape[1]
    member = lax.rem(lax.axis_index("tm"), len(parts))
    for k, part in enumerate(parts):
        part[...] = snapshots_buf[:, pl.ds(pl.multiple_of((member ^ k) * width, width), width)]
    value = None
    for i, start in enumerate(range(0, points, depth)):
        copies[i].wait()
        high, low = split(snapshots_buf[:, start : start + depth])
        factor_high, factor_low = split(factor_buf[start : start + depth, :])
        both = dot(jnp.concatenate([high, low], axis=0), factor_high)
        term = both[:rows] + (both[rows:] + dot(high, factor_low))
        value = term if value is None else value + term
    first = lax.rem(lax.axis_index("space"), 2) == 0
    mine_ref[...] = jnp.where(first, value[:half], value[half:])
    other_ref[...] = jnp.where(first, value[half:], value[:half])


def project(snapshots, space_factor, group):
    rows, points = snapshots.shape
    rank = space_factor.shape[1]
    depth = min(512, points)
    half = jax.ShapeDtypeStruct((rows // 2, rank), jnp.float32)
    part = jax.ShapeDtypeStruct((rows, points // group), jnp.float32)
    mine, other, *parts = pl.pallas_call(
        functools.partial(project_kernel, depth),
        in_specs=[HBM, HBM],
        out_specs=[VMEM] * (2 + group),
        out_shape=[half, half] + [part] * group,
        scratch_shapes=[
            pltpu.VMEM((rows, points), jnp.float32),
            pltpu.VMEM((points, rank), jnp.float32),
            pltpu.SemaphoreType.DMA((points // depth + 1,)),
        ],
        compiler_params=params(52),
        cost_estimate=FREE,
    )(snapshots, space_factor)
    return mine, other, parts


def mix_kernel(times, order, index_ref, mine_ref, theirs_ref, high_t_ref, low_t_ref, own_ref):
    total_half, rank = mine_ref.shape
    half = total_half // times
    mine = mine_ref[...].reshape(times, half, rank)
    theirs = theirs_ref[...].reshape(times, half, rank)
    first = index_ref[1] == 0
    low_rows, high_rows = jnp.where(first, mine, theirs), jnp.where(first, theirs, mine)
    projected = jnp.concatenate([low_rows, high_rows], axis=1).reshape(2 * total_half, rank)
    high, low = split(projected)
    cross = dot(high, low, ROWS_BY_ROWS)
    gram = dot(high, high, ROWS_BY_ROWS) + (cross + cross.T)
    row = lax.broadcasted_iota(jnp.int32, (rank, rank), 0)
    column = lax.broadcasted_iota(jnp.int32, (rank, rank), 1)
    total = jnp.sum(projected * projected)
    correlation = gram / total
    correlation_split = split(correlation)
    square = product(correlation_split, correlation_split)
    tail = jnp.where(row == column, 1.6875, 0.0) - 0.5625 * correlation + 0.0625 * square
    mixing = (jnp.where(row == column, 2.25, 0.0) - 2.4375 * correlation) + product(split(square), split(tail))
    mixing_high, mixing_low = split(mixing)

    rows = 2 * half
    group = high_t_ref.shape[1] // rows
    places = [order.index(k) for k in range(group)]
    high = jnp.concatenate([high[i * rows : (i + 1) * rows] for i in places], axis=0)
    low = jnp.concatenate([low[i * rows : (i + 1) * rows] for i in places], axis=0)
    factor = product((high, low), (mixing_high, mixing_low)) * lax.rsqrt(total)
    own_ref[...] = factor[:rows] * math.sqrt(times * rows)
    high_t_ref[...], low_t_ref[...] = split(factor.T)


def mix(index, mine, theirs, times, group, order):
    total_half, rank = mine.shape
    rows = 2 * total_half // times
    factor = jax.ShapeDtypeStruct((rank, group * rows), jnp.bfloat16)
    return pl.pallas_call(
        functools.partial(mix_kernel, times, order),
        in_specs=[SMEM, VMEM, VMEM],
        out_specs=[VMEM] * 3,
        out_shape=[factor, factor, jax.ShapeDtypeStruct((rows, rank), jnp.float32)],
        compiler_params=params(),
        cost_estimate=FREE,
    )(index, mine, theirs)


def load_kernel(group, index_ref, high_ref, low_ref, *refs):
    parts, blocks = refs[:group], refs[group:]
    times = len(blocks)
    rank = high_ref.shape[0]
    width = rank // times
    if width % 16 == 0:
        starts = [pl.multiple_of((index_ref[0] ^ k) * width, width) for k in range(times)]
        high, low = [
            jnp.concatenate([ref[pl.ds(start, width), :] for start in starts], axis=0) for ref in (high_ref, low_ref)
        ]
    else:
        row = lax.broadcasted_iota(jnp.int32, (rank, rank), 0)
        source = ((row // width) ^ index_ref[0]) * width + row % width
        column = lax.broadcasted_iota(jnp.int32, row.shape, 1)
        move = jnp.where(source == column, 1.0, 0.0).astype(jnp.bfloat16)
        high, low = [dot(move, ref[...]).astype(jnp.bfloat16) for ref in (high_ref, low_ref)]
    columns = jnp.concatenate([part[...] for part in parts], axis=0)
    value = product((high, low), split(columns))
    for i, block in enumerate(blocks):
        block[...] = value[i * width : (i + 1) * width]


def load(index, high, low, parts, times):
    rank = high.shape[0]
    columns = parts[0].shape[1]
    return pl.pallas_call(
        functools.partial(load_kernel, len(parts)),
        in_specs=[SMEM] + [VMEM] * (2 + len(parts)),
        out_specs=[VMEM] * times,
        out_shape=[jax.ShapeDtypeStruct((rank // times, columns), jnp.float32)] * times,
        compiler_params=params(),
        cost_estimate=FREE,
    )(index, high, low, *parts)


def join_kernel(group, *refs):
    *terms, out_ref, buf, sems = refs
    width = terms[0].shape[1]
    member = lax.rem(lax.axis_index("tm"), group)
    copies = []
    for k in range(group):
        value = terms[k][...]
        for term in terms[group + k :: group]:
            value = value + term[...]
        buf[k] = value
        span = pl.ds(pl.multiple_of((member ^ k) * width, width), width)
        copies.append(pltpu.make_async_copy(buf.at[k], out_ref.at[:, span], sems.at[k]))
        copies[-1].start()
    for copy in copies:
        copy.wait()


def join(terms, group):
    rows, width = terms[0].shape
    return pl.pallas_call(
        functools.partial(join_kernel, group),
        in_specs=[VMEM] * len(terms),
        out_specs=HBM,
        out_shape=jax.ShapeDtypeStruct((rows, group * width), jnp.float32),
        scratch_shapes=[pltpu.VMEM((group, rows, width), jnp.float32), pltpu.SemaphoreType.DMA((group,))],
        compiler_params=params(),
        cost_estimate=FREE,
    )(*terms)


def swap(value, axis, offset):
    return lax.ppermute(value, axis, [(i, i ^ offset) for i in range(lax.axis_size(axis))])


def on_device(snapshots, space_factor):
    rows, points = snapshots.shape
    rank = space_factor.shape[1]
    times, spaces = lax.axis_size("tm"), lax.axis_size("space")
    group = min(4, times)
    index = lax.axis_index("tm")
    core = lax.axis_index("space") % 2

    mine, other, parts = project(snapshots, space_factor, group)
    parts = [part if k == 0 else swap(part, "tm", k) for k, part in enumerate(parts)]

    mine = mine + swap(other, "space", 1)
    for i in range(1, spaces.bit_length() - 1):
        mine = mine + swap(mine, "space", 1 << i)

    near = group // 2
    order = [k for k in range(times) if k % group < near]
    mine = jnp.concatenate([mine] + [swap(mine, "tm", k) for k in order[1:]], axis=0)
    mine, *parts[2:] = lax.optimization_barrier((mine, *parts[2:]))
    for offset in range(near, group, near):
        mine = jnp.concatenate([mine, swap(mine, "tm", offset)], axis=0)
        order = order + [k ^ offset for k in order]
    mine, parts[1] = lax.optimization_barrier((mine, parts[1]))
    theirs = swap(mine, "space", 1)
    high_t, low_t, own = mix(jnp.stack([index, core]), mine, theirs, times, group, order)

    blocks = list(load(index.reshape(1), high_t, low_t, parts, times))
    terms = [blocks[0]] + [None] * (times - 1)
    for k in [*range(group, times), *range(1, group)]:
        if k == group - 1:
            blocks[k], terms[1] = lax.optimization_barrier((blocks[k], terms[1]))
        terms[k] = swap(blocks[k], "tm", k)
    return own, join(terms, group)


def solution(mesh):
    return jax.shard_map(
        on_device,
        mesh=mesh,
        in_specs=(P("tm", "space"), P("space", None)),
        out_specs=(P("tm", None), P("tm", "space")),
        check_vma=False,
    )
```

```python
import functools
import math

import jax
import jax.numpy as jnp
from jax import lax
from jax.experimental import pallas as pl
from jax.experimental.pallas import tpu as pltpu
from jax.sharding import PartitionSpec as P

MIB = 1024 * 1024
HBM = pl.BlockSpec(memory_space=pltpu.HBM)
SMEM = pl.BlockSpec(memory_space=pltpu.SMEM)
VMEM = pl.BlockSpec(memory_space=pltpu.VMEM)
FREE = pl.CostEstimate(flops=0, bytes_accessed=0, transcendentals=0)
ROWS_BY_ROWS = (((0,), (0,)), ((), ()))
ROWS_BY_COLUMNS = (((1,), (0,)), ((), ()))
COLUMNS_BY_COLUMNS = (((1,), (1,)), ((), ()))


def params(mib=48):
    return pltpu.CompilerParams(vmem_limit_bytes=mib * MIB)


def split(value):
    high = value.astype(jnp.bfloat16)
    return high, (value - high.astype(jnp.float32)).astype(jnp.bfloat16)


def dot(left, right, dims=ROWS_BY_COLUMNS):
    return lax.dot_general(left, right, dims, preferred_element_type=jnp.float32)


def product(left, right, dims=ROWS_BY_COLUMNS):
    (left_high, left_low), (right_high, right_low) = left, right
    return dot(left_high, right_high, dims) + (
        dot(left_high, right_low, dims) + dot(left_low, right_high, dims)
    )


def project_kernel(depth, snapshots_ref, factor_ref, mine_ref, other_ref, *refs):
    *parts, snapshots_buf, factor_buf, sems = refs
    rows, points = snapshots_ref.shape
    half = rows // 2
    snapshots_copy = pltpu.make_async_copy(snapshots_ref, snapshots_buf, sems.at[points // depth])
    snapshots_copy.start()
    copies = []
    for i, start in enumerate(range(0, points, depth)):
        span = pl.ds(start, depth)
        copies.append(pltpu.make_async_copy(factor_ref.at[span, :], factor_buf.at[span, :], sems.at[i]))
        copies[-1].start()
    snapshots_copy.wait()
    width = parts[0].shape[1]
    member = lax.rem(lax.axis_index("tm"), len(parts))
    for k, part in enumerate(parts):
        part[...] = snapshots_buf[:, pl.ds(pl.multiple_of((member ^ k) * width, width), width)]
    value = None
    for i, start in enumerate(range(0, points, depth)):
        copies[i].wait()
        high, low = split(snapshots_buf[:, start : start + depth])
        factor_high, factor_low = split(factor_buf[start : start + depth, :])
        both = dot(jnp.concatenate([high, low], axis=0), factor_high)
        term = both[:rows] + (both[rows:] + dot(high, factor_low))
        value = term if value is None else value + term
    first = lax.rem(lax.axis_index("space"), 2) == 0
    mine_ref[...] = jnp.where(first, value[:half], value[half:])
    other_ref[...] = jnp.where(first, value[half:], value[:half])


def project(snapshots, space_factor, group):
    rows, points = snapshots.shape
    rank = space_factor.shape[1]
    depth = min(512, points)
    half = jax.ShapeDtypeStruct((rows // 2, rank), jnp.float32)
    part = jax.ShapeDtypeStruct((rows, points // group), jnp.float32)
    mine, other, *parts = pl.pallas_call(
        functools.partial(project_kernel, depth),
        in_specs=[HBM, HBM],
        out_specs=[VMEM] * (2 + group),
        out_shape=[half, half] + [part] * group,
        scratch_shapes=[
            pltpu.VMEM((rows, points), jnp.float32),
            pltpu.VMEM((points, rank), jnp.float32),
            pltpu.SemaphoreType.DMA((points // depth + 1,)),
        ],
        compiler_params=params(52),
        cost_estimate=FREE,
    )(snapshots, space_factor)
    return mine, other, parts


def mix_kernel(times, order, index_ref, mine_ref, theirs_ref, high_t_ref, low_t_ref, own_ref):
    total_half, rank = mine_ref.shape
    half = total_half // times
    mine = mine_ref[...].reshape(times, half, rank)
    theirs = theirs_ref[...].reshape(times, half, rank)
    first = index_ref[1] == 0
    low_rows, high_rows = jnp.where(first, mine, theirs), jnp.where(first, theirs, mine)
    projected = jnp.concatenate([low_rows, high_rows], axis=1).reshape(2 * total_half, rank)
    high, low = split(projected)
    cross = dot(high, low, ROWS_BY_ROWS)
    gram = dot(high, high, ROWS_BY_ROWS) + (cross + cross.T)
    row = lax.broadcasted_iota(jnp.int32, (rank, rank), 0)
    column = lax.broadcasted_iota(jnp.int32, (rank, rank), 1)
    total = jnp.sum(projected * projected)
    correlation = gram / total
    correlation_split = split(correlation)
    square = product(correlation_split, correlation_split)
    tail = jnp.where(row == column, 1.6875, 0.0) - 0.5625 * correlation + 0.0625 * square
    mixing = (jnp.where(row == column, 2.25, 0.0) - 2.4375 * correlation) + product(split(square), split(tail))
    mixing_high, mixing_low = split(mixing)

    rows = 2 * half
    group = high_t_ref.shape[1] // rows
    places = [order.index(k) for k in range(group)]
    high = jnp.concatenate([high[i * rows : (i + 1) * rows] for i in places], axis=0)
    low = jnp.concatenate([low[i * rows : (i + 1) * rows] for i in places], axis=0)
    scale = lax.rsqrt(total)
    own = product((high[:rows], low[:rows]), (mixing_high, mixing_low))
    own_ref[...] = own * (scale * math.sqrt(times * rows))
    width = rank // times
    source = ((row // width) ^ index_ref[0]) * width + row % width
    move = jnp.where(source == column, 1.0, 0.0).astype(jnp.bfloat16)
    moved = dot(move, jnp.concatenate([mixing_high, mixing_low], axis=1)).astype(jnp.bfloat16)
    turned = product((moved[:, :rank], moved[:, rank:]), (high, low), COLUMNS_BY_COLUMNS) * scale
    high_t_ref[...], low_t_ref[...] = split(turned)


def mix(index, mine, theirs, times, group, order):
    total_half, rank = mine.shape
    rows = 2 * total_half // times
    factor = jax.ShapeDtypeStruct((rank, group * rows), jnp.bfloat16)
    return pl.pallas_call(
        functools.partial(mix_kernel, times, order),
        in_specs=[SMEM, VMEM, VMEM],
        out_specs=[VMEM] * 3,
        out_shape=[factor, factor, jax.ShapeDtypeStruct((rows, rank), jnp.float32)],
        compiler_params=params(),
        cost_estimate=FREE,
    )(index, mine, theirs)


def load_kernel(group, high_ref, low_ref, *refs):
    parts, blocks = refs[:group], refs[group:]
    columns = jnp.concatenate([part[...] for part in parts], axis=0)
    value = product((high_ref[...], low_ref[...]), split(columns))
    width = value.shape[0] // len(blocks)
    for i, block in enumerate(blocks):
        block[...] = value[i * width : (i + 1) * width]


def load(high, low, parts, blocks):
    rank = high.shape[0]
    columns = parts[0].shape[1]
    return pl.pallas_call(
        functools.partial(load_kernel, len(parts)),
        in_specs=[VMEM] * (2 + len(parts)),
        out_specs=[VMEM] * blocks,
        out_shape=[jax.ShapeDtypeStruct((rank // blocks, columns), jnp.float32)] * blocks,
        compiler_params=params(),
        cost_estimate=FREE,
    )(high, low, *parts)


def join_kernel(group, *refs):
    *terms, out_ref, buf, sems = refs
    width = terms[0].shape[1]
    member = lax.rem(lax.axis_index("tm"), group)
    copies = []
    for k in range(group):
        value = terms[k][...]
        for term in terms[group + k :: group]:
            value = value + term[...]
        buf[k] = value
        span = pl.ds(pl.multiple_of((member ^ k) * width, width), width)
        copies.append(pltpu.make_async_copy(buf.at[k], out_ref.at[:, span], sems.at[k]))
        copies[-1].start()
    for copy in copies:
        copy.wait()


def join(terms, group):
    rows, width = terms[0].shape
    return pl.pallas_call(
        functools.partial(join_kernel, group),
        in_specs=[VMEM] * len(terms),
        out_specs=HBM,
        out_shape=jax.ShapeDtypeStruct((rows, group * width), jnp.float32),
        scratch_shapes=[pltpu.VMEM((group, rows, width), jnp.float32), pltpu.SemaphoreType.DMA((group,))],
        compiler_params=params(),
        cost_estimate=FREE,
    )(*terms)


def swap(value, axis, offset):
    return lax.ppermute(value, axis, [(i, i ^ offset) for i in range(lax.axis_size(axis))])


def on_device(snapshots, space_factor):
    rows, points = snapshots.shape
    rank = space_factor.shape[1]
    times, spaces = lax.axis_size("tm"), lax.axis_size("space")
    group = min(4, times)
    index = lax.axis_index("tm")
    core = lax.axis_index("space") % 2

    mine, other, parts = project(snapshots, space_factor, group)
    parts = [part if k == 0 else swap(part, "tm", k) for k, part in enumerate(parts)]

    terms = [mine] + [swap(other if k % 2 else mine, "space", k) for k in range(1, spaces)]
    while len(terms) > 1:
        terms = [a + b for a, b in zip(terms[::2], terms[1::2])]
    mine = terms[0]

    near = group // 2
    order = [k for k in range(times) if k % group < near]
    mine = jnp.concatenate([mine] + [swap(mine, "tm", k) for k in order[1:]], axis=0)
    mine, *parts[2:] = lax.optimization_barrier((mine, *parts[2:]))
    for offset in range(near, group, near):
        mine = jnp.concatenate([mine, swap(mine, "tm", offset)], axis=0)
        order = order + [k ^ offset for k in order]
    theirs, parts[1] = lax.optimization_barrier((swap(mine, "space", 1), parts[1]))
    high_t, low_t, own = mix(jnp.stack([index, core]), mine, theirs, times, group, order)

    blocks = list(load(high_t, low_t, parts, times))
    terms = [blocks[0]] + [None] * (times - 1)
    for k in [*range(group, times), *range(1, group)]:
        if k == group - 1:
            blocks[k], terms[1] = lax.optimization_barrier((blocks[k], terms[1]))
        terms[k] = swap(blocks[k], "tm", k)
    return own, join(terms, group)


def solution(mesh):
    return jax.shard_map(
        on_device,
        mesh=mesh,
        in_specs=(P("tm", "space"), P("space", None)),
        out_specs=(P("tm", None), P("tm", "space")),
        check_vma=False,
    )
```

```python
import functools
import math

import jax
import jax.numpy as jnp
from jax import lax
from jax.experimental import pallas as pl
from jax.experimental.pallas import tpu as pltpu
from jax.sharding import PartitionSpec as P

MIB = 1024 * 1024
HBM = pl.BlockSpec(memory_space=pltpu.HBM)
SMEM = pl.BlockSpec(memory_space=pltpu.SMEM)
VMEM = pl.BlockSpec(memory_space=pltpu.VMEM)
FREE = pl.CostEstimate(flops=0, bytes_accessed=0, transcendentals=0)
ROWS_BY_ROWS = (((0,), (0,)), ((), ()))
ROWS_BY_COLUMNS = (((1,), (0,)), ((), ()))
COLUMNS_BY_COLUMNS = (((1,), (1,)), ((), ()))


def params(mib=48):
    return pltpu.CompilerParams(vmem_limit_bytes=mib * MIB)


def split(value):
    high = value.astype(jnp.bfloat16)
    return high, (value - high.astype(jnp.float32)).astype(jnp.bfloat16)


def dot(left, right, dims=ROWS_BY_COLUMNS):
    return lax.dot_general(left, right, dims, preferred_element_type=jnp.float32)


def product(left, right, dims=ROWS_BY_COLUMNS):
    (left_high, left_low), (right_high, right_low) = left, right
    return dot(left_high, right_high, dims) + (
        dot(left_high, right_low, dims) + dot(left_low, right_high, dims)
    )


def project_kernel(depth, snapshots_ref, factor_ref, mine_ref, other_ref, *refs):
    *parts, snapshots_buf, factor_buf, sems = refs
    rows, points = snapshots_ref.shape
    half = rows // 2
    snapshots_copy = pltpu.make_async_copy(snapshots_ref, snapshots_buf, sems.at[points // depth])
    snapshots_copy.start()
    copies = []
    for i, start in enumerate(range(0, points, depth)):
        span = pl.ds(start, depth)
        copies.append(pltpu.make_async_copy(factor_ref.at[span, :], factor_buf.at[span, :], sems.at[i]))
        copies[-1].start()
    snapshots_copy.wait()
    width = parts[0].shape[1]
    member = lax.rem(lax.axis_index("tm"), len(parts))
    for k, part in enumerate(parts):
        part[...] = snapshots_buf[:, pl.ds(pl.multiple_of((member ^ k) * width, width), width)]
    value = None
    for i, start in enumerate(range(0, points, depth)):
        copies[i].wait()
        high, low = split(snapshots_buf[:, start : start + depth])
        factor_high, factor_low = split(factor_buf[start : start + depth, :])
        both = dot(jnp.concatenate([high, low], axis=0), factor_high)
        term = both[:rows] + (both[rows:] + dot(high, factor_low))
        value = term if value is None else value + term
    first = lax.rem(lax.axis_index("space"), 2) == 0
    mine_ref[...] = jnp.where(first, value[:half], value[half:])
    other_ref[...] = jnp.where(first, value[half:], value[:half])


def project(snapshots, space_factor, group):
    rows, points = snapshots.shape
    rank = space_factor.shape[1]
    depth = min(512, points)
    half = jax.ShapeDtypeStruct((rows // 2, rank), jnp.float32)
    part = jax.ShapeDtypeStruct((rows, points // group), jnp.float32)
    mine, other, *parts = pl.pallas_call(
        functools.partial(project_kernel, depth),
        in_specs=[HBM, HBM],
        out_specs=[VMEM] * (2 + group),
        out_shape=[half, half] + [part] * group,
        scratch_shapes=[
            pltpu.VMEM((rows, points), jnp.float32),
            pltpu.VMEM((points, rank), jnp.float32),
            pltpu.SemaphoreType.DMA((points // depth + 1,)),
        ],
        compiler_params=params(52),
        cost_estimate=FREE,
    )(snapshots, space_factor)
    return mine, other, parts


def mix_kernel(times, order, index_ref, mine_ref, theirs_ref, high_t_ref, low_t_ref, own_ref):
    total_half, rank = mine_ref.shape
    half = total_half // times
    mine = mine_ref[...].reshape(times, half, rank)
    theirs = theirs_ref[...].reshape(times, half, rank)
    first = index_ref[1] == 0
    low_rows, high_rows = jnp.where(first, mine, theirs), jnp.where(first, theirs, mine)
    projected = jnp.concatenate([low_rows, high_rows], axis=1).reshape(2 * total_half, rank)
    high, low = split(projected)
    cross = dot(high, low, ROWS_BY_ROWS)
    gram = dot(high, high, ROWS_BY_ROWS) + (cross + cross.T)
    row = lax.broadcasted_iota(jnp.int32, (rank, rank), 0)
    column = lax.broadcasted_iota(jnp.int32, (rank, rank), 1)
    total = jnp.sum(projected * projected)
    correlation = gram / total
    correlation_split = split(correlation)
    square = product(correlation_split, correlation_split)
    tail = jnp.where(row == column, 1.6875, 0.0) - 0.5625 * correlation + 0.0625 * square
    mixing = (jnp.where(row == column, 2.25, 0.0) - 2.4375 * correlation) + product(split(square), split(tail))
    mixing_high, mixing_low = split(mixing)

    rows = 2 * half
    group = high_t_ref.shape[1] // rows
    places = [order.index(k) for k in range(group)]
    high = jnp.concatenate([high[i * rows : (i + 1) * rows] for i in places], axis=0)
    low = jnp.concatenate([low[i * rows : (i + 1) * rows] for i in places], axis=0)
    scale = lax.rsqrt(total)
    own = product((high[:rows], low[:rows]), (mixing_high, mixing_low))
    own_ref[...] = own * (scale * math.sqrt(times * rows))
    width = rank // times
    source = ((row // width) ^ index_ref[0]) * width + row % width
    move = jnp.where(source == column, 1.0, 0.0).astype(jnp.bfloat16)
    moved = dot(move, jnp.concatenate([mixing_high, mixing_low], axis=1)).astype(jnp.bfloat16)
    turned = product((moved[:, :rank], moved[:, rank:]), (high, low), COLUMNS_BY_COLUMNS) * scale
    high_t_ref[...], low_t_ref[...] = split(turned)


def mix(index, mine, theirs, times, group, order):
    total_half, rank = mine.shape
    rows = 2 * total_half // times
    factor = jax.ShapeDtypeStruct((rank, group * rows), jnp.bfloat16)
    return pl.pallas_call(
        functools.partial(mix_kernel, times, order),
        in_specs=[SMEM, VMEM, VMEM],
        out_specs=[VMEM] * 3,
        out_shape=[factor, factor, jax.ShapeDtypeStruct((rows, rank), jnp.float32)],
        compiler_params=params(),
        cost_estimate=FREE,
    )(index, mine, theirs)


def load_kernel(group, high_ref, low_ref, *refs):
    parts, blocks = refs[:group], refs[group:]
    columns = jnp.concatenate([part[...] for part in parts], axis=0)
    value = product((high_ref[...], low_ref[...]), split(columns))
    width = value.shape[0] // len(blocks)
    for i, block in enumerate(blocks):
        block[...] = value[i * width : (i + 1) * width]


def load(high, low, parts, blocks):
    rank = high.shape[0]
    columns = parts[0].shape[1]
    return pl.pallas_call(
        functools.partial(load_kernel, len(parts)),
        in_specs=[VMEM] * (2 + len(parts)),
        out_specs=[VMEM] * blocks,
        out_shape=[jax.ShapeDtypeStruct((rank // blocks, columns), jnp.float32)] * blocks,
        compiler_params=params(),
        cost_estimate=FREE,
    )(high, low, *parts)


def join_kernel(group, *refs):
    *terms, out_ref, buf, sems = refs
    width = terms[0].shape[1]
    member = lax.rem(lax.axis_index("tm"), group)
    copies = []
    for k in range(group):
        value = terms[k][...]
        for term in terms[group + k :: group]:
            value = value + term[...]
        buf[k] = value
        span = pl.ds(pl.multiple_of((member ^ k) * width, width), width)
        copies.append(pltpu.make_async_copy(buf.at[k], out_ref.at[:, span], sems.at[k]))
        copies[-1].start()
    for copy in copies:
        copy.wait()


def join(terms, group):
    rows, width = terms[0].shape
    return pl.pallas_call(
        functools.partial(join_kernel, group),
        in_specs=[VMEM] * len(terms),
        out_specs=HBM,
        out_shape=jax.ShapeDtypeStruct((rows, group * width), jnp.float32),
        scratch_shapes=[pltpu.VMEM((group, rows, width), jnp.float32), pltpu.SemaphoreType.DMA((group,))],
        compiler_params=params(),
        cost_estimate=FREE,
    )(*terms)


def swap(value, axis, offset):
    return lax.ppermute(value, axis, [(i, i ^ offset) for i in range(lax.axis_size(axis))])


def on_device(snapshots, space_factor):
    rows, points = snapshots.shape
    rank = space_factor.shape[1]
    times, spaces = lax.axis_size("tm"), lax.axis_size("space")
    group = min(4, times)
    index = lax.axis_index("tm")
    core = lax.axis_index("space") % 2

    mine, other, parts = project(snapshots, space_factor, group)
    parts = [part if k == 0 else swap(part, "tm", k) for k, part in enumerate(parts)]

    terms = [mine] + [swap(other if k % 2 else mine, "space", k) for k in range(1, spaces)]
    while len(terms) > 1:
        terms = [a + b for a, b in zip(terms[::2], terms[1::2])]
    mine = terms[0]

    near = group // 2
    order = [k for k in range(times) if k % group < near]
    mine = jnp.concatenate([mine] + [swap(mine, "tm", k) for k in order[1:]], axis=0)
    mine, parts[2] = lax.optimization_barrier((mine, parts[2]))
    for offset in range(near, group, near):
        mine = jnp.concatenate([mine, swap(mine, "tm", offset)], axis=0)
        order = order + [k ^ offset for k in order]
    mine, parts[3] = lax.optimization_barrier((mine, parts[3]))
    theirs, parts[1] = lax.optimization_barrier((swap(mine, "space", 1), parts[1]))
    high_t, low_t, own = mix(jnp.stack([index, core]), mine, theirs, times, group, order)

    blocks = list(load(high_t, low_t, parts, times))
    terms = [blocks[0]] + [None] * (times - 1)
    for k in [*range(group, times), *range(1, group)]:
        if k == group - 1:
            blocks[k], terms[1] = lax.optimization_barrier((blocks[k], terms[1]))
        terms[k] = swap(blocks[k], "tm", k)
    return own, join(terms, group)


def solution(mesh):
    return jax.shard_map(
        on_device,
        mesh=mesh,
        in_specs=(P("tm", "space"), P("space", None)),
        out_specs=(P("tm", None), P("tm", "space")),
        check_vma=False,
    )
```

```python
import functools
import math

import jax
import jax.numpy as jnp
from jax import lax
from jax.experimental import pallas as pl
from jax.experimental.pallas import tpu as pltpu
from jax.sharding import PartitionSpec as P

MIB = 1024 * 1024
HBM = pl.BlockSpec(memory_space=pltpu.HBM)
SMEM = pl.BlockSpec(memory_space=pltpu.SMEM)
VMEM = pl.BlockSpec(memory_space=pltpu.VMEM)
FREE = pl.CostEstimate(flops=0, bytes_accessed=0, transcendentals=0)
ROWS_BY_ROWS = (((0,), (0,)), ((), ()))
ROWS_BY_COLUMNS = (((1,), (0,)), ((), ()))
COLUMNS_BY_COLUMNS = (((1,), (1,)), ((), ()))


def params(mib=48):
    return pltpu.CompilerParams(vmem_limit_bytes=mib * MIB)


def split(value):
    high = value.astype(jnp.bfloat16)
    return high, (value - high.astype(jnp.float32)).astype(jnp.bfloat16)


def dot(left, right, dims=ROWS_BY_COLUMNS):
    return lax.dot_general(left, right, dims, preferred_element_type=jnp.float32)


def product(left, right, dims=ROWS_BY_COLUMNS):
    (left_high, left_low), (right_high, right_low) = left, right
    return dot(left_high, right_high, dims) + (
        dot(left_high, right_low, dims) + dot(left_low, right_high, dims)
    )


def project_kernel(depth, snapshots_ref, factor_ref, mine_ref, other_ref, *refs):
    *parts, snapshots_buf, factor_buf, sems = refs
    rows, points = snapshots_ref.shape
    half = rows // 2
    snapshots_copy = pltpu.make_async_copy(snapshots_ref, snapshots_buf, sems.at[points // depth])
    snapshots_copy.start()
    copies = []
    for i, start in enumerate(range(0, points, depth)):
        span = pl.ds(start, depth)
        copies.append(pltpu.make_async_copy(factor_ref.at[span, :], factor_buf.at[span, :], sems.at[i]))
        copies[-1].start()
    snapshots_copy.wait()
    width = parts[0].shape[1]
    member = lax.rem(lax.axis_index("tm"), len(parts))
    for k, part in enumerate(parts):
        part[...] = snapshots_buf[:, pl.ds(pl.multiple_of((member ^ k) * width, width), width)]
    value = None
    for i, start in enumerate(range(0, points, depth)):
        copies[i].wait()
        high, low = split(snapshots_buf[:, start : start + depth])
        factor_high, factor_low = split(factor_buf[start : start + depth, :])
        both = dot(jnp.concatenate([high, low], axis=0), factor_high)
        term = both[:rows] + (both[rows:] + dot(high, factor_low))
        value = term if value is None else value + term
    first = lax.rem(lax.axis_index("space"), 2) == 0
    mine_ref[...] = jnp.where(first, value[:half], value[half:])
    other_ref[...] = jnp.where(first, value[half:], value[:half])


def project(snapshots, space_factor, group):
    rows, points = snapshots.shape
    rank = space_factor.shape[1]
    depth = min(512, points)
    half = jax.ShapeDtypeStruct((rows // 2, rank), jnp.float32)
    part = jax.ShapeDtypeStruct((rows, points // group), jnp.float32)
    mine, other, *parts = pl.pallas_call(
        functools.partial(project_kernel, depth),
        in_specs=[HBM, HBM],
        out_specs=[VMEM] * (2 + group),
        out_shape=[half, half] + [part] * group,
        scratch_shapes=[
            pltpu.VMEM((rows, points), jnp.float32),
            pltpu.VMEM((points, rank), jnp.float32),
            pltpu.SemaphoreType.DMA((points // depth + 1,)),
        ],
        compiler_params=params(52),
        cost_estimate=FREE,
    )(snapshots, space_factor)
    return mine, other, parts


def mix_kernel(times, order, index_ref, *refs):
    *halves, high_t_ref, low_t_ref, own_ref = refs
    rank = own_ref.shape[1]
    mine, theirs = [jnp.concatenate([ref[...] for ref in halves[i::2]], axis=0) for i in range(2)]
    total_half = mine.shape[0]
    half = total_half // times
    mine = mine.reshape(times, half, rank)
    theirs = theirs.reshape(times, half, rank)
    first = index_ref[1] == 0
    low_rows, high_rows = jnp.where(first, mine, theirs), jnp.where(first, theirs, mine)
    projected = jnp.concatenate([low_rows, high_rows], axis=1).reshape(2 * total_half, rank)
    high, low = split(projected)
    cross = dot(high, low, ROWS_BY_ROWS)
    gram = dot(high, high, ROWS_BY_ROWS) + (cross + cross.T)
    row = lax.broadcasted_iota(jnp.int32, (rank, rank), 0)
    column = lax.broadcasted_iota(jnp.int32, (rank, rank), 1)
    total = jnp.sum(projected * projected)
    correlation = gram / total
    correlation_split = split(correlation)
    square = product(correlation_split, correlation_split)
    tail = jnp.where(row == column, 1.6875, 0.0) - 0.5625 * correlation + 0.0625 * square
    mixing = (jnp.where(row == column, 2.25, 0.0) - 2.4375 * correlation) + product(split(square), split(tail))
    mixing_high, mixing_low = split(mixing)

    rows = 2 * half
    group = high_t_ref.shape[1] // rows
    places = [order.index(k) for k in range(group)]
    high = jnp.concatenate([high[i * rows : (i + 1) * rows] for i in places], axis=0)
    low = jnp.concatenate([low[i * rows : (i + 1) * rows] for i in places], axis=0)
    scale = lax.rsqrt(total)
    own = product((high[:rows], low[:rows]), (mixing_high, mixing_low))
    own_ref[...] = own * (scale * math.sqrt(times * rows))
    width = rank // times
    source = ((row // width) ^ index_ref[0]) * width + row % width
    move = jnp.where(source == column, 1.0, 0.0).astype(jnp.bfloat16)
    moved = dot(move, jnp.concatenate([mixing_high, mixing_low], axis=1)).astype(jnp.bfloat16)
    turned = product((moved[:, :rank], moved[:, rank:]), (high, low), COLUMNS_BY_COLUMNS) * scale
    high_t_ref[...], low_t_ref[...] = split(turned)


def mix(index, pairs, times, group, order):
    halves = [half for pair in pairs for half in pair]
    rank = halves[0].shape[1]
    rows = sum(half.shape[0] for half in halves) // times
    factor = jax.ShapeDtypeStruct((rank, group * rows), jnp.bfloat16)
    return pl.pallas_call(
        functools.partial(mix_kernel, times, order),
        in_specs=[SMEM] + [VMEM] * len(halves),
        out_specs=[VMEM] * 3,
        out_shape=[factor, factor, jax.ShapeDtypeStruct((rows, rank), jnp.float32)],
        compiler_params=params(),
        cost_estimate=FREE,
    )(index, *halves)


def load_kernel(group, high_ref, low_ref, *refs):
    parts, blocks = refs[:group], refs[group:]
    columns = jnp.concatenate([part[...] for part in parts], axis=0)
    value = product((high_ref[...], low_ref[...]), split(columns))
    width = value.shape[0] // len(blocks)
    for i, block in enumerate(blocks):
        block[...] = value[i * width : (i + 1) * width]


def load(high, low, parts, blocks):
    rank = high.shape[0]
    columns = parts[0].shape[1]
    return pl.pallas_call(
        functools.partial(load_kernel, len(parts)),
        in_specs=[VMEM] * (2 + len(parts)),
        out_specs=[VMEM] * blocks,
        out_shape=[jax.ShapeDtypeStruct((rank // blocks, columns), jnp.float32)] * blocks,
        compiler_params=params(),
        cost_estimate=FREE,
    )(high, low, *parts)


def join_kernel(group, *refs):
    *terms, out_ref, buf, sems = refs
    width = terms[0].shape[1]
    member = lax.rem(lax.axis_index("tm"), group)
    copies = []
    for k in range(group):
        value = terms[k][...]
        for term in terms[group + k :: group]:
            value = value + term[...]
        buf[k] = value
        span = pl.ds(pl.multiple_of((member ^ k) * width, width), width)
        copies.append(pltpu.make_async_copy(buf.at[k], out_ref.at[:, span], sems.at[k]))
        copies[-1].start()
    for copy in copies:
        copy.wait()


def join(terms, group):
    rows, width = terms[0].shape
    return pl.pallas_call(
        functools.partial(join_kernel, group),
        in_specs=[VMEM] * len(terms),
        out_specs=HBM,
        out_shape=jax.ShapeDtypeStruct((rows, group * width), jnp.float32),
        scratch_shapes=[pltpu.VMEM((group, rows, width), jnp.float32), pltpu.SemaphoreType.DMA((group,))],
        compiler_params=params(),
        cost_estimate=FREE,
    )(*terms)


def swap(value, axis, offset):
    return lax.ppermute(value, axis, [(i, i ^ offset) for i in range(lax.axis_size(axis))])


def on_device(snapshots, space_factor):
    rows, points = snapshots.shape
    rank = space_factor.shape[1]
    times, spaces = lax.axis_size("tm"), lax.axis_size("space")
    group = min(4, times)
    index = lax.axis_index("tm")
    core = lax.axis_index("space") % 2

    mine, other, parts = project(snapshots, space_factor, group)
    parts = [part if k == 0 else swap(part, "tm", k) for k, part in enumerate(parts)]

    terms = [mine] + [swap(other if k % 2 else mine, "space", k) for k in range(1, spaces)]
    while len(terms) > 1:
        terms = [a + b for a, b in zip(terms[::2], terms[1::2])]
    mine = terms[0]

    near = group // 2
    order = [k for k in range(times) if k % group < near]
    mine = jnp.concatenate([mine] + [swap(mine, "tm", k) for k in order[1:]], axis=0)
    mine, parts[2] = lax.optimization_barrier((mine, parts[2]))
    rest = swap(mine, "tm", near)
    pairs = [(mine, swap(mine, "space", 1))]
    rest, parts[1] = lax.optimization_barrier((rest, parts[1]))
    pairs.append((rest, swap(rest, "space", 1)))
    order = order + [k ^ near for k in order]
    high_t, low_t, own = mix(jnp.stack([index, core]), pairs, times, group, order)

    blocks = list(load(high_t, low_t, parts, times))
    terms = [blocks[0]] + [None] * (times - 1)
    for k in [*range(group, times), *range(1, group)]:
        if k == group - 1:
            blocks[k], terms[1] = lax.optimization_barrier((blocks[k], terms[1]))
        terms[k] = swap(blocks[k], "tm", k)
    return own, join(terms, group)


def solution(mesh):
    return jax.shard_map(
        on_device,
        mesh=mesh,
        in_specs=(P("tm", "space"), P("space", None)),
        out_specs=(P("tm", None), P("tm", "space")),
        check_vma=False,
    )
```

```python
import functools
import math

import jax
import jax.numpy as jnp
from jax import lax
from jax.experimental import pallas as pl
from jax.experimental.pallas import tpu as pltpu
from jax.sharding import PartitionSpec as P

MIB = 1024 * 1024
HBM = pl.BlockSpec(memory_space=pltpu.HBM)
SMEM = pl.BlockSpec(memory_space=pltpu.SMEM)
VMEM = pl.BlockSpec(memory_space=pltpu.VMEM)
FREE = pl.CostEstimate(flops=0, bytes_accessed=0, transcendentals=0)
ROWS_BY_ROWS = (((0,), (0,)), ((), ()))
ROWS_BY_COLUMNS = (((1,), (0,)), ((), ()))
COLUMNS_BY_COLUMNS = (((1,), (1,)), ((), ()))


def params(mib=48):
    return pltpu.CompilerParams(vmem_limit_bytes=mib * MIB)


def split(value):
    high = value.astype(jnp.bfloat16)
    return high, (value - high.astype(jnp.float32)).astype(jnp.bfloat16)


def dot(left, right, dims=ROWS_BY_COLUMNS):
    return lax.dot_general(left, right, dims, preferred_element_type=jnp.float32)


def product(left, right, dims=ROWS_BY_COLUMNS):
    (left_high, left_low), (right_high, right_low) = left, right
    return dot(left_high, right_high, dims) + (
        dot(left_high, right_low, dims) + dot(left_low, right_high, dims)
    )


def project_kernel(depth, snapshots_ref, factor_ref, mine_ref, other_ref, *refs):
    *parts, snapshots_buf, factor_buf, sems = refs
    rows, points = snapshots_ref.shape
    half = rows // 2
    snapshots_copy = pltpu.make_async_copy(snapshots_ref, snapshots_buf, sems.at[points // depth])
    snapshots_copy.start()
    copies = []
    for i, start in enumerate(range(0, points, depth)):
        span = pl.ds(start, depth)
        copies.append(pltpu.make_async_copy(factor_ref.at[span, :], factor_buf.at[span, :], sems.at[i]))
        copies[-1].start()
    snapshots_copy.wait()
    width = parts[0].shape[1]
    member = lax.rem(lax.axis_index("tm"), len(parts))
    for k, part in enumerate(parts):
        part[...] = snapshots_buf[:, pl.ds(pl.multiple_of((member ^ k) * width, width), width)]
    value = None
    for i, start in enumerate(range(0, points, depth)):
        copies[i].wait()
        high, low = split(snapshots_buf[:, start : start + depth])
        factor_high, factor_low = split(factor_buf[start : start + depth, :])
        both = dot(jnp.concatenate([high, low], axis=0), factor_high)
        term = both[:rows] + (both[rows:] + dot(high, factor_low))
        value = term if value is None else value + term
    first = lax.rem(lax.axis_index("space"), 2) == 0
    mine_ref[...] = jnp.where(first, value[:half], value[half:])
    other_ref[...] = jnp.where(first, value[half:], value[:half])


def project(snapshots, space_factor, group):
    rows, points = snapshots.shape
    rank = space_factor.shape[1]
    depth = min(512, points)
    half = jax.ShapeDtypeStruct((rows // 2, rank), jnp.float32)
    part = jax.ShapeDtypeStruct((rows, points // group), jnp.float32)
    mine, other, *parts = pl.pallas_call(
        functools.partial(project_kernel, depth),
        in_specs=[HBM, HBM],
        out_specs=[VMEM] * (2 + group),
        out_shape=[half, half] + [part] * group,
        scratch_shapes=[
            pltpu.VMEM((rows, points), jnp.float32),
            pltpu.VMEM((points, rank), jnp.float32),
            pltpu.SemaphoreType.DMA((points // depth + 1,)),
        ],
        compiler_params=params(52),
        cost_estimate=FREE,
    )(snapshots, space_factor)
    return mine, other, parts


def mix_kernel(times, order, index_ref, *refs):
    *halves, high_t_ref, low_t_ref, own_ref = refs
    rank = own_ref.shape[1]
    mine, theirs = [jnp.concatenate([ref[...] for ref in halves[i::2]], axis=0) for i in range(2)]
    total_half = mine.shape[0]
    half = total_half // times
    mine = mine.reshape(times, half, rank)
    theirs = theirs.reshape(times, half, rank)
    first = index_ref[1] == 0
    low_rows, high_rows = jnp.where(first, mine, theirs), jnp.where(first, theirs, mine)
    projected = jnp.concatenate([low_rows, high_rows], axis=1).reshape(2 * total_half, rank)
    high, low = split(projected)
    cross = dot(high, low, ROWS_BY_ROWS)
    gram = dot(high, high, ROWS_BY_ROWS) + (cross + cross.T)
    row = lax.broadcasted_iota(jnp.int32, (rank, rank), 0)
    column = lax.broadcasted_iota(jnp.int32, (rank, rank), 1)
    total = jnp.sum(projected * projected)
    correlation = gram / total
    correlation_split = split(correlation)
    square = product(correlation_split, correlation_split)
    tail = jnp.where(row == column, 1.6875, 0.0) - 0.5625 * correlation + 0.0625 * square
    mixing = (jnp.where(row == column, 2.25, 0.0) - 2.4375 * correlation) + product(split(square), split(tail))
    mixing_high, mixing_low = split(mixing)

    rows = 2 * half
    group = high_t_ref.shape[1] // rows
    places = [order.index(k) for k in range(group)]
    high = jnp.concatenate([high[i * rows : (i + 1) * rows] for i in places], axis=0)
    low = jnp.concatenate([low[i * rows : (i + 1) * rows] for i in places], axis=0)
    scale = lax.rsqrt(total)
    own = product((high[:rows], low[:rows]), (mixing_high, mixing_low))
    own_ref[...] = own * (scale * math.sqrt(times * rows))
    width = rank // times
    source = ((row // width) ^ index_ref[0]) * width + row % width
    move = jnp.where(source == column, 1.0, 0.0).astype(jnp.bfloat16)
    moved = dot(move, jnp.concatenate([mixing_high, mixing_low], axis=1)).astype(jnp.bfloat16)
    turned = product((moved[:, :rank], moved[:, rank:]), (high, low), COLUMNS_BY_COLUMNS) * scale
    high_t_ref[...], low_t_ref[...] = split(turned)


def mix(index, pairs, times, group, order):
    halves = [half for pair in pairs for half in pair]
    rank = halves[0].shape[1]
    rows = sum(half.shape[0] for half in halves) // times
    factor = jax.ShapeDtypeStruct((rank, group * rows), jnp.bfloat16)
    return pl.pallas_call(
        functools.partial(mix_kernel, times, order),
        in_specs=[SMEM] + [VMEM] * len(halves),
        out_specs=[VMEM] * 3,
        out_shape=[factor, factor, jax.ShapeDtypeStruct((rows, rank), jnp.float32)],
        compiler_params=params(),
        cost_estimate=FREE,
    )(index, *halves)


def load_kernel(group, high_ref, low_ref, *refs):
    parts, blocks = refs[:group], refs[group:]
    columns = jnp.concatenate([part[...] for part in parts], axis=0)
    value = product((high_ref[...], low_ref[...]), split(columns))
    width = value.shape[0] // len(blocks)
    for i, block in enumerate(blocks):
        block[...] = value[i * width : (i + 1) * width]


def load(high, low, parts, blocks):
    rank = high.shape[0]
    columns = parts[0].shape[1]
    return pl.pallas_call(
        functools.partial(load_kernel, len(parts)),
        in_specs=[VMEM] * (2 + len(parts)),
        out_specs=[VMEM] * blocks,
        out_shape=[jax.ShapeDtypeStruct((rank // blocks, columns), jnp.float32)] * blocks,
        compiler_params=params(),
        cost_estimate=FREE,
    )(high, low, *parts)


def join_kernel(group, sequence, *refs):
    *terms, out_ref, buf, sems = refs
    terms = [terms[sequence.index(k)] for k in range(len(terms))]
    width = terms[0].shape[1]
    member = lax.rem(lax.axis_index("tm"), group)
    copies = []
    for k in range(group):
        value = terms[k][...]
        for term in terms[group + k :: group]:
            value = value + term[...]
        buf[k] = value
        span = pl.ds(pl.multiple_of((member ^ k) * width, width), width)
        copies.append(pltpu.make_async_copy(buf.at[k], out_ref.at[:, span], sems.at[k]))
        copies[-1].start()
    for copy in copies:
        copy.wait()


def join(terms, group, sequence):
    rows, width = terms[0].shape
    return pl.pallas_call(
        functools.partial(join_kernel, group, sequence),
        in_specs=[VMEM] * len(terms),
        out_specs=HBM,
        out_shape=jax.ShapeDtypeStruct((rows, group * width), jnp.float32),
        scratch_shapes=[pltpu.VMEM((group, rows, width), jnp.float32), pltpu.SemaphoreType.DMA((group,))],
        compiler_params=params(),
        cost_estimate=FREE,
    )(*[terms[k] for k in sequence])


def swap(value, axis, offset):
    return lax.ppermute(value, axis, [(i, i ^ offset) for i in range(lax.axis_size(axis))])


def on_device(snapshots, space_factor):
    rows, points = snapshots.shape
    rank = space_factor.shape[1]
    times, spaces = lax.axis_size("tm"), lax.axis_size("space")
    group = min(4, times)
    index = lax.axis_index("tm")
    core = lax.axis_index("space") % 2

    mine, other, parts = project(snapshots, space_factor, group)
    parts = [part if k == 0 else swap(part, "tm", k) for k, part in enumerate(parts)]

    terms = [mine] + [swap(other if k % 2 else mine, "space", k) for k in range(1, spaces)]
    while len(terms) > 1:
        terms = [a + b for a, b in zip(terms[::2], terms[1::2])]
    mine = terms[0]

    near = group // 2
    order = [k for k in range(times) if k % group < near]
    mine = jnp.concatenate([mine] + [swap(mine, "tm", k) for k in order[1:]], axis=0)
    mine, *parts[1:3] = lax.optimization_barrier((mine, *parts[1:3]))
    rest = swap(mine, "tm", near)
    pairs = [(mine, swap(mine, "space", 1))]
    pairs.append((rest, swap(rest, "space", 1)))
    order = order + [k ^ near for k in order]
    high_t, low_t, own = mix(jnp.stack([index, core]), pairs, times, group, order)

    blocks = list(load(high_t, low_t, parts, times))
    terms = [blocks[0]] + [None] * (times - 1)
    near, far = list(range(1, group)), list(range(group, times))
    sequence = [*far[:2], *near[:2], *far[2:], *near[2:], 0]
    for k in sequence[:-1]:
        if k == near[-1]:
            blocks[k], terms[1] = lax.optimization_barrier((blocks[k], terms[1]))
        terms[k] = swap(blocks[k], "tm", k)
    return own, join(terms, group, sequence)


def solution(mesh):
    return jax.shard_map(
        on_device,
        mesh=mesh,
        in_specs=(P("tm", "space"), P("space", None)),
        out_specs=(P("tm", None), P("tm", "space")),
        check_vma=False,
    )
```

```python
import functools
import math

import jax
import jax.numpy as jnp
from jax import lax
from jax.experimental import pallas as pl
from jax.experimental.pallas import tpu as pltpu
from jax.sharding import PartitionSpec as P

MIB = 1024 * 1024
HBM = pl.BlockSpec(memory_space=pltpu.HBM)
SMEM = pl.BlockSpec(memory_space=pltpu.SMEM)
VMEM = pl.BlockSpec(memory_space=pltpu.VMEM)
FREE = pl.CostEstimate(flops=0, bytes_accessed=0, transcendentals=0)
ROWS_BY_ROWS = (((0,), (0,)), ((), ()))
ROWS_BY_COLUMNS = (((1,), (0,)), ((), ()))
COLUMNS_BY_COLUMNS = (((1,), (1,)), ((), ()))


def params(mib=48):
    return pltpu.CompilerParams(vmem_limit_bytes=mib * MIB)


def split(value):
    high = value.astype(jnp.bfloat16)
    return high, (value - high.astype(jnp.float32)).astype(jnp.bfloat16)


def dot(left, right, dims=ROWS_BY_COLUMNS):
    return lax.dot_general(left, right, dims, preferred_element_type=jnp.float32)


def product(left, right, dims=ROWS_BY_COLUMNS):
    (left_high, left_low), (right_high, right_low) = left, right
    return dot(left_high, right_high, dims) + (
        dot(left_high, right_low, dims) + dot(left_low, right_high, dims)
    )


def project_kernel(depth, snapshots_ref, factor_ref, mine_ref, other_ref, *refs):
    *parts, snapshots_buf, factor_buf, sems = refs
    rows, points = snapshots_ref.shape
    half = rows // 2
    snapshots_copy = pltpu.make_async_copy(snapshots_ref, snapshots_buf, sems.at[points // depth])
    snapshots_copy.start()
    copies = []
    for i, start in enumerate(range(0, points, depth)):
        span = pl.ds(start, depth)
        copies.append(pltpu.make_async_copy(factor_ref.at[span, :], factor_buf.at[span, :], sems.at[i]))
        copies[-1].start()
    snapshots_copy.wait()
    width = parts[0].shape[1]
    member = lax.rem(lax.axis_index("tm"), len(parts))
    for k, part in enumerate(parts):
        part[...] = snapshots_buf[:, pl.ds(pl.multiple_of((member ^ k) * width, width), width)]
    value = None
    for i, start in enumerate(range(0, points, depth)):
        copies[i].wait()
        high, low = split(snapshots_buf[:, start : start + depth])
        factor_high, factor_low = split(factor_buf[start : start + depth, :])
        both = dot(jnp.concatenate([high, low], axis=0), factor_high)
        term = both[:rows] + (both[rows:] + dot(high, factor_low))
        value = term if value is None else value + term
    first = lax.rem(lax.axis_index("space"), 2) == 0
    mine_ref[...] = jnp.where(first, value[:half], value[half:])
    other_ref[...] = jnp.where(first, value[half:], value[:half])


def project(snapshots, space_factor, group):
    rows, points = snapshots.shape
    rank = space_factor.shape[1]
    depth = min(512, points)
    half = jax.ShapeDtypeStruct((rows // 2, rank), jnp.float32)
    part = jax.ShapeDtypeStruct((rows, points // group), jnp.float32)
    mine, other, *parts = pl.pallas_call(
        functools.partial(project_kernel, depth),
        in_specs=[HBM, HBM],
        out_specs=[VMEM] * (2 + group),
        out_shape=[half, half] + [part] * group,
        scratch_shapes=[
            pltpu.VMEM((rows, points), jnp.float32),
            pltpu.VMEM((points, rank), jnp.float32),
            pltpu.SemaphoreType.DMA((points // depth + 1,)),
        ],
        compiler_params=params(52),
        cost_estimate=FREE,
    )(snapshots, space_factor)
    return mine, other, parts


def mix_kernel(times, order, index_ref, *refs):
    *halves, high_t_ref, low_t_ref, own_ref = refs
    rank = own_ref.shape[1]
    mine, theirs = [jnp.concatenate([ref[...] for ref in halves[i::2]], axis=0) for i in range(2)]
    total_half = mine.shape[0]
    half = total_half // times
    mine = mine.reshape(times, half, rank)
    theirs = theirs.reshape(times, half, rank)
    first = index_ref[1] == 0
    low_rows, high_rows = jnp.where(first, mine, theirs), jnp.where(first, theirs, mine)
    projected = jnp.concatenate([low_rows, high_rows], axis=1).reshape(2 * total_half, rank)
    high, low = split(projected)
    cross = dot(high, low, ROWS_BY_ROWS)
    gram = dot(high, high, ROWS_BY_ROWS) + (cross + cross.T)
    row = lax.broadcasted_iota(jnp.int32, (rank, rank), 0)
    column = lax.broadcasted_iota(jnp.int32, (rank, rank), 1)
    total = jnp.sum(projected * projected)
    correlation = gram / total
    correlation_split = split(correlation)
    square = product(correlation_split, correlation_split)
    tail = jnp.where(row == column, 1.6875, 0.0) - 0.5625 * correlation + 0.0625 * square
    mixing = (jnp.where(row == column, 2.25, 0.0) - 2.4375 * correlation) + product(split(square), split(tail))
    mixing_high, mixing_low = split(mixing)

    rows = 2 * half
    group = high_t_ref.shape[1] // rows
    places = [order.index(k) for k in range(group)]
    high = jnp.concatenate([high[i * rows : (i + 1) * rows] for i in places], axis=0)
    low = jnp.concatenate([low[i * rows : (i + 1) * rows] for i in places], axis=0)
    scale = lax.rsqrt(total)
    own = product((high[:rows], low[:rows]), (mixing_high, mixing_low))
    own_ref[...] = own * (scale * math.sqrt(times * rows))
    width = rank // times
    source = ((row // width) ^ index_ref[0]) * width + row % width
    move = jnp.where(source == column, 1.0, 0.0).astype(jnp.bfloat16)
    moved = dot(move, jnp.concatenate([mixing_high, mixing_low], axis=1)).astype(jnp.bfloat16)
    turned = product((moved[:, :rank], moved[:, rank:]), (high, low), COLUMNS_BY_COLUMNS) * scale
    high_t_ref[...], low_t_ref[...] = split(turned)


def mix(index, pairs, times, group, order):
    halves = [half for pair in pairs for half in pair]
    rank = halves[0].shape[1]
    rows = sum(half.shape[0] for half in halves) // times
    factor = jax.ShapeDtypeStruct((rank, group * rows), jnp.bfloat16)
    return pl.pallas_call(
        functools.partial(mix_kernel, times, order),
        in_specs=[SMEM] + [VMEM] * len(halves),
        out_specs=[VMEM] * 3,
        out_shape=[factor, factor, jax.ShapeDtypeStruct((rows, rank), jnp.float32)],
        compiler_params=params(),
        cost_estimate=FREE,
    )(index, *halves)


def load_kernel(group, high_ref, low_ref, *refs):
    parts, blocks = refs[:group], refs[group:]
    columns = jnp.concatenate([part[...] for part in parts], axis=0)
    value = product((high_ref[...], low_ref[...]), split(columns))
    width = value.shape[0] // len(blocks)
    for i, block in enumerate(blocks):
        block[...] = value[i * width : (i + 1) * width]


def load(high, low, parts, blocks):
    rank = high.shape[0]
    columns = parts[0].shape[1]
    return pl.pallas_call(
        functools.partial(load_kernel, len(parts)),
        in_specs=[VMEM] * (2 + len(parts)),
        out_specs=[VMEM] * blocks,
        out_shape=[jax.ShapeDtypeStruct((rank // blocks, columns), jnp.float32)] * blocks,
        compiler_params=params(),
        cost_estimate=FREE,
    )(high, low, *parts)


def join_kernel(group, sequence, own_ref, *refs):
    *terms, own_out_ref, out_ref, buf, sems = refs
    terms = [terms[sequence.index(k)] for k in range(len(terms))]
    width = terms[0].shape[1]
    member = lax.rem(lax.axis_index("tm"), group)
    copies = [pltpu.make_async_copy(own_ref, own_out_ref, sems.at[group])]
    copies[0].start()
    for k in range(group):
        value = terms[k][...]
        for term in terms[group + k :: group]:
            value = value + term[...]
        buf[k] = value
        span = pl.ds(pl.multiple_of((member ^ k) * width, width), width)
        copies.append(pltpu.make_async_copy(buf.at[k], out_ref.at[:, span], sems.at[k]))
        copies[-1].start()
    for copy in copies:
        copy.wait()


def join(own, terms, group, sequence):
    rows, width = terms[0].shape
    return pl.pallas_call(
        functools.partial(join_kernel, group, sequence),
        in_specs=[VMEM] * (1 + len(terms)),
        out_specs=[HBM] * 2,
        out_shape=[
            jax.ShapeDtypeStruct(own.shape, jnp.float32),
            jax.ShapeDtypeStruct((rows, group * width), jnp.float32),
        ],
        scratch_shapes=[pltpu.VMEM((group, rows, width), jnp.float32), pltpu.SemaphoreType.DMA((group + 1,))],
        compiler_params=params(),
        cost_estimate=FREE,
    )(own, *[terms[k] for k in sequence])


def swap(value, axis, offset):
    return lax.ppermute(value, axis, [(i, i ^ offset) for i in range(lax.axis_size(axis))])


def on_device(snapshots, space_factor):
    rows, points = snapshots.shape
    rank = space_factor.shape[1]
    times, spaces = lax.axis_size("tm"), lax.axis_size("space")
    group = min(4, times)
    index = lax.axis_index("tm")
    core = lax.axis_index("space") % 2

    mine, other, parts = project(snapshots, space_factor, group)
    parts = [part if k == 0 else swap(part, "tm", k) for k, part in enumerate(parts)]

    terms = [mine] + [swap(other if k % 2 else mine, "space", k) for k in range(1, spaces)]
    while len(terms) > 1:
        terms = [a + b for a, b in zip(terms[::2], terms[1::2])]
    mine = terms[0]

    near = group // 2
    order = [k for k in range(times) if k % group < near]
    mine = jnp.concatenate([mine] + [swap(mine, "tm", k) for k in order[1:]], axis=0)
    mine, *parts[1:3] = lax.optimization_barrier((mine, *parts[1:3]))
    rest = swap(mine, "tm", near)
    pairs = [(mine, swap(mine, "space", 1))]
    pairs.append((rest, swap(rest, "space", 1)))
    order = order + [k ^ near for k in order]
    high_t, low_t, own = mix(jnp.stack([index, core]), pairs, times, group, order)

    blocks = list(load(high_t, low_t, parts, times))
    terms = [blocks[0]] + [None] * (times - 1)
    near, far = list(range(1, group)), list(range(group, times))
    sequence = [*far[:2], *near[:2], *far[2:], *near[2:], 0]
    for k in sequence[:-1]:
        if k == near[-1]:
            blocks[k], terms[1] = lax.optimization_barrier((blocks[k], terms[1]))
        terms[k] = swap(blocks[k], "tm", k)
    return tuple(join(own, terms, group, sequence))


def solution(mesh):
    return jax.shard_map(
        on_device,
        mesh=mesh,
        in_specs=(P("tm", "space"), P("space", None)),
        out_specs=(P("tm", None), P("tm", "space")),
        check_vma=False,
    )
```

```python
import functools
import math

import jax
import jax.numpy as jnp
from jax import lax
from jax.experimental import pallas as pl
from jax.experimental.pallas import tpu as pltpu
from jax.sharding import PartitionSpec as P

MIB = 1024 * 1024
HBM = pl.BlockSpec(memory_space=pltpu.HBM)
SMEM = pl.BlockSpec(memory_space=pltpu.SMEM)
VMEM = pl.BlockSpec(memory_space=pltpu.VMEM)
FREE = pl.CostEstimate(flops=0, bytes_accessed=0, transcendentals=0)
ROWS_BY_ROWS = (((0,), (0,)), ((), ()))
ROWS_BY_COLUMNS = (((1,), (0,)), ((), ()))
COLUMNS_BY_COLUMNS = (((1,), (1,)), ((), ()))


def params(mib=48):
    return pltpu.CompilerParams(vmem_limit_bytes=mib * MIB)


def split(value):
    high = value.astype(jnp.bfloat16)
    return high, (value - high.astype(jnp.float32)).astype(jnp.bfloat16)


def dot(left, right, dims=ROWS_BY_COLUMNS):
    return lax.dot_general(left, right, dims, preferred_element_type=jnp.float32)


def product(left, right, dims=ROWS_BY_COLUMNS):
    (left_high, left_low), (right_high, right_low) = left, right
    return dot(left_high, right_high, dims) + (
        dot(left_high, right_low, dims) + dot(left_low, right_high, dims)
    )


def project_kernel(depth, snapshots_ref, factor_ref, partial_ref, *refs):
    *parts, snapshots_buf, factor_buf, sems = refs
    rows, points = snapshots_ref.shape
    snapshots_copy = pltpu.make_async_copy(snapshots_ref, snapshots_buf, sems.at[points // depth])
    snapshots_copy.start()
    copies = []
    for i, start in enumerate(range(0, points, depth)):
        span = pl.ds(start, depth)
        copies.append(pltpu.make_async_copy(factor_ref.at[span, :], factor_buf.at[span, :], sems.at[i]))
        copies[-1].start()
    snapshots_copy.wait()
    width = parts[0].shape[1]
    member = lax.rem(lax.axis_index("tm"), len(parts))
    for k, part in enumerate(parts):
        part[...] = snapshots_buf[:, pl.ds(pl.multiple_of((member ^ k) * width, width), width)]
    value = None
    for i, start in enumerate(range(0, points, depth)):
        copies[i].wait()
        high, low = split(snapshots_buf[:, start : start + depth])
        factor_high, factor_low = split(factor_buf[start : start + depth, :])
        both = dot(jnp.concatenate([high, low], axis=0), factor_high)
        term = both[:rows] + (both[rows:] + dot(high, factor_low))
        value = term if value is None else value + term
    partial_ref[...] = value


def project(snapshots, space_factor, group):
    rows, points = snapshots.shape
    rank = space_factor.shape[1]
    depth = min(512, points)
    part = jax.ShapeDtypeStruct((rows, points // group), jnp.float32)
    partial, *parts = pl.pallas_call(
        functools.partial(project_kernel, depth),
        in_specs=[HBM, HBM],
        out_specs=[VMEM] * (1 + group),
        out_shape=[jax.ShapeDtypeStruct((rows, rank), jnp.float32)] + [part] * group,
        scratch_shapes=[
            pltpu.VMEM((rows, points), jnp.float32),
            pltpu.VMEM((points, rank), jnp.float32),
            pltpu.SemaphoreType.DMA((points // depth + 1,)),
        ],
        compiler_params=params(52),
        cost_estimate=FREE,
    )(snapshots, space_factor)
    return partial, parts


def mix_kernel(times, order, index_ref, *refs):
    *halves, high_t_ref, low_t_ref, own_ref = refs
    rank = own_ref.shape[1]
    mine, theirs = [jnp.concatenate([ref[...] for ref in halves[i::2]], axis=0) for i in range(2)]
    first = index_ref[1] == 0
    projected = jnp.concatenate([jnp.where(first, mine, theirs), jnp.where(first, theirs, mine)], axis=0)
    high, low = split(projected)
    cross = dot(high, low, ROWS_BY_ROWS)
    gram = dot(high, high, ROWS_BY_ROWS) + (cross + cross.T)
    row = lax.broadcasted_iota(jnp.int32, (rank, rank), 0)
    column = lax.broadcasted_iota(jnp.int32, (rank, rank), 1)
    total = jnp.sum(projected * projected)
    correlation = gram / total
    correlation_split = split(correlation)
    square = product(correlation_split, correlation_split)
    tail = jnp.where(row == column, 1.6875, 0.0) - 0.5625 * correlation + 0.0625 * square
    mixing = (jnp.where(row == column, 2.25, 0.0) - 2.4375 * correlation) + product(split(square), split(tail))
    mixing_high, mixing_low = split(mixing)

    rows = own_ref.shape[0]
    group = high_t_ref.shape[1] // rows
    places = [order.index(k) for k in range(group)]
    high = jnp.concatenate([high[i * rows : (i + 1) * rows] for i in places], axis=0)
    low = jnp.concatenate([low[i * rows : (i + 1) * rows] for i in places], axis=0)
    scale = lax.rsqrt(total)
    own = product((high[:rows], low[:rows]), (mixing_high, mixing_low))
    own_ref[...] = own * (scale * math.sqrt(times * rows))
    width = rank // times
    source = ((row // width) ^ index_ref[0]) * width + row % width
    move = jnp.where(source == column, 1.0, 0.0).astype(jnp.bfloat16)
    moved = dot(move, jnp.concatenate([mixing_high, mixing_low], axis=1)).astype(jnp.bfloat16)
    turned = product((moved[:, :rank], moved[:, rank:]), (high, low), COLUMNS_BY_COLUMNS) * scale
    high_t_ref[...], low_t_ref[...] = split(turned)


def mix(index, pairs, times, group, order):
    halves = [half for pair in pairs for half in pair]
    rank = halves[0].shape[1]
    rows = sum(half.shape[0] for half in halves) // times
    factor = jax.ShapeDtypeStruct((rank, group * rows), jnp.bfloat16)
    return pl.pallas_call(
        functools.partial(mix_kernel, times, order),
        in_specs=[SMEM] + [VMEM] * len(halves),
        out_specs=[VMEM] * 3,
        out_shape=[factor, factor, jax.ShapeDtypeStruct((rows, rank), jnp.float32)],
        compiler_params=params(),
        cost_estimate=FREE,
    )(index, *halves)


def load_kernel(group, high_ref, low_ref, *refs):
    parts, blocks = refs[:group], refs[group:]
    columns = jnp.concatenate([part[...] for part in parts], axis=0)
    value = product((high_ref[...], low_ref[...]), split(columns))
    width = value.shape[0] // len(blocks)
    for i, block in enumerate(blocks):
        block[...] = value[i * width : (i + 1) * width]


def load(high, low, parts, blocks):
    rank = high.shape[0]
    columns = parts[0].shape[1]
    return pl.pallas_call(
        functools.partial(load_kernel, len(parts)),
        in_specs=[VMEM] * (2 + len(parts)),
        out_specs=[VMEM] * blocks,
        out_shape=[jax.ShapeDtypeStruct((rank // blocks, columns), jnp.float32)] * blocks,
        compiler_params=params(),
        cost_estimate=FREE,
    )(high, low, *parts)


def join_kernel(group, sequence, own_ref, *refs):
    *terms, own_out_ref, out_ref, buf, sems = refs
    terms = [terms[sequence.index(k)] for k in range(len(terms))]
    width = terms[0].shape[1]
    member = lax.rem(lax.axis_index("tm"), group)
    copies = [pltpu.make_async_copy(own_ref, own_out_ref, sems.at[group])]
    copies[0].start()
    for k in range(group):
        value = terms[k][...]
        for term in terms[group + k :: group]:
            value = value + term[...]
        buf[k] = value
        span = pl.ds(pl.multiple_of((member ^ k) * width, width), width)
        copies.append(pltpu.make_async_copy(buf.at[k], out_ref.at[:, span], sems.at[k]))
        copies[-1].start()
    for copy in copies:
        copy.wait()


def join(own, terms, group, sequence):
    rows, width = terms[0].shape
    return pl.pallas_call(
        functools.partial(join_kernel, group, sequence),
        in_specs=[VMEM] * (1 + len(terms)),
        out_specs=[HBM] * 2,
        out_shape=[
            jax.ShapeDtypeStruct(own.shape, jnp.float32),
            jax.ShapeDtypeStruct((rows, group * width), jnp.float32),
        ],
        scratch_shapes=[pltpu.VMEM((group, rows, width), jnp.float32), pltpu.SemaphoreType.DMA((group + 1,))],
        compiler_params=params(),
        cost_estimate=FREE,
    )(own, *[terms[k] for k in sequence])


def swap(value, axis, offset):
    return lax.ppermute(value, axis, [(i, i ^ offset) for i in range(lax.axis_size(axis))])


def swap_by_core(value, offset, other_offset):
    spaces = lax.axis_size("space")
    pairs = []
    for t in range(lax.axis_size("tm")):
        for s in range(spaces):
            step = other_offset if s % 2 else offset
            if step:
                pairs.append((t * spaces + s, (t ^ step) * spaces + s))
    return lax.ppermute(value, ("tm", "space"), pairs)


def on_device(snapshots, space_factor):
    rows, points = snapshots.shape
    rank = space_factor.shape[1]
    times, spaces = lax.axis_size("tm"), lax.axis_size("space")
    group = min(4, times)
    index = lax.axis_index("tm")
    core = lax.axis_index("space") % 2

    partial, parts = project(snapshots, space_factor, group)
    parts[1:3] = [swap(parts[k], "tm", k) for k in (1, 2)]

    terms = [partial] + [swap(partial, "space", k) for k in range(1, spaces)]
    while len(terms) > 1:
        terms = [a + b for a, b in zip(terms[::2], terms[1::2])]
    projected = terms[0]
    projected, *parts[1:3] = lax.optimization_barrier((projected, *parts[1:3]))

    offsets = [*range(group, times), *range(1, group), 0]
    orders = offsets[: times - group : 2] + offsets[times - group :: 2], offsets[1 : times - group : 2] + offsets[times - group + 1 :: 2]
    mine = [swap_by_core(projected, a, b) for a, b in zip(*orders)]
    mine[0], parts[3] = lax.optimization_barrier((mine[0], parts[3]))
    parts[3] = swap(parts[3], "tm", 3)
    for i in range(2):
        if orders[i][-1] == 0:
            mine[-1] = jnp.where(core == i, projected, mine[-1])
    middle = len(mine) // 2
    pairs = []
    for half in (mine[:middle], mine[middle:]):
        half = jnp.concatenate(half, axis=0)
        pairs.append((half, swap(half, "space", 1)))
    high_t, low_t, own = mix(jnp.stack([index, core]), pairs, times, group, orders[0] + orders[1])

    blocks = list(load(high_t, low_t, parts, times))
    terms = [blocks[0]] + [None] * (times - 1)
    near, far = list(range(1, group)), list(range(group, times))
    sequence = [*far[:2], *near[:2], *far[2:], *near[2:], 0]
    for k in sequence[:-1]:
        if k == near[-1]:
            blocks[k], terms[1] = lax.optimization_barrier((blocks[k], terms[1]))
        terms[k] = swap(blocks[k], "tm", k)
    return tuple(join(own, terms, group, sequence))


def solution(mesh):
    return jax.shard_map(
        on_device,
        mesh=mesh,
        in_specs=(P("tm", "space"), P("space", None)),
        out_specs=(P("tm", None), P("tm", "space")),
        check_vma=False,
    )
```

```python
import functools
import math

import jax
import jax.numpy as jnp
from jax import lax
from jax.experimental import pallas as pl
from jax.experimental.pallas import tpu as pltpu
from jax.sharding import PartitionSpec as P

MIB = 1024 * 1024
HBM = pl.BlockSpec(memory_space=pltpu.HBM)
SMEM = pl.BlockSpec(memory_space=pltpu.SMEM)
VMEM = pl.BlockSpec(memory_space=pltpu.VMEM)
FREE = pl.CostEstimate(flops=0, bytes_accessed=0, transcendentals=0)
ROWS_BY_ROWS = (((0,), (0,)), ((), ()))
ROWS_BY_COLUMNS = (((1,), (0,)), ((), ()))
COLUMNS_BY_COLUMNS = (((1,), (1,)), ((), ()))


def params(mib=48):
    return pltpu.CompilerParams(vmem_limit_bytes=mib * MIB)


def split(value):
    high = value.astype(jnp.bfloat16)
    return high, (value - high.astype(jnp.float32)).astype(jnp.bfloat16)


def dot(left, right, dims=ROWS_BY_COLUMNS):
    return lax.dot_general(left, right, dims, preferred_element_type=jnp.float32)


def product(left, right, dims=ROWS_BY_COLUMNS):
    (left_high, left_low), (right_high, right_low) = left, right
    return dot(left_high, right_high, dims) + (
        dot(left_high, right_low, dims) + dot(left_low, right_high, dims)
    )


def project_kernel(depth, snapshots_ref, factor_ref, mine_ref, other_ref, *refs):
    *parts, snapshots_buf, factor_buf, sems = refs
    rows, points = snapshots_ref.shape
    half = rows // 2
    snapshots_copy = pltpu.make_async_copy(snapshots_ref, snapshots_buf, sems.at[points // depth])
    snapshots_copy.start()
    copies = []
    for i, start in enumerate(range(0, points, depth)):
        span = pl.ds(start, depth)
        copies.append(pltpu.make_async_copy(factor_ref.at[span, :], factor_buf.at[span, :], sems.at[i]))
        copies[-1].start()
    snapshots_copy.wait()
    width = parts[0].shape[1]
    member = lax.rem(lax.axis_index("tm"), len(parts))
    for k, part in enumerate(parts):
        part[...] = snapshots_buf[:, pl.ds(pl.multiple_of((member ^ k) * width, width), width)]
    value = None
    for i, start in enumerate(range(0, points, depth)):
        copies[i].wait()
        high, low = split(snapshots_buf[:, start : start + depth])
        factor_high, factor_low = split(factor_buf[start : start + depth, :])
        both = dot(jnp.concatenate([high, low], axis=0), factor_high)
        term = both[:rows] + (both[rows:] + dot(high, factor_low))
        value = term if value is None else value + term
    first = lax.rem(lax.axis_index("space"), 2) == 0
    mine_ref[...] = jnp.where(first, value[:half], value[half:])
    other_ref[...] = jnp.where(first, value[half:], value[:half])


def project(snapshots, space_factor, group):
    rows, points = snapshots.shape
    rank = space_factor.shape[1]
    depth = min(512, points)
    half = jax.ShapeDtypeStruct((rows // 2, rank), jnp.float32)
    part = jax.ShapeDtypeStruct((rows, points // group), jnp.float32)
    mine, other, *parts = pl.pallas_call(
        functools.partial(project_kernel, depth),
        in_specs=[HBM, HBM],
        out_specs=[VMEM] * (2 + group),
        out_shape=[half, half] + [part] * group,
        scratch_shapes=[
            pltpu.VMEM((rows, points), jnp.float32),
            pltpu.VMEM((points, rank), jnp.float32),
            pltpu.SemaphoreType.DMA((points // depth + 1,)),
        ],
        compiler_params=params(52),
        cost_estimate=FREE,
    )(snapshots, space_factor)
    return mine, other, parts


def mix_kernel(times, order, index_ref, *refs):
    *halves, high_t_ref, low_t_ref, own_ref = refs
    rank = own_ref.shape[1]
    mine, theirs = [jnp.concatenate([ref[...] for ref in halves[i::2]], axis=0) for i in range(2)]
    total_half = mine.shape[0]
    half = total_half // times
    mine = mine.reshape(times, half, rank)
    theirs = theirs.reshape(times, half, rank)
    first = index_ref[1] == 0
    low_rows, high_rows = jnp.where(first, mine, theirs), jnp.where(first, theirs, mine)
    projected = jnp.concatenate([low_rows, high_rows], axis=1).reshape(2 * total_half, rank)
    high, low = split(projected)
    cross = dot(high, low, ROWS_BY_ROWS)
    gram = dot(high, high, ROWS_BY_ROWS) + (cross + cross.T)
    row = lax.broadcasted_iota(jnp.int32, (rank, rank), 0)
    column = lax.broadcasted_iota(jnp.int32, (rank, rank), 1)
    total = jnp.sum(projected * projected)
    correlation = gram / total
    correlation_split = split(correlation)
    square = product(correlation_split, correlation_split)
    tail = jnp.where(row == column, 1.6875, 0.0) - 0.5625 * correlation + 0.0625 * square
    mixing = (jnp.where(row == column, 2.25, 0.0) - 2.4375 * correlation) + product(split(square), split(tail))
    mixing_high, mixing_low = split(mixing)

    rows = 2 * half
    group = high_t_ref.shape[1] // rows
    places = [order.index(k) for k in range(group)]
    high = jnp.concatenate([high[i * rows : (i + 1) * rows] for i in places], axis=0)
    low = jnp.concatenate([low[i * rows : (i + 1) * rows] for i in places], axis=0)
    scale = lax.rsqrt(total)
    own = product((high[:rows], low[:rows]), (mixing_high, mixing_low))
    own_ref[...] = own * (scale * math.sqrt(times * rows))
    width = rank // times
    source = ((row // width) ^ index_ref[0]) * width + row % width
    move = jnp.where(source == column, 1.0, 0.0).astype(jnp.bfloat16)
    moved = dot(move, jnp.concatenate([mixing_high, mixing_low], axis=1)).astype(jnp.bfloat16)
    turned = product((moved[:, :rank], moved[:, rank:]), (high, low), COLUMNS_BY_COLUMNS) * scale
    high_t_ref[...], low_t_ref[...] = split(turned)


def mix(index, pairs, times, group, order):
    halves = [half for pair in pairs for half in pair]
    rank = halves[0].shape[1]
    rows = sum(half.shape[0] for half in halves) // times
    factor = jax.ShapeDtypeStruct((rank, group * rows), jnp.bfloat16)
    return pl.pallas_call(
        functools.partial(mix_kernel, times, order),
        in_specs=[SMEM] + [VMEM] * len(halves),
        out_specs=[VMEM] * 3,
        out_shape=[factor, factor, jax.ShapeDtypeStruct((rows, rank), jnp.float32)],
        compiler_params=params(),
        cost_estimate=FREE,
    )(index, *halves)


def load_kernel(group, high_ref, low_ref, *refs):
    parts, blocks = refs[:group], refs[group:]
    columns = jnp.concatenate([part[...] for part in parts], axis=0)
    value = product((high_ref[...], low_ref[...]), split(columns))
    width = value.shape[0] // len(blocks)
    for i, block in enumerate(blocks):
        block[...] = value[i * width : (i + 1) * width]


def load(high, low, parts, blocks):
    rank = high.shape[0]
    columns = parts[0].shape[1]
    return pl.pallas_call(
        functools.partial(load_kernel, len(parts)),
        in_specs=[VMEM] * (2 + len(parts)),
        out_specs=[VMEM] * blocks,
        out_shape=[jax.ShapeDtypeStruct((rank // blocks, columns), jnp.float32)] * blocks,
        compiler_params=params(),
        cost_estimate=FREE,
    )(high, low, *parts)


def join_kernel(group, sequence, own_ref, *refs):
    *terms, own_out_ref, out_ref, buf, sems = refs
    terms = [terms[sequence.index(k)] for k in range(len(terms))]
    width = terms[0].shape[1]
    member = lax.rem(lax.axis_index("tm"), group)
    copies = [pltpu.make_async_copy(own_ref, own_out_ref, sems.at[group])]
    copies[0].start()
    for k in range(group):
        value = terms[k][...]
        for term in terms[group + k :: group]:
            value = value + term[...]
        buf[k] = value
        span = pl.ds(pl.multiple_of((member ^ k) * width, width), width)
        copies.append(pltpu.make_async_copy(buf.at[k], out_ref.at[:, span], sems.at[k]))
        copies[-1].start()
    for copy in copies:
        copy.wait()


def join(own, terms, group, sequence):
    rows, width = terms[0].shape
    return pl.pallas_call(
        functools.partial(join_kernel, group, sequence),
        in_specs=[VMEM] * (1 + len(terms)),
        out_specs=[HBM] * 2,
        out_shape=[
            jax.ShapeDtypeStruct(own.shape, jnp.float32),
            jax.ShapeDtypeStruct((rows, group * width), jnp.float32),
        ],
        scratch_shapes=[pltpu.VMEM((group, rows, width), jnp.float32), pltpu.SemaphoreType.DMA((group + 1,))],
        compiler_params=params(),
        cost_estimate=FREE,
    )(own, *[terms[k] for k in sequence])


def swap(value, axis, offset):
    return lax.ppermute(value, axis, [(i, i ^ offset) for i in range(lax.axis_size(axis))])


def on_device(snapshots, space_factor):
    rows, points = snapshots.shape
    rank = space_factor.shape[1]
    times, spaces = lax.axis_size("tm"), lax.axis_size("space")
    group = min(4, times)
    index = lax.axis_index("tm")
    core = lax.axis_index("space") % 2

    mine, other, parts = project(snapshots, space_factor, group)
    parts = [part if k == 0 else swap(part, "tm", k) for k, part in enumerate(parts)]

    terms = [mine] + [swap(other if k % 2 else mine, "space", k) for k in range(1, spaces)]
    while len(terms) > 1:
        terms = [a + b for a, b in zip(terms[::2], terms[1::2])]
    mine = terms[0]

    near = group // 2
    order = [k for k in range(times) if k % group < near]
    mine = jnp.concatenate([mine] + [swap(mine, "tm", k) for k in order[1:]], axis=0)
    mine, *parts[1:3] = lax.optimization_barrier((mine, *parts[1:3]))
    rest = swap(mine, "tm", near)
    pairs = [(mine, swap(mine, "space", 1))]
    pairs.append((rest, swap(rest, "space", 1)))
    order = order + [k ^ near for k in order]
    high_t, low_t, own = mix(jnp.stack([index, core]), pairs, times, group, order)

    blocks = list(load(high_t, low_t, parts, times))
    terms = [blocks[0]] + [None] * (times - 1)
    near, far = list(range(1, group)), list(range(group, times))
    sequence = [*far, *near, 0]
    for k in sequence[:-1]:
        if k == near[-1]:
            blocks[k], terms[1] = lax.optimization_barrier((blocks[k], terms[1]))
        terms[k] = swap(blocks[k], "tm", k)
    return tuple(join(own, terms, group, sequence))


def solution(mesh):
    return jax.shard_map(
        on_device,
        mesh=mesh,
        in_specs=(P("tm", "space"), P("space", None)),
        out_specs=(P("tm", None), P("tm", "space")),
        check_vma=False,
    )
```

```python
import functools
import math

import jax
import jax.numpy as jnp
from jax import lax
from jax.experimental import pallas as pl
from jax.experimental.pallas import tpu as pltpu
from jax.sharding import PartitionSpec as P

MIB = 1024 * 1024
HBM = pl.BlockSpec(memory_space=pltpu.HBM)
SMEM = pl.BlockSpec(memory_space=pltpu.SMEM)
VMEM = pl.BlockSpec(memory_space=pltpu.VMEM)
FREE = pl.CostEstimate(flops=0, bytes_accessed=0, transcendentals=0)
ROWS_BY_ROWS = (((0,), (0,)), ((), ()))
ROWS_BY_COLUMNS = (((1,), (0,)), ((), ()))
COLUMNS_BY_COLUMNS = (((1,), (1,)), ((), ()))


def params(mib=48):
    return pltpu.CompilerParams(vmem_limit_bytes=mib * MIB)


def split(value):
    high = value.astype(jnp.bfloat16)
    return high, (value - high.astype(jnp.float32)).astype(jnp.bfloat16)


def dot(left, right, dims=ROWS_BY_COLUMNS):
    return lax.dot_general(left, right, dims, preferred_element_type=jnp.float32)


def product(left, right, dims=ROWS_BY_COLUMNS):
    (left_high, left_low), (right_high, right_low) = left, right
    rows = left_high.shape[0]
    both = dot(jnp.concatenate([left_high, left_low], axis=0), right_high, dims)
    return both[:rows] + (both[rows:] + dot(left_high, right_low, dims))


def project_kernel(depth, snapshots_ref, factor_ref, mine_ref, other_ref, *refs):
    *parts, snapshots_buf, factor_buf, sems = refs
    rows, points = snapshots_ref.shape
    half = rows // 2
    count = sems.shape[0] - points // depth
    snapshots_copies = []
    for i in range(count):
        span = pl.ds(i * (rows // count), rows // count)
        snapshots_copies.append(
            pltpu.make_async_copy(snapshots_ref.at[span, :], snapshots_buf.at[span, :], sems.at[points // depth + i])
        )
        snapshots_copies[-1].start()
    copies = []
    for i, start in enumerate(range(0, points, depth)):
        span = pl.ds(start, depth)
        copies.append(pltpu.make_async_copy(factor_ref.at[span, :], factor_buf.at[span, :], sems.at[i]))
        copies[-1].start()
    for copy in snapshots_copies:
        copy.wait()
    width = parts[0].shape[1]
    member = lax.rem(lax.axis_index("tm"), len(parts))
    for k, part in enumerate(parts):
        part[...] = snapshots_buf[:, pl.ds(pl.multiple_of((member ^ k) * width, width), width)]
    value = None
    for i, start in enumerate(range(0, points, depth)):
        copies[i].wait()
        high, low = split(snapshots_buf[:, start : start + depth])
        factor_high, factor_low = split(factor_buf[start : start + depth, :])
        both = dot(jnp.concatenate([high, low], axis=0), factor_high)
        term = both[:rows] + (both[rows:] + dot(high, factor_low))
        value = term if value is None else value + term
    first = lax.rem(lax.axis_index("space"), 2) == 0
    mine_ref[...] = jnp.where(first, value[:half], value[half:])
    other_ref[...] = jnp.where(first, value[half:], value[:half])


def project(snapshots, space_factor, group):
    rows, points = snapshots.shape
    rank = space_factor.shape[1]
    depth = min(256, points)
    count = 4 if rows % 32 == 0 else 1
    half = jax.ShapeDtypeStruct((rows // 2, rank), jnp.float32)
    part = jax.ShapeDtypeStruct((rows, points // group), jnp.float32)
    mine, other, *parts = pl.pallas_call(
        functools.partial(project_kernel, depth),
        in_specs=[HBM, HBM],
        out_specs=[VMEM] * (2 + group),
        out_shape=[half, half] + [part] * group,
        scratch_shapes=[
            pltpu.VMEM((rows, points), jnp.float32),
            pltpu.VMEM((points, rank), jnp.float32),
            pltpu.SemaphoreType.DMA((points // depth + count,)),
        ],
        compiler_params=params(52),
        cost_estimate=FREE,
    )(snapshots, space_factor)
    return mine, other, parts


def mix_kernel(times, order, index_ref, *refs):
    *halves, high_t_ref, low_t_ref, own_ref = refs
    rank = own_ref.shape[1]
    mine, theirs = [jnp.concatenate([ref[...] for ref in halves[i::2]], axis=0) for i in range(2)]
    total_half = mine.shape[0]
    half = total_half // times
    mine = mine.reshape(times, half, rank)
    theirs = theirs.reshape(times, half, rank)
    first = index_ref[1] == 0
    low_rows, high_rows = jnp.where(first, mine, theirs), jnp.where(first, theirs, mine)
    projected = jnp.concatenate([low_rows, high_rows], axis=1).reshape(2 * total_half, rank)
    high, low = split(projected)
    cross = dot(high, low, ROWS_BY_ROWS)
    gram = dot(high, high, ROWS_BY_ROWS) + (cross + cross.T)
    row = lax.broadcasted_iota(jnp.int32, (rank, rank), 0)
    column = lax.broadcasted_iota(jnp.int32, (rank, rank), 1)
    total = jnp.sum(projected * projected)
    correlation = gram / total
    correlation_split = split(correlation)
    square = product(correlation_split, correlation_split)
    tail = jnp.where(row == column, 1.6875, 0.0) - 0.5625 * correlation + 0.0625 * square
    mixing = (jnp.where(row == column, 2.25, 0.0) - 2.4375 * correlation) + product(split(square), split(tail))
    mixing_high, mixing_low = split(mixing)

    rows = 2 * half
    group = high_t_ref.shape[1] // rows
    places = [order.index(k) for k in range(group)]
    high = jnp.concatenate([high[i * rows : (i + 1) * rows] for i in places], axis=0)
    low = jnp.concatenate([low[i * rows : (i + 1) * rows] for i in places], axis=0)
    scale = lax.rsqrt(total)
    own = product((high[:rows], low[:rows]), (mixing_high, mixing_low))
    own_ref[...] = own * (scale * math.sqrt(times * rows))
    width = rank // times
    source = ((row // width) ^ index_ref[0]) * width + row % width
    move = jnp.where(source == column, 1.0, 0.0).astype(jnp.bfloat16)
    moved = dot(move, jnp.concatenate([mixing_high, mixing_low], axis=1)).astype(jnp.bfloat16)
    turned = product((moved[:, :rank], moved[:, rank:]), (high, low), COLUMNS_BY_COLUMNS) * scale
    high_t_ref[...], low_t_ref[...] = split(turned)


def mix(index, pairs, times, group, order):
    halves = [half for pair in pairs for half in pair]
    rank = halves[0].shape[1]
    rows = sum(half.shape[0] for half in halves) // times
    factor = jax.ShapeDtypeStruct((rank, group * rows), jnp.bfloat16)
    return pl.pallas_call(
        functools.partial(mix_kernel, times, order),
        in_specs=[SMEM] + [VMEM] * len(halves),
        out_specs=[VMEM] * 3,
        out_shape=[factor, factor, jax.ShapeDtypeStruct((rows, rank), jnp.float32)],
        compiler_params=params(),
        cost_estimate=FREE,
    )(index, *halves)


def load_kernel(group, high_ref, low_ref, *refs):
    parts, blocks = refs[:group], refs[group:]
    columns = jnp.concatenate([part[...] for part in parts], axis=0)
    value = product((high_ref[...], low_ref[...]), split(columns))
    width = value.shape[0] // len(blocks)
    for i, block in enumerate(blocks):
        block[...] = value[i * width : (i + 1) * width]


def load(high, low, parts, blocks):
    rank = high.shape[0]
    columns = parts[0].shape[1]
    return pl.pallas_call(
        functools.partial(load_kernel, len(parts)),
        in_specs=[VMEM] * (2 + len(parts)),
        out_specs=[VMEM] * blocks,
        out_shape=[jax.ShapeDtypeStruct((rank // blocks, columns), jnp.float32)] * blocks,
        compiler_params=params(),
        cost_estimate=FREE,
    )(high, low, *parts)


def join_kernel(group, sequence, own_ref, *refs):
    *terms, own_out_ref, out_ref, buf, sems = refs
    terms = [terms[sequence.index(k)] for k in range(len(terms))]
    width = terms[0].shape[1]
    member = lax.rem(lax.axis_index("tm"), group)
    copies = [pltpu.make_async_copy(own_ref, own_out_ref, sems.at[group])]
    copies[0].start()
    for k in range(group):
        value = terms[k][...]
        for term in terms[group + k :: group]:
            value = value + term[...]
        buf[k] = value
        span = pl.ds(pl.multiple_of((member ^ k) * width, width), width)
        copies.append(pltpu.make_async_copy(buf.at[k], out_ref.at[:, span], sems.at[k]))
        copies[-1].start()
    for copy in copies:
        copy.wait()


def join(own, terms, group, sequence):
    rows, width = terms[0].shape
    return pl.pallas_call(
        functools.partial(join_kernel, group, sequence),
        in_specs=[VMEM] * (1 + len(terms)),
        out_specs=[HBM] * 2,
        out_shape=[
            jax.ShapeDtypeStruct(own.shape, jnp.float32),
            jax.ShapeDtypeStruct((rows, group * width), jnp.float32),
        ],
        scratch_shapes=[pltpu.VMEM((group, rows, width), jnp.float32), pltpu.SemaphoreType.DMA((group + 1,))],
        compiler_params=params(),
        cost_estimate=FREE,
    )(own, *[terms[k] for k in sequence])


def swap(value, axis, offset):
    return lax.ppermute(value, axis, [(i, i ^ offset) for i in range(lax.axis_size(axis))])


def on_device(snapshots, space_factor):
    rows, points = snapshots.shape
    rank = space_factor.shape[1]
    times, spaces = lax.axis_size("tm"), lax.axis_size("space")
    group = min(4, times)
    index = lax.axis_index("tm")
    core = lax.axis_index("space") % 2

    mine, other, parts = project(snapshots, space_factor, group)
    parts = [part if k == 0 else swap(part, "tm", k) for k, part in enumerate(parts)]

    terms = [mine] + [swap(other if k % 2 else mine, "space", k) for k in range(1, spaces)]
    while len(terms) > 1:
        terms = [a + b for a, b in zip(terms[::2], terms[1::2])]
    mine = terms[0]

    near = group // 2
    order = [k for k in range(times) if k % group < near]
    mine = jnp.concatenate([mine] + [swap(mine, "tm", k) for k in order[1:]], axis=0)
    mine, *parts[1:3] = lax.optimization_barrier((mine, *parts[1:3]))
    rest = swap(mine, "tm", near)
    pairs = [(mine, swap(mine, "space", 1))]
    pairs.append((rest, swap(rest, "space", 1)))
    order = order + [k ^ near for k in order]
    high_t, low_t, own = mix(jnp.stack([index, core]), pairs, times, group, order)

    blocks = list(load(high_t, low_t, parts, times))
    terms = [blocks[0]] + [None] * (times - 1)
    near, far = list(range(1, group)), list(range(group, times))
    sequence = [*far[:2], *near[:2], *far[2:], *near[2:], 0]
    for k in sequence[:-1]:
        if k == near[-1]:
            blocks[k], terms[1] = lax.optimization_barrier((blocks[k], terms[1]))
        terms[k] = swap(blocks[k], "tm", k)
    return tuple(join(own, terms, group, sequence))


def solution(mesh):
    return jax.shard_map(
        on_device,
        mesh=mesh,
        in_specs=(P("tm", "space"), P("space", None)),
        out_specs=(P("tm", None), P("tm", "space")),
        check_vma=False,
    )
```

```python
import functools
import math

import jax
import jax.numpy as jnp
from jax import lax
from jax.experimental import pallas as pl
from jax.experimental.pallas import tpu as pltpu
from jax.sharding import PartitionSpec as P

MIB = 1024 * 1024
HBM = pl.BlockSpec(memory_space=pltpu.HBM)
SMEM = pl.BlockSpec(memory_space=pltpu.SMEM)
VMEM = pl.BlockSpec(memory_space=pltpu.VMEM)
FREE = pl.CostEstimate(flops=0, bytes_accessed=0, transcendentals=0)
ROWS_BY_ROWS = (((0,), (0,)), ((), ()))
ROWS_BY_COLUMNS = (((1,), (0,)), ((), ()))
COLUMNS_BY_COLUMNS = (((1,), (1,)), ((), ()))


def params(mib=48):
    return pltpu.CompilerParams(vmem_limit_bytes=mib * MIB)


def split(value):
    high = value.astype(jnp.bfloat16)
    return high, (value - high.astype(jnp.float32)).astype(jnp.bfloat16)


def dot(left, right, dims=ROWS_BY_COLUMNS):
    return lax.dot_general(left, right, dims, preferred_element_type=jnp.float32)


def product(left, right, dims=ROWS_BY_COLUMNS):
    (left_high, left_low), (right_high, right_low) = left, right
    rows = left_high.shape[0]
    both = dot(jnp.concatenate([left_high, left_low], axis=0), right_high, dims)
    return both[:rows] + (both[rows:] + dot(left_high, right_low, dims))


def project_kernel(depth, snapshots_ref, factor_ref, mine_ref, other_ref, *refs):
    *parts, snapshots_buf, factor_buf, sems = refs
    rows, points = snapshots_ref.shape
    half = rows // 2
    snapshots_copy = pltpu.make_async_copy(snapshots_ref, snapshots_buf, sems.at[points // depth])
    snapshots_copy.start()
    copies = []
    for i, start in enumerate(range(0, points, depth)):
        span = pl.ds(start, depth)
        copies.append(pltpu.make_async_copy(factor_ref.at[span, :], factor_buf.at[span, :], sems.at[i]))
        copies[-1].start()
    snapshots_copy.wait()
    width = parts[0].shape[1]
    member = lax.rem(lax.axis_index("tm"), len(parts))
    for k, part in enumerate(parts):
        part[...] = snapshots_buf[:, pl.ds(pl.multiple_of((member ^ k) * width, width), width)]
    value = None
    for i, start in enumerate(range(0, points, depth)):
        copies[i].wait()
        high, low = split(snapshots_buf[:, start : start + depth])
        factor_high, factor_low = split(factor_buf[start : start + depth, :])
        both = dot(jnp.concatenate([high, low], axis=0), factor_high)
        term = both[:rows] + (both[rows:] + dot(high, factor_low))
        value = term if value is None else value + term
    first = lax.rem(lax.axis_index("space"), 2) == 0
    mine_ref[...] = jnp.where(first, value[:half], value[half:])
    other_ref[...] = jnp.where(first, value[half:], value[:half])


def project(snapshots, space_factor, group):
    rows, points = snapshots.shape
    rank = space_factor.shape[1]
    depth = min(512, points)
    half = jax.ShapeDtypeStruct((rows // 2, rank), jnp.float32)
    part = jax.ShapeDtypeStruct((rows, points // group), jnp.float32)
    mine, other, *parts = pl.pallas_call(
        functools.partial(project_kernel, depth),
        in_specs=[HBM, HBM],
        out_specs=[VMEM] * (2 + group),
        out_shape=[half, half] + [part] * group,
        scratch_shapes=[
            pltpu.VMEM((rows, points), jnp.float32),
            pltpu.VMEM((points, rank), jnp.float32),
            pltpu.SemaphoreType.DMA((points // depth + 1,)),
        ],
        compiler_params=params(52),
        cost_estimate=FREE,
    )(snapshots, space_factor)
    return mine, other, parts


def mix_kernel(times, order, index_ref, *refs):
    *halves, high_t_ref, low_t_ref, own_ref = refs
    rank = own_ref.shape[1]
    mine, theirs = [jnp.concatenate([ref[...] for ref in halves[i::2]], axis=0) for i in range(2)]
    total_half = mine.shape[0]
    half = total_half // times
    mine = mine.reshape(times, half, rank)
    theirs = theirs.reshape(times, half, rank)
    first = index_ref[1] == 0
    low_rows, high_rows = jnp.where(first, mine, theirs), jnp.where(first, theirs, mine)
    projected = jnp.concatenate([low_rows, high_rows], axis=1).reshape(2 * total_half, rank)
    high, low = split(projected)
    cross = dot(high, low, ROWS_BY_ROWS)
    gram = dot(high, high, ROWS_BY_ROWS) + (cross + cross.T)
    row = lax.broadcasted_iota(jnp.int32, (rank, rank), 0)
    column = lax.broadcasted_iota(jnp.int32, (rank, rank), 1)
    total = jnp.sum(projected * projected)
    correlation = gram / total
    correlation_split = split(correlation)
    square = product(correlation_split, correlation_split)
    tail = jnp.where(row == column, 1.6875, 0.0) - 0.5625 * correlation + 0.0625 * square
    mixing = (jnp.where(row == column, 2.25, 0.0) - 2.4375 * correlation) + product(split(square), split(tail))
    mixing_high, mixing_low = split(mixing)

    rows = 2 * half
    group = high_t_ref.shape[1] // rows
    places = [order.index(k) for k in range(group)]
    high = jnp.concatenate([high[i * rows : (i + 1) * rows] for i in places], axis=0)
    low = jnp.concatenate([low[i * rows : (i + 1) * rows] for i in places], axis=0)
    scale = lax.rsqrt(total)
    own = product((high[:rows], low[:rows]), (mixing_high, mixing_low))
    own_ref[...] = own * (scale * math.sqrt(times * rows))
    width = rank // times
    source = ((row // width) ^ index_ref[0]) * width + row % width
    move = jnp.where(source == column, 1.0, 0.0).astype(jnp.bfloat16)
    moved = dot(move, jnp.concatenate([mixing_high, mixing_low], axis=1)).astype(jnp.bfloat16)
    turned = product((moved[:, :rank], moved[:, rank:]), (high, low), COLUMNS_BY_COLUMNS) * scale
    high_t_ref[...], low_t_ref[...] = split(turned)


def mix(index, pairs, times, group, order):
    halves = [half for pair in pairs for half in pair]
    rank = halves[0].shape[1]
    rows = sum(half.shape[0] for half in halves) // times
    factor = jax.ShapeDtypeStruct((rank, group * rows), jnp.bfloat16)
    return pl.pallas_call(
        functools.partial(mix_kernel, times, order),
        in_specs=[SMEM] + [VMEM] * len(halves),
        out_specs=[VMEM] * 3,
        out_shape=[factor, factor, jax.ShapeDtypeStruct((rows, rank), jnp.float32)],
        compiler_params=params(),
        cost_estimate=FREE,
    )(index, *halves)


def load_kernel(group, high_ref, low_ref, *refs):
    parts, blocks = refs[:group], refs[group:]
    columns = jnp.concatenate([part[...] for part in parts], axis=0)
    value = product((high_ref[...], low_ref[...]), split(columns))
    width = value.shape[0] // len(blocks)
    for i, block in enumerate(blocks):
        block[...] = value[i * width : (i + 1) * width]


def load(high, low, parts, blocks):
    rank = high.shape[0]
    columns = parts[0].shape[1]
    return pl.pallas_call(
        functools.partial(load_kernel, len(parts)),
        in_specs=[VMEM] * (2 + len(parts)),
        out_specs=[VMEM] * blocks,
        out_shape=[jax.ShapeDtypeStruct((rank // blocks, columns), jnp.float32)] * blocks,
        compiler_params=params(),
        cost_estimate=FREE,
    )(high, low, *parts)


def join_kernel(group, members, count, *refs):
    *refs, out_ref, buf, sems = refs
    terms = refs[:count]
    width = buf.shape[2]
    member = lax.rem(lax.axis_index("tm"), group)
    copies = []
    if len(refs) > count + 1:
        own_ref, own_out_ref = refs[count:]
        copies.append(pltpu.make_async_copy(own_ref, own_out_ref, sems.at[len(members)]))
        copies[0].start()
    for i, k in enumerate(members):
        value = terms[i][...]
        for term in terms[i + len(members) :: len(members)]:
            value = value + term[...]
        buf[i] = value
        span = pl.ds(pl.multiple_of((member ^ k) * width, width), width)
        copies.append(pltpu.make_async_copy(buf.at[i], out_ref.at[:, span], sems.at[i]))
        copies[-1].start()
    for copy in copies:
        copy.wait()


def join(own, terms, group):
    rows, width = terms[0].shape
    loadings = jax.ShapeDtypeStruct((rows, group * width), jnp.float32)

    def call(members, value, spec, out_shape, aliases):
        firsts = reversed(range(0, len(terms), group))
        picked = [terms[first + k] for first in firsts for k in members]
        return pl.pallas_call(
            functools.partial(join_kernel, group, members, len(picked)),
            in_specs=[VMEM] * len(picked) + [spec],
            out_specs=[HBM] * len(out_shape),
            out_shape=out_shape,
            scratch_shapes=[
                pltpu.VMEM((len(members), rows, width), jnp.float32),
                pltpu.SemaphoreType.DMA((len(members) + 1,)),
            ],
            input_output_aliases={len(picked): 0} if aliases else {},
            compiler_params=params(),
            cost_estimate=FREE,
        )(*picked, value)

    half = group // 2
    own_shape = jax.ShapeDtypeStruct(own.shape, jnp.float32)
    own, loaded = call(range(half), own, VMEM, [own_shape, loadings], False)
    return own, call(range(half, group), loaded, HBM, [loadings], True)[0]


def swap(value, axis, offset):
    return lax.ppermute(value, axis, [(i, i ^ offset) for i in range(lax.axis_size(axis))])


def on_device(snapshots, space_factor):
    rows, points = snapshots.shape
    rank = space_factor.shape[1]
    times, spaces = lax.axis_size("tm"), lax.axis_size("space")
    group = min(4, times)
    index = lax.axis_index("tm")
    core = lax.axis_index("space") % 2

    mine, other, parts = project(snapshots, space_factor, group)
    parts = [part if k == 0 else swap(part, "tm", k) for k, part in enumerate(parts)]

    terms = [mine] + [swap(other if k % 2 else mine, "space", k) for k in range(1, spaces)]
    while len(terms) > 1:
        terms = [a + b for a, b in zip(terms[::2], terms[1::2])]
    mine = terms[0]

    near = group // 2
    order = [k for k in range(times) if k % group < near]
    mine = jnp.concatenate([mine] + [swap(mine, "tm", k) for k in order[1:]], axis=0)
    mine, *parts[1:3] = lax.optimization_barrier((mine, *parts[1:3]))
    rest = swap(mine, "tm", near)
    pairs = [(mine, swap(mine, "space", 1))]
    pairs.append((rest, swap(rest, "space", 1)))
    order = order + [k ^ near for k in order]
    high_t, low_t, own = mix(jnp.stack([index, core]), pairs, times, group, order)

    blocks = list(load(high_t, low_t, parts, times))
    terms = [blocks[0]] + [None] * (times - 1)
    near, far = list(range(1, group)), list(range(group, times))
    sequence = [*far[:2], *near[:2], *far[2:], *near[2:], 0]
    for k in sequence[:-1]:
        if k == near[-1]:
            blocks[k], terms[1] = lax.optimization_barrier((blocks[k], terms[1]))
        terms[k] = swap(blocks[k], "tm", k)
    return join(own, terms, group)


def solution(mesh):
    return jax.shard_map(
        on_device,
        mesh=mesh,
        in_specs=(P("tm", "space"), P("space", None)),
        out_specs=(P("tm", None), P("tm", "space")),
        check_vma=False,
    )
```

```python
import functools
import math

import jax
import jax.numpy as jnp
from jax import lax
from jax.experimental import pallas as pl
from jax.experimental.pallas import tpu as pltpu
from jax.sharding import PartitionSpec as P

MIB = 1024 * 1024
HBM = pl.BlockSpec(memory_space=pltpu.HBM)
SMEM = pl.BlockSpec(memory_space=pltpu.SMEM)
VMEM = pl.BlockSpec(memory_space=pltpu.VMEM)
FREE = pl.CostEstimate(flops=0, bytes_accessed=0, transcendentals=0)
ROWS_BY_ROWS = (((0,), (0,)), ((), ()))
ROWS_BY_COLUMNS = (((1,), (0,)), ((), ()))
COLUMNS_BY_COLUMNS = (((1,), (1,)), ((), ()))


def params(mib=48):
    return pltpu.CompilerParams(vmem_limit_bytes=mib * MIB)


def split(value):
    high = value.astype(jnp.bfloat16)
    return high, (value - high.astype(jnp.float32)).astype(jnp.bfloat16)


def dot(left, right, dims=ROWS_BY_COLUMNS):
    return lax.dot_general(left, right, dims, preferred_element_type=jnp.float32)


def product(left, right, dims=ROWS_BY_COLUMNS):
    (left_high, left_low), (right_high, right_low) = left, right
    rows = left_high.shape[0]
    both = dot(jnp.concatenate([left_high, left_low], axis=0), right_high, dims)
    return both[:rows] + (both[rows:] + dot(left_high, right_low, dims))


def project_kernel(depth, snapshots_ref, factor_ref, mine_ref, other_ref, *refs):
    *parts, snapshots_buf, factor_buf, sems = refs
    rows, points = snapshots_ref.shape
    half = rows // 2
    snapshots_copy = pltpu.make_async_copy(snapshots_ref, snapshots_buf, sems.at[points // depth])
    snapshots_copy.start()
    copies = []
    for i, start in enumerate(range(0, points, depth)):
        span = pl.ds(start, depth)
        copies.append(pltpu.make_async_copy(factor_ref.at[span, :], factor_buf.at[span, :], sems.at[i]))
        copies[-1].start()
    snapshots_copy.wait()
    width = parts[0].shape[1]
    member = lax.rem(lax.axis_index("tm"), len(parts))
    for k, part in enumerate(parts):
        part[...] = snapshots_buf[:, pl.ds(pl.multiple_of((member ^ k) * width, width), width)]
    value = None
    for i, start in enumerate(range(0, points, depth)):
        copies[i].wait()
        high, low = split(snapshots_buf[:, start : start + depth])
        factor_high, factor_low = split(factor_buf[start : start + depth, :])
        both = dot(jnp.concatenate([high, low], axis=0), factor_high)
        term = both[:rows] + (both[rows:] + dot(high, factor_low))
        value = term if value is None else value + term
    first = lax.rem(lax.axis_index("space"), 2) == 0
    mine_ref[...] = jnp.where(first, value[:half], value[half:])
    other_ref[...] = jnp.where(first, value[half:], value[:half])


def project(snapshots, space_factor, group):
    rows, points = snapshots.shape
    rank = space_factor.shape[1]
    depth = min(512, points)
    half = jax.ShapeDtypeStruct((rows // 2, rank), jnp.float32)
    part = jax.ShapeDtypeStruct((rows, points // group), jnp.float32)
    mine, other, *parts = pl.pallas_call(
        functools.partial(project_kernel, depth),
        in_specs=[HBM, HBM],
        out_specs=[VMEM] * (2 + group),
        out_shape=[half, half] + [part] * group,
        scratch_shapes=[
            pltpu.VMEM((rows, points), jnp.float32),
            pltpu.VMEM((points, rank), jnp.float32),
            pltpu.SemaphoreType.DMA((points // depth + 1,)),
        ],
        compiler_params=params(52),
        cost_estimate=FREE,
    )(snapshots, space_factor)
    return mine, other, parts


def mix_kernel(times, order, index_ref, *refs):
    *halves, high_t_ref, low_t_ref, own_ref = refs
    rank = own_ref.shape[1]
    mine, theirs = [jnp.concatenate([ref[...] for ref in halves[i::2]], axis=0) for i in range(2)]
    total_half = mine.shape[0]
    half = total_half // times
    mine = mine.reshape(times, half, rank)
    theirs = theirs.reshape(times, half, rank)
    first = index_ref[1] == 0
    low_rows, high_rows = jnp.where(first, mine, theirs), jnp.where(first, theirs, mine)
    projected = jnp.concatenate([low_rows, high_rows], axis=1).reshape(2 * total_half, rank)
    high, low = split(projected)
    cross = dot(high, low, ROWS_BY_ROWS)
    gram = dot(high, high, ROWS_BY_ROWS) + (cross + cross.T)
    row = lax.broadcasted_iota(jnp.int32, (rank, rank), 0)
    column = lax.broadcasted_iota(jnp.int32, (rank, rank), 1)
    total = jnp.sum(projected * projected)
    correlation = gram / total
    correlation_split = split(correlation)
    square = product(correlation_split, correlation_split)
    tail = jnp.where(row == column, 1.6875, 0.0) - 0.5625 * correlation + 0.0625 * square
    mixing = (jnp.where(row == column, 2.25, 0.0) - 2.4375 * correlation) + product(split(square), split(tail))
    mixing_high, mixing_low = split(mixing)

    rows = 2 * half
    group = high_t_ref.shape[1] // rows
    places = [order.index(k) for k in range(group)]
    high = jnp.concatenate([high[i * rows : (i + 1) * rows] for i in places], axis=0)
    low = jnp.concatenate([low[i * rows : (i + 1) * rows] for i in places], axis=0)
    scale = lax.rsqrt(total)
    own = product((high[:rows], low[:rows]), (mixing_high, mixing_low))
    own_ref[...] = own * (scale * math.sqrt(times * rows))
    width = rank // times
    source = ((row // width) ^ index_ref[0]) * width + row % width
    move = jnp.where(source == column, 1.0, 0.0).astype(jnp.bfloat16)
    moved = dot(move, jnp.concatenate([mixing_high, mixing_low], axis=1)).astype(jnp.bfloat16)
    turned = product((moved[:, :rank], moved[:, rank:]), (high, low), COLUMNS_BY_COLUMNS) * scale
    high_t_ref[...], low_t_ref[...] = split(turned)


def mix(index, pairs, times, group, order):
    halves = [half for pair in pairs for half in pair]
    rank = halves[0].shape[1]
    rows = sum(half.shape[0] for half in halves) // times
    factor = jax.ShapeDtypeStruct((rank, group * rows), jnp.bfloat16)
    return pl.pallas_call(
        functools.partial(mix_kernel, times, order),
        in_specs=[SMEM] + [VMEM] * len(halves),
        out_specs=[VMEM] * 3,
        out_shape=[factor, factor, jax.ShapeDtypeStruct((rows, rank), jnp.float32)],
        compiler_params=params(),
        cost_estimate=FREE,
    )(index, *halves)


def load_kernel(group, high_ref, low_ref, *refs):
    parts, blocks = refs[:group], refs[group:]
    columns = jnp.concatenate([part[...] for part in parts], axis=0)
    value = product((high_ref[...], low_ref[...]), split(columns))
    width = value.shape[0] // len(blocks)
    for i, block in enumerate(blocks):
        block[...] = value[i * width : (i + 1) * width]


def load(high, low, parts, blocks):
    rank = high.shape[0]
    columns = parts[0].shape[1]
    return pl.pallas_call(
        functools.partial(load_kernel, len(parts)),
        in_specs=[VMEM] * (2 + len(parts)),
        out_specs=[VMEM] * blocks,
        out_shape=[jax.ShapeDtypeStruct((rank // blocks, columns), jnp.float32)] * blocks,
        compiler_params=params(),
        cost_estimate=FREE,
    )(high, low, *parts)


def join_kernel(group, sequence, own_ref, *refs):
    *terms, own_out_ref, out_ref, buf, sems = refs
    terms = [terms[sequence.index(k)] for k in range(len(terms))]
    width = terms[0].shape[1]
    member = lax.rem(lax.axis_index("tm"), group)
    copies = [pltpu.make_async_copy(own_ref, own_out_ref, sems.at[group])]
    copies[0].start()
    for k in range(group):
        value = terms[k][...]
        for term in terms[group + k :: group]:
            value = value + term[...]
        buf[k] = value
        span = pl.ds(pl.multiple_of((member ^ k) * width, width), width)
        copies.append(pltpu.make_async_copy(buf.at[k], out_ref.at[:, span], sems.at[k]))
        copies[-1].start()
    for copy in copies:
        copy.wait()


def join(own, terms, group, sequence):
    rows, width = terms[0].shape
    return pl.pallas_call(
        functools.partial(join_kernel, group, sequence),
        in_specs=[VMEM] * (1 + len(terms)),
        out_specs=[HBM] * 2,
        out_shape=[
            jax.ShapeDtypeStruct(own.shape, jnp.float32),
            jax.ShapeDtypeStruct((rows, group * width), jnp.float32),
        ],
        scratch_shapes=[pltpu.VMEM((group, rows, width), jnp.float32), pltpu.SemaphoreType.DMA((group + 1,))],
        compiler_params=params(),
        cost_estimate=FREE,
    )(own, *[terms[k] for k in sequence])


def swap(value, axis, offset):
    return lax.ppermute(value, axis, [(i, i ^ offset) for i in range(lax.axis_size(axis))])


def on_device(snapshots, space_factor):
    rows, points = snapshots.shape
    rank = space_factor.shape[1]
    times, spaces = lax.axis_size("tm"), lax.axis_size("space")
    group = min(4, times)
    index = lax.axis_index("tm")
    core = lax.axis_index("space") % 2

    mine, other, parts = project(snapshots, space_factor, group)
    parts = [part if k == 0 else swap(part, "tm", k) for k, part in enumerate(parts)]

    terms = [mine] + [swap(other if k % 2 else mine, "space", k) for k in range(1, spaces)]
    while len(terms) > 1:
        terms = [a + b for a, b in zip(terms[::2], terms[1::2])]
    mine = terms[0]

    near = group // 2
    order = [k for k in range(times) if k % group < near]
    mine = jnp.concatenate([mine] + [swap(mine, "tm", k) for k in order[1:]], axis=0)
    mine, *parts[1:3] = lax.optimization_barrier((mine, *parts[1:3]))
    rest = swap(mine, "tm", near)
    pairs = [(mine, swap(mine, "space", 1))]
    pairs.append((rest, swap(rest, "space", 1)))
    order = order + [k ^ near for k in order]
    high_t, low_t, own = mix(jnp.stack([index, core]), pairs, times, group, order)

    blocks = list(load(high_t, low_t, parts, times))
    terms = [blocks[0]] + [None] * (times - 1)
    near, far = list(range(1, group)), list(range(group, times))
    sequence = [*far[:2], *near[:2], *far[2:], *near[2:], 0]
    for k in sequence[:-1]:
        if k == near[-1]:
            blocks[k], terms[1] = lax.optimization_barrier((blocks[k], terms[1]))
        terms[k] = swap(blocks[k], "tm", k)
    return tuple(join(own, terms, group, sequence))


def solution(mesh):
    return jax.shard_map(
        on_device,
        mesh=mesh,
        in_specs=(P("tm", "space"), P("space", None)),
        out_specs=(P("tm", None), P("tm", "space")),
        check_vma=False,
    )
```

```python
import functools
import math

import jax
import jax.numpy as jnp
from jax import lax
from jax.experimental import pallas as pl
from jax.experimental.pallas import tpu as pltpu
from jax.sharding import PartitionSpec as P

MIB = 1024 * 1024
HBM = pl.BlockSpec(memory_space=pltpu.HBM)
SMEM = pl.BlockSpec(memory_space=pltpu.SMEM)
VMEM = pl.BlockSpec(memory_space=pltpu.VMEM)
FREE = pl.CostEstimate(flops=0, bytes_accessed=0, transcendentals=0)
ROWS_BY_ROWS = (((0,), (0,)), ((), ()))
ROWS_BY_COLUMNS = (((1,), (0,)), ((), ()))
COLUMNS_BY_COLUMNS = (((1,), (1,)), ((), ()))


def params(mib=48):
    return pltpu.CompilerParams(vmem_limit_bytes=mib * MIB)


def split(value):
    high = value.astype(jnp.bfloat16)
    return high, (value - high.astype(jnp.float32)).astype(jnp.bfloat16)


def dot(left, right, dims=ROWS_BY_COLUMNS):
    return lax.dot_general(left, right, dims, preferred_element_type=jnp.float32)


def product(left, right, dims=ROWS_BY_COLUMNS):
    (left_high, left_low), (right_high, right_low) = left, right
    return dot(left_high, right_high, dims) + (
        dot(left_high, right_low, dims) + dot(left_low, right_high, dims)
    )


def project_kernel(depth, snapshots_ref, factor_ref, mine_ref, other_ref, *refs):
    *parts, snapshots_buf, factor_buf, sems = refs
    rows, points = snapshots_ref.shape
    half = rows // 2
    snapshots_copy = pltpu.make_async_copy(snapshots_ref, snapshots_buf, sems.at[points // depth])
    snapshots_copy.start()
    copies = []
    for i, start in enumerate(range(0, points, depth)):
        span = pl.ds(start, depth)
        copies.append(pltpu.make_async_copy(factor_ref.at[span, :], factor_buf.at[span, :], sems.at[i]))
        copies[-1].start()
    snapshots_copy.wait()
    width = parts[0].shape[1]
    member = lax.rem(lax.axis_index("tm"), len(parts))
    for k, part in enumerate(parts):
        part[...] = snapshots_buf[:, pl.ds(pl.multiple_of((member ^ k) * width, width), width)]
    value = None
    for i, start in enumerate(range(0, points, depth)):
        copies[i].wait()
        high, low = split(snapshots_buf[:, start : start + depth])
        factor_high, factor_low = split(factor_buf[start : start + depth, :])
        both = dot(jnp.concatenate([high, low], axis=0), factor_high)
        term = both[:rows] + (both[rows:] + dot(high, factor_low))
        value = term if value is None else value + term
    first = lax.rem(lax.axis_index("space"), 2) == 0
    mine_ref[...] = jnp.where(first, value[:half], value[half:])
    other_ref[...] = jnp.where(first, value[half:], value[:half])


def project(snapshots, space_factor, group):
    rows, points = snapshots.shape
    rank = space_factor.shape[1]
    depth = min(512, points)
    half = jax.ShapeDtypeStruct((rows // 2, rank), jnp.float32)
    part = jax.ShapeDtypeStruct((rows, points // group), jnp.float32)
    mine, other, *parts = pl.pallas_call(
        functools.partial(project_kernel, depth),
        in_specs=[HBM, HBM],
        out_specs=[VMEM] * (2 + group),
        out_shape=[half, half] + [part] * group,
        scratch_shapes=[
            pltpu.VMEM((rows, points), jnp.float32),
            pltpu.VMEM((points, rank), jnp.float32),
            pltpu.SemaphoreType.DMA((points // depth + 1,)),
        ],
        compiler_params=params(52),
        cost_estimate=FREE,
    )(snapshots, space_factor)
    return mine, other, parts


def mix_kernel(times, order, index_ref, *refs):
    *halves, high_t_ref, low_t_ref, own_ref = refs
    rank = own_ref.shape[1]
    mine, theirs = [jnp.concatenate([ref[...] for ref in halves[i::2]], axis=0) for i in range(2)]
    total_half = mine.shape[0]
    half = total_half // times
    mine = mine.reshape(times, half, rank)
    theirs = theirs.reshape(times, half, rank)
    first = index_ref[1] == 0
    low_rows, high_rows = jnp.where(first, mine, theirs), jnp.where(first, theirs, mine)
    projected = jnp.concatenate([low_rows, high_rows], axis=1).reshape(2 * total_half, rank)
    high, low = split(projected)
    cross = dot(high, low, ROWS_BY_ROWS)
    gram = dot(high, high, ROWS_BY_ROWS) + (cross + cross.T)
    row = lax.broadcasted_iota(jnp.int32, (rank, rank), 0)
    column = lax.broadcasted_iota(jnp.int32, (rank, rank), 1)
    total = jnp.sum(projected * projected)
    correlation = gram / total
    correlation_split = split(correlation)
    square = product(correlation_split, correlation_split)
    tail = jnp.where(row == column, 1.6875, 0.0) - 0.5625 * correlation + 0.0625 * square
    mixing = (jnp.where(row == column, 2.25, 0.0) - 2.4375 * correlation) + product(split(square), split(tail))
    mixing_high, mixing_low = split(mixing)

    rows = 2 * half
    group = high_t_ref.shape[1] // rows
    places = [order.index(k) for k in range(group)]
    high = jnp.concatenate([high[i * rows : (i + 1) * rows] for i in places], axis=0)
    low = jnp.concatenate([low[i * rows : (i + 1) * rows] for i in places], axis=0)
    scale = lax.rsqrt(total)
    own = product((high[:rows], low[:rows]), (mixing_high, mixing_low))
    own_ref[...] = own * (scale * math.sqrt(times * rows))
    width = rank // times
    source = ((row // width) ^ index_ref[0]) * width + row % width
    move = jnp.where(source == column, 1.0, 0.0).astype(jnp.bfloat16)
    moved = dot(move, jnp.concatenate([mixing_high, mixing_low], axis=1)).astype(jnp.bfloat16)
    turned = product((moved[:, :rank], moved[:, rank:]), (high, low), COLUMNS_BY_COLUMNS) * scale
    high_t_ref[...], low_t_ref[...] = split(turned)


def mix(index, pairs, times, group, order):
    halves = [half for pair in pairs for half in pair]
    rank = halves[0].shape[1]
    rows = sum(half.shape[0] for half in halves) // times
    factor = jax.ShapeDtypeStruct((rank, group * rows), jnp.bfloat16)
    return pl.pallas_call(
        functools.partial(mix_kernel, times, order),
        in_specs=[SMEM] + [VMEM] * len(halves),
        out_specs=[VMEM] * 3,
        out_shape=[factor, factor, jax.ShapeDtypeStruct((rows, rank), jnp.float32)],
        compiler_params=params(),
        cost_estimate=FREE,
    )(index, *halves)


def load_kernel(group, high_ref, low_ref, *refs):
    parts, blocks = refs[:group], refs[group:]
    columns = jnp.concatenate([part[...] for part in parts], axis=0)
    value = product((high_ref[...], low_ref[...]), split(columns))
    width = value.shape[0] // len(blocks)
    for i, block in enumerate(blocks):
        block[...] = value[i * width : (i + 1) * width]


def load(high, low, parts, blocks):
    rank = high.shape[0]
    columns = parts[0].shape[1]
    return pl.pallas_call(
        functools.partial(load_kernel, len(parts)),
        in_specs=[VMEM] * (2 + len(parts)),
        out_specs=[VMEM] * blocks,
        out_shape=[jax.ShapeDtypeStruct((rank // blocks, columns), jnp.float32)] * blocks,
        compiler_params=params(),
        cost_estimate=FREE,
    )(high, low, *parts)


def join_kernel(group, sequence, own_ref, *refs):
    *terms, own_out_ref, out_ref, buf, sems = refs
    terms = [terms[sequence.index(k)] for k in range(len(terms))]
    width = terms[0].shape[1]
    member = lax.rem(lax.axis_index("tm"), group)
    copies = [pltpu.make_async_copy(own_ref, own_out_ref, sems.at[group])]
    copies[0].start()
    for k in range(group):
        value = terms[k][...]
        for term in terms[group + k :: group]:
            value = value + term[...]
        buf[k] = value
        span = pl.ds(pl.multiple_of((member ^ k) * width, width), width)
        copies.append(pltpu.make_async_copy(buf.at[k], out_ref.at[:, span], sems.at[k]))
        copies[-1].start()
    for copy in copies:
        copy.wait()


def join(own, terms, group, sequence):
    rows, width = terms[0].shape
    return pl.pallas_call(
        functools.partial(join_kernel, group, sequence),
        in_specs=[VMEM] * (1 + len(terms)),
        out_specs=[HBM] * 2,
        out_shape=[
            jax.ShapeDtypeStruct(own.shape, jnp.float32),
            jax.ShapeDtypeStruct((rows, group * width), jnp.float32),
        ],
        scratch_shapes=[pltpu.VMEM((group, rows, width), jnp.float32), pltpu.SemaphoreType.DMA((group + 1,))],
        compiler_params=params(),
        cost_estimate=FREE,
    )(own, *[terms[k] for k in sequence])


def swap(value, axis, offset):
    return lax.ppermute(value, axis, [(i, i ^ offset) for i in range(lax.axis_size(axis))])


def on_device(snapshots, space_factor):
    rows, points = snapshots.shape
    rank = space_factor.shape[1]
    times, spaces = lax.axis_size("tm"), lax.axis_size("space")
    group = min(4, times)
    index = lax.axis_index("tm")
    core = lax.axis_index("space") % 2

    mine, other, parts = project(snapshots, space_factor, group)
    parts = [part if k == 0 else swap(part, "tm", k) for k, part in enumerate(parts)]

    terms = [mine] + [swap(other if k % 2 else mine, "space", k) for k in range(1, spaces)]
    while len(terms) > 1:
        terms = [a + b for a, b in zip(terms[::2], terms[1::2])]
    mine = terms[0]

    near = group // 2
    order = [0] + [k for k in [*range(group, times), *range(1, group)] if k % group < near]
    mine = jnp.concatenate([mine] + [swap(mine, "tm", k) for k in order[1:]], axis=0)
    mine, *parts[1:3] = lax.optimization_barrier((mine, *parts[1:3]))
    rest = swap(mine, "tm", near)
    pairs = [(mine, swap(mine, "space", 1))]
    pairs.append((rest, swap(rest, "space", 1)))
    order = order + [k ^ near for k in order]
    high_t, low_t, own = mix(jnp.stack([index, core]), pairs, times, group, order)

    blocks = list(load(high_t, low_t, parts, times))
    terms = [blocks[0]] + [None] * (times - 1)
    near, far = list(range(1, group)), list(range(group, times))
    sequence = [*far[:2], *near[:2], *far[2:], *near[2:], 0]
    for k in sequence[:-1]:
        if k == near[-1]:
            blocks[k], terms[1] = lax.optimization_barrier((blocks[k], terms[1]))
        terms[k] = swap(blocks[k], "tm", k)
    return tuple(join(own, terms, group, sequence))


def solution(mesh):
    return jax.shard_map(
        on_device,
        mesh=mesh,
        in_specs=(P("tm", "space"), P("space", None)),
        out_specs=(P("tm", None), P("tm", "space")),
        check_vma=False,
    )
```

```python
import functools
import math

import jax
import jax.numpy as jnp
from jax import lax
from jax.experimental import pallas as pl
from jax.experimental.pallas import tpu as pltpu
from jax.sharding import PartitionSpec as P

MIB = 1024 * 1024
HBM = pl.BlockSpec(memory_space=pltpu.HBM)
SMEM = pl.BlockSpec(memory_space=pltpu.SMEM)
VMEM = pl.BlockSpec(memory_space=pltpu.VMEM)
FREE = pl.CostEstimate(flops=0, bytes_accessed=0, transcendentals=0)
ROWS_BY_ROWS = (((0,), (0,)), ((), ()))
ROWS_BY_COLUMNS = (((1,), (0,)), ((), ()))
COLUMNS_BY_COLUMNS = (((1,), (1,)), ((), ()))


def params(mib=48):
    return pltpu.CompilerParams(vmem_limit_bytes=mib * MIB)


def split(value):
    high = value.astype(jnp.bfloat16)
    return high, (value - high.astype(jnp.float32)).astype(jnp.bfloat16)


def dot(left, right, dims=ROWS_BY_COLUMNS):
    return lax.dot_general(left, right, dims, preferred_element_type=jnp.float32)


def product(left, right, dims=ROWS_BY_COLUMNS):
    (left_high, left_low), (right_high, right_low) = left, right
    rows = left_high.shape[0]
    both = dot(jnp.concatenate([left_high, left_low], axis=0), right_high, dims)
    return both[:rows] + (both[rows:] + dot(left_high, right_low, dims))


def project_kernel(depth, snapshots_ref, factor_ref, mine_ref, other_ref, *refs):
    *parts, snapshots_buf, factor_buf, sems = refs
    rows, points = snapshots_ref.shape
    half = rows // 2
    snapshots_copy = pltpu.make_async_copy(snapshots_ref, snapshots_buf, sems.at[points // depth])
    snapshots_copy.start()
    copies = []
    for i, start in enumerate(range(0, points, depth)):
        span = pl.ds(start, depth)
        copies.append(pltpu.make_async_copy(factor_ref.at[span, :], factor_buf.at[span, :], sems.at[i]))
        copies[-1].start()
    snapshots_copy.wait()
    width = parts[0].shape[1]
    member = lax.rem(lax.axis_index("tm"), len(parts))
    for k, part in enumerate(parts):
        part[...] = snapshots_buf[:, pl.ds(pl.multiple_of((member ^ k) * width, width), width)]
    value = None
    for i, start in enumerate(range(0, points, depth)):
        copies[i].wait()
        high, low = split(snapshots_buf[:, start : start + depth])
        factor_high, factor_low = split(factor_buf[start : start + depth, :])
        both = dot(jnp.concatenate([high, low], axis=0), factor_high)
        term = both[:rows] + (both[rows:] + dot(high, factor_low))
        value = term if value is None else value + term
    first = lax.rem(lax.axis_index("space"), 2) == 0
    mine_ref[...] = jnp.where(first, value[:half], value[half:])
    other_ref[...] = jnp.where(first, value[half:], value[:half])


def project(snapshots, space_factor, group):
    rows, points = snapshots.shape
    rank = space_factor.shape[1]
    depth = min(512, points)
    half = jax.ShapeDtypeStruct((rows // 2, rank), jnp.float32)
    part = jax.ShapeDtypeStruct((rows, points // group), jnp.float32)
    mine, other, *parts = pl.pallas_call(
        functools.partial(project_kernel, depth),
        in_specs=[HBM, HBM],
        out_specs=[VMEM] * (2 + group),
        out_shape=[half, half] + [part] * group,
        scratch_shapes=[
            pltpu.VMEM((rows, points), jnp.float32),
            pltpu.VMEM((points, rank), jnp.float32),
            pltpu.SemaphoreType.DMA((points // depth + 1,)),
        ],
        compiler_params=params(52),
        cost_estimate=FREE,
    )(snapshots, space_factor)
    return mine, other, parts


def mix_kernel(times, order, index_ref, *refs):
    *halves, high_t_ref, low_t_ref, own_ref = refs
    rank = own_ref.shape[1]
    mine, theirs = [jnp.concatenate([ref[...] for ref in halves[i::2]], axis=0) for i in range(2)]
    total_half = mine.shape[0]
    half = total_half // times
    mine = mine.reshape(times, half, rank)
    theirs = theirs.reshape(times, half, rank)
    first = index_ref[1] == 0
    low_rows, high_rows = jnp.where(first, mine, theirs), jnp.where(first, theirs, mine)
    projected = jnp.concatenate([low_rows, high_rows], axis=1).reshape(2 * total_half, rank)
    high, low = split(projected)
    cross = dot(high, low, ROWS_BY_ROWS)
    gram = dot(high, high, ROWS_BY_ROWS) + (cross + cross.T)
    row = lax.broadcasted_iota(jnp.int32, (rank, rank), 0)
    column = lax.broadcasted_iota(jnp.int32, (rank, rank), 1)
    total = jnp.sum(projected * projected)
    correlation = gram / total
    correlation_split = split(correlation)
    square = product(correlation_split, correlation_split)
    tail = jnp.where(row == column, 1.6875, 0.0) - 0.5625 * correlation + 0.0625 * square
    mixing = (jnp.where(row == column, 2.25, 0.0) - 2.4375 * correlation) + product(split(square), split(tail))
    mixing_high, mixing_low = split(mixing)

    rows = 2 * half
    group = high_t_ref.shape[1] // rows
    places = [order.index(k) for k in range(group)]
    high = jnp.concatenate([high[i * rows : (i + 1) * rows] for i in places], axis=0)
    low = jnp.concatenate([low[i * rows : (i + 1) * rows] for i in places], axis=0)
    scale = lax.rsqrt(total)
    own = product((high[:rows], low[:rows]), (mixing_high, mixing_low))
    own_ref[...] = own * (scale * math.sqrt(times * rows))
    width = rank // times
    source = ((row // width) ^ index_ref[0]) * width + row % width
    move = jnp.where(source == column, 1.0, 0.0).astype(jnp.bfloat16)
    moved = dot(move, jnp.concatenate([mixing_high, mixing_low], axis=1)).astype(jnp.bfloat16)
    turned = product((moved[:, :rank], moved[:, rank:]), (high, low), COLUMNS_BY_COLUMNS) * scale
    high_t_ref[...], low_t_ref[...] = split(turned)


def mix(index, pairs, times, group, order):
    halves = [half for pair in pairs for half in pair]
    rank = halves[0].shape[1]
    rows = sum(half.shape[0] for half in halves) // times
    factor = jax.ShapeDtypeStruct((rank, group * rows), jnp.bfloat16)
    return pl.pallas_call(
        functools.partial(mix_kernel, times, order),
        in_specs=[SMEM] + [VMEM] * len(halves),
        out_specs=[VMEM] * 3,
        out_shape=[factor, factor, jax.ShapeDtypeStruct((rows, rank), jnp.float32)],
        compiler_params=params(),
        cost_estimate=FREE,
    )(index, *halves)


def load_kernel(group, start, stop, high_ref, low_ref, *refs):
    parts, refs = refs[: stop - start], refs[stop - start :]
    depth = high_ref.shape[1] // group
    span = slice(start * depth, stop * depth)
    columns = jnp.concatenate([part[...] for part in parts], axis=0)
    value = product((high_ref[:, span], low_ref[:, span]), split(columns))
    if start == 0:
        refs[0][...] = value
        return
    sum_ref, *blocks = refs
    width = value.shape[0] // len(blocks)
    for i, block in enumerate(blocks):
        rows = slice(i * width, (i + 1) * width)
        block[...] = sum_ref[rows] + value[rows]


def load(high, low, parts, blocks):
    rank = high.shape[0]
    group = len(parts)
    columns = parts[0].shape[1]

    def call(start, stop, out_shape, *sums):
        return pl.pallas_call(
            functools.partial(load_kernel, group, start, stop),
            in_specs=[VMEM] * (2 + stop - start + len(sums)),
            out_specs=[VMEM] * len(out_shape),
            out_shape=out_shape,
            compiler_params=params(),
            cost_estimate=FREE,
        )(high, low, *parts[start:stop], *sums)

    early = call(0, group - 1, [jax.ShapeDtypeStruct((rank, columns), jnp.float32)])
    return call(group - 1, group, [jax.ShapeDtypeStruct((rank // blocks, columns), jnp.float32)] * blocks, *early)


def join_kernel(group, sequence, own_ref, *refs):
    *terms, own_out_ref, out_ref, buf, sems = refs
    terms = [terms[sequence.index(k)] for k in range(len(terms))]
    width = terms[0].shape[1]
    member = lax.rem(lax.axis_index("tm"), group)
    copies = [pltpu.make_async_copy(own_ref, own_out_ref, sems.at[group])]
    copies[0].start()
    for k in range(group):
        value = terms[k][...]
        for term in terms[group + k :: group]:
            value = value + term[...]
        buf[k] = value
        span = pl.ds(pl.multiple_of((member ^ k) * width, width), width)
        copies.append(pltpu.make_async_copy(buf.at[k], out_ref.at[:, span], sems.at[k]))
        copies[-1].start()
    for copy in copies:
        copy.wait()


def join(own, terms, group, sequence):
    rows, width = terms[0].shape
    return pl.pallas_call(
        functools.partial(join_kernel, group, sequence),
        in_specs=[VMEM] * (1 + len(terms)),
        out_specs=[HBM] * 2,
        out_shape=[
            jax.ShapeDtypeStruct(own.shape, jnp.float32),
            jax.ShapeDtypeStruct((rows, group * width), jnp.float32),
        ],
        scratch_shapes=[pltpu.VMEM((group, rows, width), jnp.float32), pltpu.SemaphoreType.DMA((group + 1,))],
        compiler_params=params(),
        cost_estimate=FREE,
    )(own, *[terms[k] for k in sequence])


def swap(value, axis, offset):
    return lax.ppermute(value, axis, [(i, i ^ offset) for i in range(lax.axis_size(axis))])


def on_device(snapshots, space_factor):
    rows, points = snapshots.shape
    rank = space_factor.shape[1]
    times, spaces = lax.axis_size("tm"), lax.axis_size("space")
    group = min(4, times)
    index = lax.axis_index("tm")
    core = lax.axis_index("space") % 2

    mine, other, parts = project(snapshots, space_factor, group)
    parts = [part if k == 0 else swap(part, "tm", k) for k, part in enumerate(parts)]

    terms = [mine] + [swap(other if k % 2 else mine, "space", k) for k in range(1, spaces)]
    while len(terms) > 1:
        terms = [a + b for a, b in zip(terms[::2], terms[1::2])]
    mine = terms[0]

    near = group // 2
    order = [k for k in range(times) if k % group < near]
    mine = jnp.concatenate([mine] + [swap(mine, "tm", k) for k in order[1:]], axis=0)
    mine, *parts[1:3] = lax.optimization_barrier((mine, *parts[1:3]))
    rest = swap(mine, "tm", near)
    pairs = [(mine, swap(mine, "space", 1))]
    pairs.append((rest, swap(rest, "space", 1)))
    order = order + [k ^ near for k in order]
    high_t, low_t, own = mix(jnp.stack([index, core]), pairs, times, group, order)

    blocks = list(load(high_t, low_t, parts, times))
    terms = [blocks[0]] + [None] * (times - 1)
    near, far = list(range(1, group)), list(range(group, times))
    sequence = [*far[:2], *near[:2], *far[2:], *near[2:], 0]
    for k in sequence[:-1]:
        if k == near[-1]:
            blocks[k], terms[1] = lax.optimization_barrier((blocks[k], terms[1]))
        terms[k] = swap(blocks[k], "tm", k)
    return tuple(join(own, terms, group, sequence))


def solution(mesh):
    return jax.shard_map(
        on_device,
        mesh=mesh,
        in_specs=(P("tm", "space"), P("space", None)),
        out_specs=(P("tm", None), P("tm", "space")),
        check_vma=False,
    )
```

```python
import functools
import math

import jax
import jax.numpy as jnp
from jax import lax
from jax.experimental import pallas as pl
from jax.experimental.pallas import tpu as pltpu
from jax.sharding import PartitionSpec as P

MIB = 1024 * 1024
HBM = pl.BlockSpec(memory_space=pltpu.HBM)
SMEM = pl.BlockSpec(memory_space=pltpu.SMEM)
VMEM = pl.BlockSpec(memory_space=pltpu.VMEM)
FREE = pl.CostEstimate(flops=0, bytes_accessed=0, transcendentals=0)
ROWS_BY_ROWS = (((0,), (0,)), ((), ()))
ROWS_BY_COLUMNS = (((1,), (0,)), ((), ()))
COLUMNS_BY_COLUMNS = (((1,), (1,)), ((), ()))


def params(mib=48):
    return pltpu.CompilerParams(vmem_limit_bytes=mib * MIB)


def split(value):
    high = value.astype(jnp.bfloat16)
    return high, (value - high.astype(jnp.float32)).astype(jnp.bfloat16)


def dot(left, right, dims=ROWS_BY_COLUMNS):
    return lax.dot_general(left, right, dims, preferred_element_type=jnp.float32)


def product(left, right, dims=ROWS_BY_COLUMNS):
    (left_high, left_low), (right_high, right_low) = left, right
    return dot(left_high, right_high, dims) + (
        dot(left_high, right_low, dims) + dot(left_low, right_high, dims)
    )


def project_kernel(depth, snapshots_ref, factor_ref, mine_ref, other_ref, *refs):
    *parts, snapshots_buf, factor_buf, sems = refs
    rows, points = snapshots_ref.shape
    half = rows // 2
    snapshots_copy = pltpu.make_async_copy(snapshots_ref, snapshots_buf, sems.at[points // depth])
    snapshots_copy.start()
    copies = []
    for i, start in enumerate(range(0, points, depth)):
        span = pl.ds(start, depth)
        copies.append(pltpu.make_async_copy(factor_ref.at[span, :], factor_buf.at[span, :], sems.at[i]))
        copies[-1].start()
    snapshots_copy.wait()
    width = parts[0].shape[1]
    member = lax.rem(lax.axis_index("tm"), len(parts))
    for k, part in enumerate(parts):
        part[...] = snapshots_buf[:, pl.ds(pl.multiple_of((member ^ k) * width, width), width)]
    value = None
    for i, start in enumerate(range(0, points, depth)):
        copies[i].wait()
        high, low = split(snapshots_buf[:, start : start + depth])
        factor_high, factor_low = split(factor_buf[start : start + depth, :])
        both = dot(jnp.concatenate([high, low], axis=0), factor_high)
        term = both[:rows] + (both[rows:] + dot(high, factor_low))
        value = term if value is None else value + term
    first = lax.rem(lax.axis_index("space"), 2) == 0
    mine_ref[...] = jnp.where(first, value[:half], value[half:])
    other_ref[...] = jnp.where(first, value[half:], value[:half])


def project(snapshots, space_factor, group):
    rows, points = snapshots.shape
    rank = space_factor.shape[1]
    depth = min(512, points)
    half = jax.ShapeDtypeStruct((rows // 2, rank), jnp.float32)
    part = jax.ShapeDtypeStruct((rows, points // group), jnp.float32)
    mine, other, *parts = pl.pallas_call(
        functools.partial(project_kernel, depth),
        in_specs=[HBM, HBM],
        out_specs=[VMEM] * (2 + group),
        out_shape=[half, half] + [part] * group,
        scratch_shapes=[
            pltpu.VMEM((rows, points), jnp.float32),
            pltpu.VMEM((points, rank), jnp.float32),
            pltpu.SemaphoreType.DMA((points // depth + 1,)),
        ],
        compiler_params=params(52),
        cost_estimate=FREE,
    )(snapshots, space_factor)
    return mine, other, parts


def mix_kernel(times, order, index_ref, *refs):
    *halves, high_t_ref, low_t_ref, own_ref = refs
    rank = own_ref.shape[1]
    mine, theirs = [jnp.concatenate([ref[...] for ref in halves[i::2]], axis=0) for i in range(2)]
    total_half = mine.shape[0]
    half = total_half // times
    mine = mine.reshape(times, half, rank)
    theirs = theirs.reshape(times, half, rank)
    first = index_ref[1] == 0
    low_rows, high_rows = jnp.where(first, mine, theirs), jnp.where(first, theirs, mine)
    projected = jnp.concatenate([low_rows, high_rows], axis=1).reshape(2 * total_half, rank)
    high, low = split(projected)
    cross = dot(high, low, ROWS_BY_ROWS)
    gram = dot(high, high, ROWS_BY_ROWS) + (cross + cross.T)
    row = lax.broadcasted_iota(jnp.int32, (rank, rank), 0)
    column = lax.broadcasted_iota(jnp.int32, (rank, rank), 1)
    total = jnp.sum(projected * projected)
    correlation = gram / total
    correlation_split = split(correlation)
    square = product(correlation_split, correlation_split)
    tail = jnp.where(row == column, 1.6875, 0.0) - 0.5625 * correlation + 0.0625 * square
    mixing = (jnp.where(row == column, 2.25, 0.0) - 2.4375 * correlation) + product(split(square), split(tail))
    mixing_high, mixing_low = split(mixing)

    rows = 2 * half
    group = high_t_ref.shape[1] // rows
    places = [order.index(k) for k in range(group)]
    high = jnp.concatenate([high[i * rows : (i + 1) * rows] for i in places], axis=0)
    low = jnp.concatenate([low[i * rows : (i + 1) * rows] for i in places], axis=0)
    scale = lax.rsqrt(total)
    own = product((high[:rows], low[:rows]), (mixing_high, mixing_low))
    own_ref[...] = own * (scale * math.sqrt(times * rows))
    width = rank // times
    source = ((row // width) ^ index_ref[0]) * width + row % width
    move = jnp.where(source == column, 1.0, 0.0).astype(jnp.bfloat16)
    moved = dot(move, jnp.concatenate([mixing_high, mixing_low], axis=1)).astype(jnp.bfloat16)
    turned = product((moved[:, :rank], moved[:, rank:]), (high, low), COLUMNS_BY_COLUMNS) * scale
    high_t_ref[...], low_t_ref[...] = split(turned)


def mix(index, pairs, times, group, order):
    halves = [half for pair in pairs for half in pair]
    rank = halves[0].shape[1]
    rows = sum(half.shape[0] for half in halves) // times
    factor = jax.ShapeDtypeStruct((rank, group * rows), jnp.bfloat16)
    return pl.pallas_call(
        functools.partial(mix_kernel, times, order),
        in_specs=[SMEM] + [VMEM] * len(halves),
        out_specs=[VMEM] * 3,
        out_shape=[factor, factor, jax.ShapeDtypeStruct((rows, rank), jnp.float32)],
        compiler_params=params(),
        cost_estimate=FREE,
    )(index, *halves)


def load_kernel(group, high_ref, low_ref, *refs):
    parts, blocks = refs[:group], refs[group:]
    columns = jnp.concatenate([part[...] for part in parts], axis=0)
    value = product((high_ref[...], low_ref[...]), split(columns))
    width = value.shape[0] // len(blocks)
    for i, block in enumerate(blocks):
        block[...] = value[i * width : (i + 1) * width]


def load(high, low, parts, blocks):
    rank = high.shape[0]
    columns = parts[0].shape[1]
    return pl.pallas_call(
        functools.partial(load_kernel, len(parts)),
        in_specs=[VMEM] * (2 + len(parts)),
        out_specs=[VMEM] * blocks,
        out_shape=[jax.ShapeDtypeStruct((rank // blocks, columns), jnp.float32)] * blocks,
        compiler_params=params(),
        cost_estimate=FREE,
    )(high, low, *parts)


def join_kernel(group, sequence, own_ref, *refs):
    *terms, own_out_ref, out_ref, buf, sems = refs
    terms = [terms[sequence.index(k)] for k in range(len(terms))]
    width = terms[0].shape[1]
    member = lax.rem(lax.axis_index("tm"), group)
    copies = [pltpu.make_async_copy(own_ref, own_out_ref, sems.at[group])]
    copies[0].start()
    for k in range(group):
        value = terms[k][...]
        for term in terms[group + k :: group]:
            value = value + term[...]
        buf[k] = value
        span = pl.ds(pl.multiple_of((member ^ k) * width, width), width)
        copies.append(pltpu.make_async_copy(buf.at[k], out_ref.at[:, span], sems.at[k]))
        copies[-1].start()
    for copy in copies:
        copy.wait()


def join(own, terms, group, sequence):
    rows, width = terms[0].shape
    return pl.pallas_call(
        functools.partial(join_kernel, group, sequence),
        in_specs=[VMEM] * (1 + len(terms)),
        out_specs=[HBM] * 2,
        out_shape=[
            jax.ShapeDtypeStruct(own.shape, jnp.float32),
            jax.ShapeDtypeStruct((rows, group * width), jnp.float32),
        ],
        scratch_shapes=[pltpu.VMEM((group, rows, width), jnp.float32), pltpu.SemaphoreType.DMA((group + 1,))],
        compiler_params=params(),
        cost_estimate=FREE,
    )(own, *[terms[k] for k in sequence])


def swap(value, axis, offset):
    return lax.ppermute(value, axis, [(i, i ^ offset) for i in range(lax.axis_size(axis))])


def on_device(snapshots, space_factor):
    rows, points = snapshots.shape
    rank = space_factor.shape[1]
    times, spaces = lax.axis_size("tm"), lax.axis_size("space")
    group = min(4, times)
    index = lax.axis_index("tm")
    core = lax.axis_index("space") % 2

    mine, other, parts = project(snapshots, space_factor, group)
    parts = [part if k == 0 else swap(part, "tm", k) for k, part in enumerate(parts)]

    terms = [mine] + [swap(other if k % 2 else mine, "space", k) for k in range(1, spaces)]
    while len(terms) > 1:
        terms = [a + b for a, b in zip(terms[::2], terms[1::2])]
    mine = terms[0]

    near = group // 2
    order = [k for k in range(times) if k % group < near]
    mine = jnp.concatenate([mine] + [swap(mine, "tm", k) for k in order[1:]], axis=0)
    mine, *parts[1:3] = lax.optimization_barrier((mine, *parts[1:3]))
    rest = swap(mine, "tm", near)
    pairs = [(mine, swap(mine, "space", 1))]
    pairs.append((rest, swap(rest, "space", 1)))
    order = order + [k ^ near for k in order]
    high_t, low_t, own = mix(jnp.stack([index, core]), pairs, times, group, order)

    blocks = list(load(high_t, low_t, parts, times))
    terms = [blocks[0]] + [None] * (times - 1)
    near, far = list(range(1, group)), list(range(group, times))
    sequence = [*far[:3], *near[:2], *far[3:], *near[2:], 0]
    for k in sequence[:-1]:
        if k == near[-1]:
            blocks[k], terms[1] = lax.optimization_barrier((blocks[k], terms[1]))
        terms[k] = swap(blocks[k], "tm", k)
    return tuple(join(own, terms, group, sequence))


def solution(mesh):
    return jax.shard_map(
        on_device,
        mesh=mesh,
        in_specs=(P("tm", "space"), P("space", None)),
        out_specs=(P("tm", None), P("tm", "space")),
        check_vma=False,
    )
```
